32 devices in a mesh: gx: 4 (over y, core), gy: 8 (over z, x).
Axes of the slice: x: 2, y: 2, z: 4, core: 2. Of those that a mesh axis runs over, the one named last changes fastest.
Arguments:
- right_side: float32 [128, 128, 256], P('gx', 'gy'), may hold values from -8 to 8
- coefficient: float32 [128, 128, 256], P('gx', 'gy'), may hold values from 0.1 to 10
Outputs:
- solution_field: float32 [128, 128, 256], P('gx', 'gy')
- residual: float32 [128, 128, 256], P('gx', 'gy')
The draws below stay inside these ranges and needn't reach their ends.
All inputs are finite; a program needn't handle non-finite values.
Results may differ from the reference program's by a relative error of at most 0.0003.
Values sent between devices are 32-bit elements; how exact they have to be, the bound alone decides.
No kernel may reach another device: no remote copies, remote signals or barrier semaphores. Data moves between devices by JAX's collectives and lax.ppermute only.
A program may use at most 128 MiB of HBM per device.

```python
import math
from functools import partial
import jax
import jax.numpy as jnp

NZ = 256
LEVELS = 5
PRE = 2
POST = 2
BOTTOM = 8
NX = 128
NY = 128


def draw_right_side(key, part):
    values = jax.random.normal(key, (NX, NY, NZ), jnp.float32)
    return jnp.clip(values, -8.0, 8.0)


def levels(stream_key, extent, shards, low, largest):
    level, own = 1.0, jax.random.fold_in(stream_key, 6)
    for dim, blocks in shards:
        heights = jnp.exp(jax.random.uniform(jax.random.fold_in(own, dim), (blocks,), jnp.float32, low / len(shards), largest / len(shards)))
        level = level * jnp.repeat(heights, extent[dim] // blocks).reshape([-1 if axis == dim else 1 for axis in range(len(extent))])
    return level


def setup_inputs(seed: int = 0) -> dict:
    key_of = jax.random.split(jax.random.key(seed), 3)
    right_side = draw_right_side(jax.random.fold_in(key_of[2], 71), 0)
    coefficient = jnp.clip(jnp.exp(math.log(10.0) - 4.6051702 * jax.random.uniform(key_of[1], (NX, NY, NZ), jnp.float32) ** levels(key_of[1], (NX, NY, NZ), ((0, 4), (1, 8)), -0.2, 0.2)), 0.1, 10.0)
    return dict(right_side=right_side, coefficient=coefficient)


SMOOTH_LO = 0.5
SMOOTH_HI = 2.0
COARSE_LO = 0.05
COARSE_HI = 2.0


def harmonic(own, other):
    return 2.0 * own * other / (own + other)


def face_weights(conduct, padded):
    lower_x = jnp.where(padded[:-2, 1:-1, :] > 0.0, padded[:-2, 1:-1, :], conduct)
    upper_x = jnp.where(padded[2:, 1:-1, :] > 0.0, padded[2:, 1:-1, :], conduct)
    lower_y = jnp.where(padded[1:-1, :-2, :] > 0.0, padded[1:-1, :-2, :], conduct)
    upper_y = jnp.where(padded[1:-1, 2:, :] > 0.0, padded[1:-1, 2:, :], conduct)
    edged = jnp.pad(conduct, ((0, 0), (0, 0), (1, 1)), mode="edge")
    lower_z = edged[:, :, :-2]
    upper_z = edged[:, :, 2:]
    faces = [harmonic(conduct, other) for other in (lower_x, upper_x, lower_y, upper_y, lower_z, upper_z)]
    total = faces[0] + faces[1] + faces[2] + faces[3] + faces[4] + faces[5]
    return tuple(faces) + (total,)


def stencil(field, padded, weights, scale):
    zpad = jnp.pad(field, ((0, 0), (0, 0), (1, 1)))
    beside = weights[0] * padded[:-2, 1:-1, :] + weights[1] * padded[2:, 1:-1, :]
    beside = beside + weights[2] * padded[1:-1, :-2, :] + weights[3] * padded[1:-1, 2:, :]
    beside = beside + weights[4] * zpad[:, :, :-2] + weights[5] * zpad[:, :, 2:]
    return scale * (weights[6] * field - beside)


def pad_plane(field):
    return jnp.pad(field, ((1, 1), (1, 1), (0, 0)))


def whole_operate(field, weights, scale):
    return stencil(field, pad_plane(field), weights, scale)


def chebyshev(source, start, sweeps, low_end, high_end, operate, inverse):
    theta_val = (high_end + low_end) / 2.0
    half_width = (high_end - low_end) / 2.0
    sigma_val = theta_val / half_width
    rho_now = 1.0 / sigma_val
    if start is None:
        update = inverse * source / theta_val
        iterate = update
    else:
        update = inverse * (source - operate(start)) / theta_val
        iterate = start + update
    for sweep_index in range(sweeps - 1):
        rho_next = 1.0 / (2.0 * sigma_val - rho_now)
        update = rho_next * rho_now * update + (2.0 * rho_next / half_width) * inverse * (source - operate(iterate))
        iterate = iterate + update
        rho_now = rho_next
    return iterate


def restrict(field):
    size_x, size_y, size_z = field.shape
    return jnp.mean(field.reshape(size_x // 2, 2, size_y // 2, 2, size_z // 2, 2), axis=(1, 3, 5))


def prolong(field):
    size_x, size_y, size_z = field.shape
    grown = jnp.broadcast_to(field[:, None, :, None, :, None], (size_x, 2, size_y, 2, size_z, 2))
    return grown.reshape(2 * size_x, 2 * size_y, 2 * size_z)


def cycle(level_index, source, conduct):
    weights = face_weights(conduct, pad_plane(conduct))
    scale = 0.25 ** level_index
    inverse = 1.0 / (scale * weights[6])
    operate = partial(whole_operate, weights=weights, scale=scale)
    if level_index == LEVELS - 1:
        return chebyshev(source, None, BOTTOM, COARSE_LO, COARSE_HI, operate, inverse)
    iterate = chebyshev(source, None, PRE, SMOOTH_LO, SMOOTH_HI, operate, inverse)
    coarse = restrict(source - operate(iterate))
    iterate = iterate + prolong(cycle(level_index + 1, coarse, restrict(conduct)))
    return chebyshev(source, iterate, POST, SMOOTH_LO, SMOOTH_HI, operate, inverse)


def reference(right_side, coefficient):
    solution_field = cycle(0, right_side, coefficient)
    weights = face_weights(coefficient, pad_plane(coefficient))
    residual = right_side - whole_operate(solution_field, weights, 1.0)
    return solution_field, residual
```

```python
import math
from functools import partial

import jax
import jax.numpy as jnp
from jax import lax
from jax.experimental import pallas as pl
from jax.experimental.pallas import tpu as pltpu
from jax.sharding import PartitionSpec as P

F32 = jnp.float32
BF16 = jnp.bfloat16

THETA = 1.25
DELTA = 0.75
SIGMA = THETA / DELTA
RHO0 = 1.0 / SIGMA
RHO1 = 1.0 / (2.0 * SIGMA - RHO0)
KEEP = RHO1 * RHO0
GAIN = 2.0 * RHO1 / DELTA
BOTTOM = 8
BOTTOM_THETA = (2.0 + 0.05) / 2.0
BOTTOM_DELTA = (2.0 - 0.05) / 2.0

K0, B0, S0 = 3, 2, 3
K1, B1 = 6, 5
R0, R1 = 4, 8
SPARE = 4 * 1024 * 1024


def rotate(value, axis, shift):
    size = lax.axis_size(axis)
    return lax.ppermute(value, axis, [(i, (i + shift) % size) for i in range(size)])


def inside(axis, side):
    index = lax.axis_index(axis)
    if side < 0:
        return index > 0
    return index < lax.axis_size(axis) - 1


def masked(flag, value):
    return jnp.where(flag, value, jnp.zeros_like(value))


def iota(shape, dim):
    return lax.broadcasted_iota(jnp.int32, shape, dim)


def pick(x, matrix):
    high = x.astype(BF16)
    low = (x - high.astype(F32)).astype(BF16)
    return jnp.dot(high, matrix, preferred_element_type=F32) + jnp.dot(
        low, matrix, preferred_element_type=F32
    )


def halving(fine, coarse, scale, first=0, valid=None):
    row, col = iota((fine, coarse), 0), iota((fine, coarse), 1)
    hit = row // 2 + first == col
    if valid is not None:
        hit = hit & (row < valid)
    return jnp.where(hit, scale, 0.0).astype(BF16)


def doubling(coarse, fine, valid):
    row, col = iota((coarse, fine), 0), iota((coarse, fine), 1)
    return jnp.where((row == col // 2) & (row < valid), 1.0, 0.0).astype(BF16)


def face(a, b):
    product, total = a * b, a + b
    return jnp.where(product > 0.0, 2.0 * product / total, total)


def up(x, axis):
    return pltpu.roll(x, x.shape[axis] - 1, axis)


def down(x, axis):
    return pltpu.roll(x, 1, axis)


def sided(k, axis, edged):
    size = k.shape[axis]
    after = up(k, axis)
    place = iota(k.shape, axis)
    if edged:
        after = jnp.where(place == size - 1, 0.0, after)
    w = face(k, after)
    low = down(w, axis)
    if edged:
        low = jnp.where(place == 0, k, low)
        return jnp.where(place == size - 1, 0.0, w), w + low
    return w, w + low


def weigh(k, wl, ws, wz, total, inverse, row_edge, lane_edge, unroll):
    planes = k.shape[0]

    def body(i, before):
        here = k[i]
        lead = face(here, k[i + 1])
        rows, row_sum = sided(here, 0, row_edge)
        lanes, lane_sum = sided(here, 1, lane_edge)
        wl[i] = lead
        ws[i] = rows
        wz[i] = lanes
        whole = (before + lead) + (row_sum + lane_sum)
        total[i] = whole
        inverse[i] = jnp.where(here > 0.0, 1.0 / whole, 0.0)
        return lead

    lax.fori_loop(0, planes - 1, body, jnp.zeros(k.shape[1:], F32), unroll=unroll)


def beside(x, wl, ws, wz, i):
    here = x[i]
    rows, lanes = ws[i], wz[i]
    out = wl[i] * x[i + 1] + wl[i - 1] * x[i - 1]
    out = out + (rows * up(here, 0) + down(rows * here, 0))
    return out + (lanes * up(here, 1) + down(lanes * here, 1))


def loop(low, high, body, unroll):
    def step(i, carry):
        body(i)
        return carry

    lax.fori_loop(low, high, step, 0, unroll=unroll)


def pre_smooth(b, first, second, w, inverse, scale, depth, unroll):
    planes = b.shape[0]

    def start(i):
        first[i] = b[i] * inverse[i] * (1.0 / (scale * THETA))

    loop(depth, planes - depth, start, unroll)

    def sweep(i):
        near = beside(first, *w, i)
        second[i] = (1.0 + KEEP + GAIN * (THETA - 1.0)) * first[i] + GAIN * (inverse[i] * near)

    loop(depth + 1, planes - depth - 1, sweep, unroll)


def post_smooth(b, first, second, w, inverse, scale, depth, unroll, store):
    planes = b.shape[0]

    def sweep(i):
        x = first[i]
        near = beside(first, *w, i)
        second[i] = x + ((b[i] * (1.0 / scale) + near) * inverse[i] - x) * (1.0 / THETA)

    loop(depth, planes - depth, sweep, unroll)

    def last(i):
        x = second[i]
        near = beside(second, *w, i)
        step = KEEP * (x - first[i]) + GAIN * ((b[i] * (1.0 / scale) + near) * inverse[i] - x)
        store(i, x + step)

    loop(depth + 1, planes - depth - 1, last, unroll)


def slab_kernel(b, k, up_out, down_out):
    rows = k.shape[1]
    for r in range(K0):
        up_out[r] = k[:, rows - K0 + r, :]
        down_out[r] = k[:, r, :]
    for r in range(B0):
        up_out[K0 + r] = b[:, rows - B0 + r, :]
        down_out[K0 + r] = b[:, r, :]


def widen(out, own, low, high, first, count, start):
    planes, rows, lanes = own.shape
    end = start + rows
    out[:, 0:start, :] = jnp.zeros((planes, start, lanes), F32)
    out[:, end:, :] = jnp.zeros((planes, out.shape[1] - end, lanes), F32)
    out[:, start:end, :] = own[...]
    below, above = inside("gy", -1), inside("gy", 1)
    for r in range(count):
        out[:, start - count + r, :] = masked(below, low(first, r))
        out[:, end + r, :] = masked(above, high(first, r))


def widen_kernel(b, k, low, high, k_out, b_out, up_out, down_out):
    widen(k_out, k, lambda f, r: low[f + r], lambda f, r: high[f + r], 0, K0, R0)
    widen(b_out, b, lambda f, r: low[f + r], lambda f, r: high[f + r], K0, B0, R0)
    planes = k.shape[0]
    up_out[0:K0] = k_out[planes - K0 :]
    up_out[K0:] = b_out[planes - B0 :]
    down_out[0:K0] = k_out[0:K0]
    down_out[K0:] = b_out[0:B0]


def join(out, own, low, high, first, count, halo):
    planes = own.shape[0]
    left, right = inside("gx", -1), inside("gx", 1)
    out[halo : halo + planes] = own[...]
    for r in range(halo):
        below, above = halo - 1 - r, halo + planes + r
        if r < count:
            out[below] = masked(left, low[first + count - 1 - r])
            out[above] = masked(right, high[first + r])
        else:
            out[below] = jnp.zeros_like(out[below])
            out[above] = jnp.zeros_like(out[above])


def fine_down_kernel(
    k_own, b_own, low, high,
    k, b, s_out, b1_out, k1_out, up_out, down_out,
    wl, ws, wz, total, inverse, first, second, pairs, halves,
):
    join(k, k_own, low, high, 0, K0, K0)
    join(b, b_own, low, high, K0, B0, K0)
    w = (wl, ws, wz)
    weigh(k, wl, ws, wz, total, inverse, False, True, 1)
    planes, rows, lanes = b.shape
    pre_smooth(b, first, second, w, inverse, 1.0, 1, 2)
    own = planes - 2 * K0
    half = own // 2

    def residual(i):
        return b[i] - total[i] * second[i] + beside(second, *w, i)

    def restrict(j):
        i = 2 * j + K0
        pairs[j] = residual(i) + residual(i + 1)
        pairs[half + j] = k[i] + k[i + 1]

    loop(0, half, restrict, 1)
    matrix = halving(lanes, lanes // 2, 0.125)
    halves[...] = pick(pairs[...].reshape(2 * half * rows, lanes), matrix).reshape(halves.shape)
    count = (rows - 2 * R0) // 2
    both = halves[:, pl.ds(R0, count, stride=2), :] + halves[:, pl.ds(R0 + 1, count, stride=2), :]
    b1_out[...] = both[:half]
    k1_out[...] = both[half:]
    s_out[...] = second[K0 : K0 + own, R0 : rows - R0, :]
    for out, k_from, b_from, s_from in (
        (up_out, count - K1, count - B1, 2 * count - S0),
        (down_out, 0, 0, 0),
    ):
        at = 0
        for r in range(K1):
            out[at : at + half] = k1_out[:, k_from + r, :]
            at += half
        for r in range(B1):
            out[at : at + half] = b1_out[:, b_from + r, :]
            at += half
        for r in range(S0):
            for h in range(2):
                out[at : at + own] = s_out[:, s_from + r, h * lanes // 2 : (h + 1) * lanes // 2]
                at += own


def widen_both_kernel(b1, k1, s, low, high, k_out, b_out, s_out, up_out, down_out):
    half, own, lanes = b1.shape[0], s.shape[0], b1.shape[2]

    def block(ref):
        return lambda first, r: ref[first + r * half : first + (r + 1) * half]

    def wide(ref):
        def get(first, r):
            at = first + 2 * r * own
            return jnp.concatenate([ref[at : at + own], ref[at + own : at + 2 * own]], axis=1)

        return get

    widen(k_out, k1, block(low), block(high), 0, K1, R1)
    widen(b_out, b1, block(low), block(high), K1 * half, B1, R1)
    widen(s_out, s, wide(low), wide(high), (K1 + B1) * half, S0, R0)
    for out, k_from, b_from, s_from in (
        (up_out, half - K1, half - B1, own - S0),
        (down_out, 0, 0, 0),
    ):
        out[0:K1] = k_out[k_from : k_from + K1]
        out[K1 : K1 + B1] = b_out[b_from : b_from + B1]
        for r in range(S0):
            for h in range(2):
                out[K1 + B1 + 2 * r + h] = s_out[s_from + r, :, h * lanes : (h + 1) * lanes]


def middle_down_kernel(
    k_own, b_own, low, high,
    k, b, second, out,
    wl, ws, wz, total, inverse, first, pairs, halves,
):
    scale = 0.25
    join(k, k_own, low, high, 0, K1, K1)
    join(b, b_own, low, high, K1, B1, K1)
    w = (wl, ws, wz)
    weigh(k, wl, ws, wz, total, inverse, False, True, 1)
    second[...] = jnp.zeros_like(second)
    pre_smooth(b, first, second, w, inverse, scale, 1, 2)
    planes, rows, lanes = b.shape
    half = (planes - 2 * K1) // 2

    def residual(i):
        return b[i] - scale * (total[i] * second[i] - beside(second, *w, i))

    def restrict(j):
        i = 2 * j + K1
        pairs[j] = residual(i) + residual(i + 1)
        pairs[half + j] = k[i] + k[i + 1]

    loop(0, half, restrict, 2)
    size = half * rows
    fields = pick(pairs[0:half].reshape(size, lanes), halving(lanes, lanes, 0.125))
    conducts = pick(pairs[half:].reshape(size, lanes), halving(lanes, lanes, 0.125, lanes // 2))
    halves[...] = (fields + conducts).reshape(halves.shape)
    count = (rows - 2 * R1) // 2
    both = halves[:, pl.ds(R1, count, stride=2), :] + halves[:, pl.ds(R1 + 1, count, stride=2), :]
    for i in range(half):
        out[0, pl.ds(i, count, stride=half), :] = both[i]

    def copy(d):
        out[d] = out[0]

    loop(1, out.shape[0], copy, 1)


def coarse_down(k, b, w, total, inverse, first, second, scale, valid, k_next, b_next):
    planes, rows, lanes = k.shape
    row_edge = True
    weigh(k, *w, total, inverse, row_edge, False, 2)
    for ref in (first, second):
        for end in (0, planes - 1):
            ref[end] = jnp.zeros((rows, lanes), F32)
    pre_smooth_whole(b, first, second, w, inverse, scale, 2)
    half = (planes - 2) // 2

    def residual(i):
        return b[i] - scale * (total[i] * second[i] - beside(second, *w, i))

    def restrict(j):
        i = 2 * j + 1
        first[j] = residual(i) + residual(i + 1)
        first[half + j] = k[i] + k[i + 1]

    loop(0, half, restrict, 2)
    size = 2 * half * rows
    matrix = halving(lanes, lanes, 0.125, 0, valid)
    pairs = first[0 : 2 * half].reshape(size, lanes)
    halves = total.at[0 : 2 * half]
    halves[...] = pick(pairs, matrix).reshape(halves.shape)
    count = rows // 2
    both = halves[:, pl.ds(0, count, stride=2), :] + halves[:, pl.ds(1, count, stride=2), :]
    b_next[1 : half + 1] = both[:half]
    k_next[1 : half + 1] = both[half:]
    for end in (0, half + 1):
        k_next[end] = jnp.zeros(k_next.shape[1:], F32)
        b_next[end] = jnp.zeros(b_next.shape[1:], F32)


def pre_smooth_whole(b, first, second, w, inverse, scale, unroll):
    planes = b.shape[0]

    def start(i):
        first[i] = b[i] * inverse[i] * (1.0 / (scale * THETA))

    loop(1, planes - 1, start, unroll)

    def sweep(i):
        near = beside(first, *w, i)
        second[i] = (1.0 + KEEP + GAIN * (THETA - 1.0)) * first[i] + GAIN * (inverse[i] * near)

    loop(1, planes - 1, sweep, unroll)


def coarse_up(correction, b, w, inverse, first, second, scale, valid, grown):
    planes, rows, lanes = b.shape
    half, count = correction.shape[0], correction.shape[1]
    wide = pick(correction.reshape(half * count, lanes), doubling(lanes, lanes, valid // 2))
    wide = wide.reshape(half, count, lanes)
    grown[:, pl.ds(0, count, stride=2), :] = wide
    grown[:, pl.ds(1, count, stride=2), :] = wide
    for end in (0, planes - 1):
        first[end] = jnp.zeros((rows, lanes), F32)

    def add(j):
        i = 2 * j + 1
        first[i] = second[i] + grown[j]
        first[i + 1] = second[i + 1] + grown[j]

    loop(0, half, add, 2)

    def sweep(i):
        x = first[i]
        near = beside(first, *w, i)
        second[i] = x + ((b[i] * (1.0 / scale) + near) * inverse[i] - x) * (1.0 / THETA)

    loop(1, planes - 1, sweep, 2)

    def last(i):
        x = second[i]
        near = beside(second, *w, i)
        step = KEEP * (x - first[i]) + GAIN * ((b[i] * (1.0 / scale) + near) * inverse[i] - x)
        first[i] = x + step

    loop(1, planes - 1, last, 2)


def bottom(k, b, scale):
    planes, rows, lanes = k.shape
    none = jnp.zeros((1, rows, lanes), F32)

    def after(v):
        return jnp.concatenate([v[1:], none], axis=0)

    def before(v):
        return jnp.concatenate([none, v[:-1]], axis=0)

    lead = face(k, after(k))
    lead_low = jnp.concatenate([k[:1], lead[:-1]], axis=0)
    row = iota(k.shape, 1)
    next_row = jnp.where(row == rows - 1, 0.0, up(k, 1))
    row_w = face(k, next_row)
    row_low = jnp.where(row == 0, k, down(row_w, 1))
    lane_w = face(k, up(k, 2))
    lane_low = down(lane_w, 2)
    whole = ((lead + lead_low) + (row_w + row_low)) + (lane_w + lane_low)
    inverse = jnp.where(k > 0.0, 1.0 / whole, 0.0)
    source = b * inverse * (1.0 / scale)
    lead_i, lead_low_i = lead * inverse, lead_low * inverse
    row_i = jnp.where(row == rows - 1, 0.0, row_w) * inverse
    row_low_i = jnp.where(row == 0, 0.0, row_low) * inverse
    lane_i, lane_low_i = lane_w * inverse, lane_low * inverse
    sigma = BOTTOM_THETA / BOTTOM_DELTA
    rho = 1.0 / sigma
    step = source * (1.0 / BOTTOM_THETA)
    x = step
    for _ in range(BOTTOM - 1):
        following = 1.0 / (2.0 * sigma - rho)
        near = (lead_i * after(x) + lead_low_i * before(x)) + (
            row_i * up(x, 1) + row_low_i * down(x, 1)
        )
        near = near + (lane_i * up(x, 2) + lane_low_i * down(x, 2))
        step = (following * rho) * step + (2.0 * following / BOTTOM_DELTA) * (source - x + near)
        x = x + step
        rho = following
    return x


def coarse_kernel(
    valid, received, region,
    k2, b2, wl2, ws2, wz2, total2, inverse2, first2, second2,
    k3, b3, wl3, ws3, wz3, total3, inverse3, first3, second3,
    k4, b4, grown2, grown3,
):
    planes, rows, lanes = k2.shape
    across, along = lax.axis_size("gx"), lax.axis_size("gy")
    block_x, block_y = rows // across, (planes - 2) // along
    lane = iota((block_x, lanes), 1)
    zero = jnp.zeros((rows, lanes), F32)
    for end in (0, planes - 1):
        k2[end] = zero
        b2[end] = zero

    def place(column):
        for row in range(across):
            for j in range(block_y):
                piece = received[row * along + column, j * block_x : (j + 1) * block_x, :]
                field = jnp.where(lane < valid, piece, 0.0)
                conduct = jnp.where(lane < valid, pltpu.roll(piece, lanes - valid, 1), 0.0)
                b2[1 + column * block_y + j, row * block_x : (row + 1) * block_x, :] = field
                k2[1 + column * block_y + j, row * block_x : (row + 1) * block_x, :] = conduct

    loop(0, along, place, 1)
    w2, w3 = (wl2, ws2, wz2), (wl3, ws3, wz3)
    coarse_down(
        k2, b2, w2, total2, inverse2, first2, second2, 0.25**2, valid, k3, b3
    )
    coarse_down(
        k3, b3, w3, total3, inverse3, first3, second3, 0.25**3, valid // 2, k4, b4
    )
    own4 = k4.shape[0] - 2
    x4 = bottom(k4[1 : own4 + 1], b4[1 : own4 + 1], 0.25**4)

    coarse_up(x4, b3, w3, inverse3, first3, second3, 0.25**3, valid // 2, grown3)
    own3 = k3.shape[0] - 2
    coarse_up(
        first3[1 : own3 + 1], b2, w2, inverse2, first2, second2, 0.25**2, valid, grown2
    )
    column, row = lax.axis_index("gy"), lax.axis_index("gx")
    margin = (region.shape[0] - block_y) // 2
    for q in range(region.shape[0]):
        plane = column * block_y + q - margin
        for side in range(3):
            block = row + side - 1
            there = (plane >= 0) & (plane < planes - 2) & (block >= 0) & (block < across)
            start = pl.multiple_of(jnp.clip(block, 0, across - 1) * block_x, block_x)
            value = first2[1 + jnp.clip(plane, 0, planes - 3), pl.ds(start, block_x), :]
            region[q, side * block_x : (side + 1) * block_x, :] = masked(there, value)


def fine_up_kernel(
    valid, region, k1, b1, s1, k, b, s_own, low, high,
    field_out, residual_out,
    wl1, ws1, wz1, total1, inverse1, first1, second1, grown,
    s, wl, ws, wz, total, inverse, second, tall,
):
    planes1, rows1, lanes1 = k1.shape
    planes, rows, lanes = k.shape
    weigh(k1, wl1, ws1, wz1, total1, inverse1, False, True, 1)
    weigh(k, wl, ws, wz, total, inverse, False, True, 1)
    w1, w = (wl1, ws1, wz1), (wl, ws, wz)
    count_y, count_x = region.shape[0], region.shape[1]
    block_x = count_x // 3
    wide = pick(region[...].reshape(count_y * count_x, lanes1), doubling(lanes1, lanes1, valid))
    wide = wide.reshape(count_y, count_x, lanes1)
    margin = 2
    grown[...] = jnp.zeros_like(grown)
    for q in range(block_x + 2 * margin):
        line = wide[:, block_x - margin + q, :]
        at = R1 - 2 * margin
        grown[q, pl.ds(at, count_y, stride=2), :] = line
        grown[q, pl.ds(at + 1, count_y, stride=2), :] = line
    begin = K1 - 2 * margin
    first1[...] = s1[...]

    def add1(q):
        for side in range(2):
            first1[begin + 2 * q + side] = first1[begin + 2 * q + side] + grown[q]

    loop(0, block_x + 2 * margin, add1, 1)
    depth = K1 - 3

    def store1(i, value):
        first1[i] = value

    post_smooth(b1, first1, second1, w1, inverse1, 0.25, depth, 2, store1)
    join(s, s_own, low, high, 0, S0, S0)
    own1 = planes1 - 2 * K1
    count = own1 + 4
    begin = K1 - 2
    part = (rows - 2 * R0) // 2 + 4
    source = first1[begin : begin + count, R1 - 2 : R1 - 2 + part, :]
    tall[:, pl.ds(0, part, stride=2), :] = source
    tall[:, pl.ds(1, part, stride=2), :] = source
    matrix = doubling(lanes1, lanes, lanes1)

    def add(q):
        grown_plane = pick(tall[q], matrix)
        for side in range(2):
            i = 2 * q + side - 1

            @pl.when((i >= 0) & (i < planes))
            def _():
                s[i] = s[i] + grown_plane

    loop(0, count, add, 1)

    def store(i, value):
        s[i] = value

    post_smooth(b, s, second, w, inverse, 1.0, 1, 2, store)
    own = planes - 2 * K0

    def finish(j):
        i = j + K0
        x = s[i]
        rest = b[i] - total[i] * x + beside(s, *w, i)
        field_out[j] = x[R0 : rows - R0, :]
        residual_out[j] = rest[R0 : rows - R0, :]

    loop(0, own, finish, 2)


def call(kernel, outs, scratch=()):
    def run(*operands):
        shapes = [operand.shape for operand in operands] + list(outs) + list(scratch)
        words = sum(math.prod(s[:-2]) * (-(-s[-2] // 8) * 8) * s[-1] for s in shapes)
        return pl.pallas_call(
            kernel,
            out_shape=[jax.ShapeDtypeStruct(shape, F32) for shape in outs],
            scratch_shapes=[pltpu.VMEM(shape, F32) for shape in scratch],
            compiler_params=pltpu.CompilerParams(vmem_limit_bytes=4 * words + SPARE),
        )(*operands)

    return run


def per_device(right_side, coefficient):
    bx, by, nz = right_side.shape
    across, along = lax.axis_size("gx"), lax.axis_size("gy")
    devices = across * along
    hx, hy, hz = bx // 2, by // 2, nz // 2
    tall, tall1 = by + 2 * R0, hy + 2 * R1

    slab = (K0 + B0, bx, nz)
    up_rows, down_rows = call(slab_kernel, [slab, slab])(right_side, coefficient)
    low, high = rotate(up_rows, "gy", 1), rotate(down_rows, "gy", -1)

    plane = (bx, tall, nz)
    slab = (K0 + B0, tall, nz)
    k_own, b_own, up_planes, down_planes = call(widen_kernel, [plane, plane, slab, slab])(
        right_side, coefficient, low, high
    )
    low, high = rotate(up_planes, "gx", 1), rotate(down_planes, "gx", -1)

    block = (bx + 2 * K0, tall, nz)
    level1 = (hx, hy, hz)
    message = ((K1 + B1) * hx + S0 * 2 * bx, hz)
    k, b, s, b1, k1, up_rows, down_rows = call(
        fine_down_kernel,
        [block, block, (bx, by, nz), level1, level1, message, message],
        [block] * 7 + [(bx, tall, nz), (bx, tall, hz)],
    )(k_own, b_own, low, high)
    low, high = rotate(up_rows, "gy", 1), rotate(down_rows, "gy", -1)

    message = (K1 + B1 + 2 * S0, tall1, hz)
    k1_own, b1_own, s_own, up_planes, down_planes = call(
        widen_both_kernel,
        [(hx, tall1, hz), (hx, tall1, hz), plane, message, message],
    )(b1, k1, s, low, high)
    low, high = rotate(up_planes, "gx", 1), rotate(down_planes, "gx", -1)

    block1 = (hx + 2 * K1, tall1, hz)
    piece = (hx // 2) * (hy // 2)
    k1, b1, s1, copies = call(
        middle_down_kernel,
        [block1, block1, block1, (devices, piece, hz)],
        [block1] * 6 + [(hx, tall1, hz), (hx // 2, tall1, hz)],
    )(k1_own, b1_own, low, high)
    received = lax.all_to_all(copies, ("gx", "gy"), 0, 0, tiled=True)

    x2, y2 = across * hx // 2, along * hy // 2
    level2, level3, level4 = (
        (y2 // s + 2, x2 // s, hz) for s in (1, 2, 4)
    )
    margin = 2
    (region,) = call(
        partial(coarse_kernel, nz // 4),
        [(hy // 2 + 2 * margin, 3 * hx // 2, hz)],
        [level2] * 9 + [level3] * 9 + [level4] * 2 + [(y2 // 2, x2, hz), (y2 // 4, x2 // 2, hz)],
    )(received)
    s_low, s_high = spread(low, K1 + B1, tall), spread(high, K1 + B1, tall)
    field, residual = call(
        partial(fine_up_kernel, nz // 4),
        [(bx, by, nz)] * 2,
        [block1] * 7 + [(hx // 2 + 2 * margin, tall1, hz)] + [block] * 7
        + [(hx + 4, tall, hz)],
    )(region, k1, b1, s1, k, b, s_own, s_low, s_high)
    return field, residual


def spread(message, first, rows):
    parts = message[first:, :rows]
    return jnp.concatenate([parts[0::2], parts[1::2]], axis=2)


def solution(mesh):
    in_specs = (P("gx", "gy", None), P("gx", "gy", None))
    out_specs = (P("gx", "gy", None), P("gx", "gy", None))

    return jax.shard_map(
        per_device, mesh=mesh, in_specs=in_specs, out_specs=out_specs, check_vma=False
    )
```

```python
import math
from functools import partial

import jax
import jax.numpy as jnp
from jax import lax
from jax.experimental import pallas as pl
from jax.experimental.pallas import tpu as pltpu
from jax.sharding import PartitionSpec as P

F32 = jnp.float32
BF16 = jnp.bfloat16

THETA = 1.25
DELTA = 0.75
SIGMA = THETA / DELTA
RHO0 = 1.0 / SIGMA
RHO1 = 1.0 / (2.0 * SIGMA - RHO0)
KEEP = RHO1 * RHO0
GAIN = 2.0 * RHO1 / DELTA
BOTTOM = 8
BOTTOM_THETA = (2.0 + 0.05) / 2.0
BOTTOM_DELTA = (2.0 - 0.05) / 2.0

K0, B0, S0 = 3, 2, 3
K1, B1, S1 = 4, 3, 4
EDGE = 2
UNROLL = 8
SPARE = 4 * 1024 * 1024


def rotate(value, axis, shift):
    size = lax.axis_size(axis)
    return lax.ppermute(value, axis, [(i, (i + shift) % size) for i in range(size)])


def inside(axis, side):
    index = lax.axis_index(axis)
    if side < 0:
        return index > 0
    return index < lax.axis_size(axis) - 1


def masked(flag, value):
    return jnp.where(flag, value, jnp.zeros_like(value))


def iota(shape, dim):
    return lax.broadcasted_iota(jnp.int32, shape, dim)


def pick(x, matrix):
    high = x.astype(BF16)
    low = (x - high.astype(F32)).astype(BF16)
    return jnp.dot(high, matrix, preferred_element_type=F32) + jnp.dot(
        low, matrix, preferred_element_type=F32
    )


def halving(fine, coarse, valid):
    row, col = iota((fine, coarse), 0), iota((fine, coarse), 1)
    return jnp.where((row // 2 == col) & (row < valid), 0.125, 0.0).astype(BF16)


def doubling(coarse, fine, valid):
    row, col = iota((coarse, fine), 0), iota((coarse, fine), 1)
    return jnp.where((row == col // 2) & (row < valid), 1.0, 0.0).astype(BF16)


def face(a, b):
    product, total = a * b, a + b
    return jnp.where(product > 0.0, 2.0 * product / total, total)


def up(x, axis):
    return pltpu.roll(x, x.shape[axis] - 1, axis)


def down(x, axis):
    return pltpu.roll(x, 1, axis)


def sided(k, axis, edged):
    size = k.shape[axis]
    after = up(k, axis)
    place = iota(k.shape, axis)
    if edged:
        after = jnp.where(place == size - 1, 0.0, after)
    w = face(k, after)
    low = down(w, axis)
    if edged:
        low = jnp.where(place == 0, k, low)
        return jnp.where(place == size - 1, 0.0, w), w + low
    return w, w + low


def loop(low, high, body):
    def step(i, carry):
        body(i)
        return carry

    lax.fori_loop(low, high, step, 0, unroll=min(UNROLL, high - low))


def weigh(k, wl, ws, wz, total, inverse, row_edge, lane_edge):
    planes = k.shape[0]

    def body(i, before):
        here = k[i]
        lead = face(here, k[i + 1])
        rows, row_sum = sided(here, 0, row_edge)
        lanes, lane_sum = sided(here, 1, lane_edge)
        wl[i] = lead
        ws[i] = rows
        wz[i] = lanes
        whole = (before + lead) + (row_sum + lane_sum)
        total[i] = whole
        inverse[i] = jnp.where(here > 0.0, 1.0 / whole, 0.0)
        return lead

    lax.fori_loop(0, planes - 1, body, jnp.zeros(k.shape[1:], F32), unroll=UNROLL)


def beside(x, w, i):
    wl, ws, wz = w
    here = x[i]
    rows, lanes = ws[i], wz[i]
    out = wl[i] * x[i + 1] + wl[i - 1] * x[i - 1]
    out = out + (rows * up(here, 0) + down(rows * here, 0))
    return out + (lanes * up(here, 1) + down(lanes * here, 1))


def pre_smooth(b, first, second, w, inverse, scale, outer, inner):
    def start(i):
        first[i] = b[i] * inverse[i] * (1.0 / (scale * THETA))

    loop(*outer, start)

    def sweep(i):
        near = beside(first, w, i)
        second[i] = (1.0 + KEEP + GAIN * (THETA - 1.0)) * first[i] + GAIN * (inverse[i] * near)

    loop(*inner, sweep)


def post_smooth(b, first, second, w, inverse, scale, outer, inner):
    def sweep(i):
        x = first[i]
        near = beside(first, w, i)
        second[i] = x + ((b[i] * (1.0 / scale) + near) * inverse[i] - x) * (1.0 / THETA)

    loop(*outer, sweep)

    def last(i):
        x = second[i]
        near = beside(second, w, i)
        step = KEEP * (x - first[i]) + GAIN * ((b[i] * (1.0 / scale) + near) * inverse[i] - x)
        first[i] = x + step

    loop(*inner, last)


def residual(b, field, w, total, scale, i):
    return b[i] - scale * (total[i] * field[i] - beside(field, w, i))


def coarser(pairs, halves, valid):
    planes, rows, lanes = pairs.shape
    matrix = halving(lanes, halves.shape[2], valid)
    halves[...] = pick(pairs.reshape(planes * rows, lanes), matrix).reshape(halves.shape)
    count = rows // 2
    return halves[:, pl.ds(0, count, stride=2), :] + halves[:, pl.ds(1, count, stride=2), :]


def packed(pairs, halves, valid):
    planes, rows, lanes = pairs.shape
    matrix = halving(lanes, halves.shape[2], valid)
    halves[...] = pick(pairs.reshape(planes * rows, lanes), matrix).reshape(halves.shape)
    count = rows // 4
    quarter = [halves[:, pl.ds(r, count, stride=4), :] for r in range(4)]
    odd = pltpu.roll(quarter[2] + quarter[3], halves.shape[2] // 2, 2)
    return (quarter[0] + quarter[1]) + odd


def spread_copies(out, rows):
    size, count = rows.shape[0], rows.shape[1]
    for i in range(size):
        out[0, pl.ds(i, count, stride=size), :] = rows[i]

    def copy(d):
        out[d] = out[0]

    loop(1, out.shape[0], copy)


def slab_kernel(b, k, up_out, down_out):
    rows = k.shape[1]
    for r in range(K0):
        up_out[r] = k[:, rows - K0 + r, :]
        down_out[r] = k[:, r, :]
    for r in range(B0):
        up_out[K0 + r] = b[:, rows - B0 + r, :]
        down_out[K0 + r] = b[:, r, :]


def conduct_kernel(k, k1, copies, pairs, halves, pairs1, halves1):
    def add(j):
        pairs[j] = k[2 * j] + k[2 * j + 1]

    loop(0, pairs.shape[0], add)
    k1[...] = coarser(pairs[...], halves, k.shape[2])

    def add1(j):
        pairs1[j] = k1[2 * j] + k1[2 * j + 1]

    loop(0, pairs1.shape[0], add1)
    spread_copies(copies, packed(pairs1[...], halves1, k1.shape[2]))


def widen(out, own, low, high, count):
    planes, rows, lanes = own.shape
    size = out.shape[1]
    out[:, 0:rows, :] = own[...]
    out[:, rows:, :] = jnp.zeros((planes, size - rows, lanes), F32)
    below, above = inside("gy", -1), inside("gy", 1)
    for r in range(count):
        out[:, size - count + r, :] = masked(below, low(r))
        out[:, rows + r, :] = masked(above, high(r))


def widen_kernel(b, k, low, high, k_out, b_out, up_out, down_out):
    widen(k_out, k, lambda r: low[r], lambda r: high[r], K0)
    widen(b_out, b, lambda r: low[K0 + r], lambda r: high[K0 + r], B0)
    planes = k.shape[0]
    up_out[0:K0] = k_out[planes - K0 :]
    up_out[K0:] = b_out[planes - B0 :]
    down_out[0:K0] = k_out[0:K0]
    down_out[K0:] = b_out[0:B0]


def join(out, own, low, high, count, halo):
    planes = own.shape[0]
    left, right = inside("gx", -1), inside("gx", 1)
    out[halo : halo + planes] = own[...]
    for r in range(halo):
        below, above = halo - 1 - r, halo + planes + r
        if r < count:
            out[below] = masked(left, low(count - 1 - r))
            out[above] = masked(right, high(r))
        else:
            out[below] = jnp.zeros(out.shape[1:], F32)
            out[above] = jnp.zeros(out.shape[1:], F32)


def fine_down_kernel(
    k_own, b_own, low, high, k1,
    wl, ws, wz, total, inverse, b, s_out, b1_out, up_out, down_out,
    k, first, second, pairs, halves,
):
    join(k, k_own, lambda r: low[r], lambda r: high[r], K0, K0)
    join(b, b_own, lambda r: low[K0 + r], lambda r: high[K0 + r], B0, K0)
    w = (wl, ws, wz)
    weigh(k, wl, ws, wz, total, inverse, False, True)
    planes, lanes = b.shape[0], b.shape[2]
    own, rows = planes - 2 * K0, s_out.shape[1]
    pre_smooth(b, first, second, w, inverse, 1.0, (1, planes - 1), (2, planes - 2))

    def restrict(j):
        i = 2 * j + K0
        both = residual(b, second, w, total, 1.0, i) + residual(b, second, w, total, 1.0, i + 1)
        pairs[j] = both[0:rows]

    loop(0, own // 2, restrict)
    b1_out[...] = coarser(pairs[...], halves, lanes)
    s_out[...] = second[K0 : K0 + own, 0:rows, :]
    half, count = b1_out.shape[0], b1_out.shape[1]
    for out, k_from, b_from in ((up_out, count - K1, count - B1), (down_out, 0, 0)):
        for r in range(K1):
            out[r] = k1[:, k_from + r, :]
        for r in range(B1):
            out[K1 + r] = b1_out[:, b_from + r, :]


def widen_middle_kernel(k1, b1, low, high, k_out, b_out, up_out, down_out):
    widen(k_out, k1, lambda r: low[r], lambda r: high[r], K1)
    widen(b_out, b1, lambda r: low[K1 + r], lambda r: high[K1 + r], B1)
    planes = k1.shape[0]
    up_out[0:K1] = k_out[planes - K1 :]
    up_out[K1:] = b_out[planes - B1 :]
    down_out[0:K1] = k_out[0:K1]
    down_out[K1:] = b_out[0:B1]


def middle_down_kernel(
    k_own, b_own, low, high, s,
    wl, ws, wz, total, inverse, b, s_out, copies, up_out, down_out,
    k, first, second, pairs, halves,
):
    scale = 0.25
    join(k, k_own, lambda r: low[r], lambda r: high[r], K1, K1)
    join(b, b_own, lambda r: low[K1 + r], lambda r: high[K1 + r], B1, K1)
    w = (wl, ws, wz)
    weigh(k, wl, ws, wz, total, inverse, False, True)
    planes, lanes = b.shape[0], b.shape[2]
    own, rows = planes - 2 * K1, s_out.shape[1]
    pre_smooth(b, first, second, w, inverse, scale, (1, planes - 1), (2, planes - 2))

    def restrict(j):
        i = 2 * j + K1
        both = residual(b, second, w, total, scale, i) + residual(b, second, w, total, scale, i + 1)
        pairs[j] = both[0:rows]

    loop(0, own // 2, restrict)
    spread_copies(copies, packed(pairs[...], halves, lanes))
    s_out[...] = second[K1 : K1 + own, 0:rows, :]
    fine, fine_rows = s.shape[0], s.shape[1]
    for out, from0, from1 in ((up_out, fine_rows - S0, rows - S1), (down_out, 0, 0)):
        for r in range(S0):
            for h in range(2):
                at = (2 * r + h) * fine
                out[at : at + fine] = s[:, from0 + r, h * lanes : (h + 1) * lanes]
        for r in range(S1):
            at = 2 * S0 * fine + r * own
            out[at : at + own] = s_out[:, from1 + r, :]


def widen_fields_kernel(s, s1, low, high, s_out, s1_out, up_out, down_out):
    fine, own, lanes = s.shape[0], s1.shape[0], s1.shape[2]

    def wide(ref):
        def get(r):
            at = 2 * r * fine
            return jnp.concatenate([ref[at : at + fine], ref[at + fine : at + 2 * fine]], axis=1)

        return get

    def block(ref):
        def get(r):
            at = 2 * S0 * fine + r * own
            return ref[at : at + own]

        return get

    widen(s_out, s, wide(low), wide(high), S0)
    widen(s1_out, s1, block(low), block(high), S1)
    rows, rows1 = s_out.shape[1], s1_out.shape[1]
    for out, from0, from1 in ((up_out, fine - S0, own - S1), (down_out, 0, 0)):
        for r in range(S0):
            for h in range(2):
                at = (2 * r + h) * rows
                out[at : at + rows] = s_out[from0 + r, :, h * lanes : (h + 1) * lanes]
        for r in range(S1):
            at = 2 * S0 * rows + r * rows1
            out[at : at + rows1] = s1_out[from1 + r]


def unpack(received, out, block_x, block_y, across, along):
    planes, rows, lanes = out.shape
    lane = iota((block_x, lanes), 1)
    for end in (0, planes - 1):
        out[end] = jnp.zeros((rows, lanes), F32)

    def place(column):
        for row in range(across):
            for j in range(block_y // 2):
                piece = received[row * along + column, j * block_x : (j + 1) * block_x, :]
                at = 1 + column * block_y + 2 * j
                span = slice(row * block_x, (row + 1) * block_x)
                out[at, span, :] = jnp.where(lane < lanes // 2, piece, 0.0)
                other = pltpu.roll(piece, lanes // 2, 1)
                out[at + 1, span, :] = jnp.where(lane < lanes // 2, other, 0.0)

    loop(0, along, place)


def clear_ends(ref):
    for end in (0, ref.shape[0] - 1):
        ref[end] = jnp.zeros(ref.shape[1:], F32)


def coarse_weights_kernel(
    valid, received,
    wl2, ws2, wz2, total2, inverse2, wl3, ws3, wz3, total3, inverse3, k4,
    k2, k3, pairs2, halves2, pairs3, halves3,
):
    planes, rows, lanes = k2.shape
    across, along = lax.axis_size("gx"), lax.axis_size("gy")
    unpack(received, k2, rows // across, (planes - 2) // along, across, along)

    def add2(j):
        pairs2[j] = k2[2 * j + 1] + k2[2 * j + 2]

    loop(0, pairs2.shape[0], add2)
    clear_ends(k3)
    k3[1 : k3.shape[0] - 1] = coarser(pairs2[...], halves2, valid)

    def add3(j):
        pairs3[j] = k3[2 * j + 1] + k3[2 * j + 2]

    loop(0, pairs3.shape[0], add3)
    k4[...] = coarser(pairs3[...], halves3, valid // 2)
    weigh(k2, wl2, ws2, wz2, total2, inverse2, True, False)
    weigh(k3, wl3, ws3, wz3, total3, inverse3, True, False)


def coarse_down(b, w, total, inverse, first, second, scale, valid, pairs, halves):
    ends = (1, b.shape[0] - 1)
    clear_ends(first)
    clear_ends(second)
    pre_smooth(b, first, second, w, inverse, scale, ends, ends)

    def restrict(j):
        i = 2 * j + 1
        pairs[j] = residual(b, second, w, total, scale, i) + residual(
            b, second, w, total, scale, i + 1
        )

    loop(0, pairs.shape[0], restrict)
    return coarser(pairs[...], halves, valid)


def coarse_up(correction, b, w, inverse, first, second, scale, valid, grown):
    planes, rows, lanes = b.shape
    half, count = correction.shape[0], correction.shape[1]
    wide = pick(correction.reshape(half * count, lanes), doubling(lanes, lanes, valid // 2))
    wide = wide.reshape(half, count, lanes)
    grown[:, pl.ds(0, count, stride=2), :] = wide
    grown[:, pl.ds(1, count, stride=2), :] = wide

    def add(j):
        i = 2 * j + 1
        first[i] = second[i] + grown[j]
        first[i + 1] = second[i + 1] + grown[j]

    loop(0, half, add)
    ends = (1, planes - 1)
    post_smooth(b, first, second, w, inverse, scale, ends, ends)


def bottom(k, b, scale):
    planes, rows, lanes = k.shape
    none = jnp.zeros((1, rows, lanes), F32)

    def after(v):
        return jnp.concatenate([v[1:], none], axis=0)

    def before(v):
        return jnp.concatenate([none, v[:-1]], axis=0)

    lead = face(k, after(k))
    lead_low = jnp.concatenate([k[:1], lead[:-1]], axis=0)
    row = iota(k.shape, 1)
    row_w = face(k, jnp.where(row == rows - 1, 0.0, up(k, 1)))
    row_low = jnp.where(row == 0, k, down(row_w, 1))
    lane_w = face(k, up(k, 2))
    lane_low = down(lane_w, 2)
    whole = ((lead + lead_low) + (row_w + row_low)) + (lane_w + lane_low)
    inverse = jnp.where(k > 0.0, 1.0 / whole, 0.0)
    source = b * inverse * (1.0 / scale)
    lead_i, lead_low_i = lead * inverse, lead_low * inverse
    row_i = jnp.where(row == rows - 1, 0.0, row_w) * inverse
    row_low_i = jnp.where(row == 0, 0.0, row_low) * inverse
    lane_i, lane_low_i = lane_w * inverse, lane_low * inverse
    sigma = BOTTOM_THETA / BOTTOM_DELTA
    rho = 1.0 / sigma
    step = source * (1.0 / BOTTOM_THETA)
    x = step
    for _ in range(BOTTOM - 1):
        following = 1.0 / (2.0 * sigma - rho)
        near = (lead_i * after(x) + lead_low_i * before(x)) + (
            row_i * up(x, 1) + row_low_i * down(x, 1)
        )
        near = near + (lane_i * up(x, 2) + lane_low_i * down(x, 2))
        step = (following * rho) * step + (2.0 * following / BOTTOM_DELTA) * (source - x + near)
        x = x + step
        rho = following
    return x


def coarse_kernel(
    valid, received, wl2, ws2, wz2, total2, inverse2, wl3, ws3, wz3, total3, inverse3, k4,
    region,
    b2, first2, second2, pairs2, halves2, b3, first3, second3, pairs3, halves3, grown2, grown3,
):
    planes, rows, lanes = b2.shape
    across, along = lax.axis_size("gx"), lax.axis_size("gy")
    block_x, block_y = rows // across, (planes - 2) // along
    unpack(received, b2, block_x, block_y, across, along)
    w2, w3 = (wl2, ws2, wz2), (wl3, ws3, wz3)
    clear_ends(b3)
    own3 = b3.shape[0] - 2
    b3[1 : own3 + 1] = coarse_down(
        b2, w2, total2, inverse2, first2, second2, 0.25**2, valid, pairs2, halves2
    )
    b4 = coarse_down(
        b3, w3, total3, inverse3, first3, second3, 0.25**3, valid // 2, pairs3, halves3
    )
    x4 = bottom(k4[...], b4, 0.25**4)
    coarse_up(x4, b3, w3, inverse3, first3, second3, 0.25**3, valid // 2, grown3)
    coarse_up(
        first3[1 : own3 + 1], b2, w2, inverse2, first2, second2, 0.25**2, valid, grown2
    )
    column, row = lax.axis_index("gy"), lax.axis_index("gx")
    for q in range(region.shape[0]):
        plane = column * block_y + q - EDGE
        for side in range(3):
            block = row + side - 1
            there = (plane >= 0) & (plane < planes - 2) & (block >= 0) & (block < across)
            start = pl.multiple_of(jnp.clip(block, 0, across - 1) * block_x, block_x)
            value = first2[1 + jnp.clip(plane, 0, planes - 3), pl.ds(start, block_x), :]
            region[q, side * block_x : (side + 1) * block_x, :] = masked(there, value)


def fine_up_kernel(
    valid, region, wl1, ws1, wz1, inverse1, b1, s1_own,
    wl, ws, wz, total, inverse, b, s_own, low, high,
    field_out, residual_out,
    first1, second1, grown, s, second, tall, thick,
):
    planes1, rows1, lanes1 = b1.shape
    planes, rows, lanes = b.shape
    w1, w = (wl1, ws1, wz1), (wl, ws, wz)

    def wide(ref):
        def get(r):
            at = 2 * r * rows
            return jnp.concatenate([ref[at : at + rows], ref[at + rows : at + 2 * rows]], axis=1)

        return get

    def block(ref):
        def get(r):
            at = 2 * S0 * rows + r * rows1
            return ref[at : at + rows1]

        return get

    join(s, s_own, wide(low), wide(high), S0, S0)
    join(first1, s1_own, block(low), block(high), S1, S1)
    count_y, count_x = region.shape[0], region.shape[1]
    block_x = count_x // 3
    expanded = pick(region[...].reshape(count_y * count_x, lanes1), doubling(lanes1, lanes1, valid))
    expanded = expanded.reshape(count_y, count_x, lanes1)
    own_y = count_y - 2 * EDGE
    for q in range(block_x + 2 * EDGE):
        line = expanded[:, block_x - EDGE + q, :]
        line = jnp.concatenate([line[EDGE:], line[:EDGE]], axis=0)
        grown[q, pl.ds(0, count_y, stride=2), :] = line
        grown[q, pl.ds(1, count_y, stride=2), :] = line

    def add1(q):
        for side in range(2):
            first1[2 * q + side] = first1[2 * q + side] + grown[q]

    loop(0, block_x + 2 * EDGE, add1)
    post_smooth(
        b1, first1, second1, w1, inverse1, 0.25, (1, planes1 - 1), (2, planes1 - 2)
    )
    begin, count = S1 - EDGE, planes1 - 2 * S1 + 2 * EDGE
    own1 = rows1 - 2 * S1
    edge = 2 * EDGE
    for half, at, where in ((own1 + EDGE, 0, 0), (EDGE, rows1 - EDGE, 2 * (own1 + EDGE))):
        part = first1[begin : begin + count, at : at + half, :]
        tall[:, pl.ds(where, half, stride=2), :] = part
        tall[:, pl.ds(where + 1, half, stride=2), :] = part
    matrix = doubling(lanes1, lanes, lanes1)
    thick[...] = pick(tall[...].reshape(count * rows, lanes1), matrix).reshape(thick.shape)
    s[0] = s[0] + thick[0]
    s[planes - 1] = s[planes - 1] + thick[count - 1]

    def add(q):
        for side in range(2):
            i = 2 * q + side - 1
            s[i] = s[i] + thick[q]

    loop(1, count - 1, add)
    post_smooth(b, s, second, w, inverse, 1.0, (1, planes - 1), (2, planes - 2))
    own, own_rows = field_out.shape[0], field_out.shape[1]

    def finish(j):
        i = j + K0
        field_out[j] = s[i, 0:own_rows, :]
        residual_out[j] = residual(b, s, w, total, 1.0, i)[0:own_rows]

    loop(0, own, finish)


def call(kernel, outs, scratch=()):
    def run(*operands):
        shapes = [operand.shape for operand in operands] + list(outs) + list(scratch)
        words = sum(math.prod(s[:-2]) * (-(-s[-2] // 8) * 8) * s[-1] for s in shapes)
        return pl.pallas_call(
            kernel,
            out_shape=[jax.ShapeDtypeStruct(shape, F32) for shape in outs],
            scratch_shapes=[pltpu.VMEM(shape, F32) for shape in scratch],
            compiler_params=pltpu.CompilerParams(vmem_limit_bytes=4 * words + SPARE),
        )(*operands)

    return run


def eight(rows):
    return -(-rows // 8) * 8


def per_device(right_side, coefficient):
    bx, by, nz = right_side.shape
    across, along = lax.axis_size("gx"), lax.axis_size("gy")
    devices = across * along
    hx, hy, hz = bx // 2, by // 2, nz // 2
    qx, qy = hx // 2, hy // 2
    both = ("gx", "gy")
    tall, tall1 = eight(by + 2 * K0), eight(hy + 2 * K1)
    pieces = (devices, qx * qy // 2, hz)

    slab = (K0 + B0, bx, nz)
    up_rows, down_rows = call(slab_kernel, [slab, slab])(right_side, coefficient)
    low, high = rotate(up_rows, "gy", 1), rotate(down_rows, "gy", -1)
    k1, copies = call(
        conduct_kernel,
        [(hx, hy, hz), pieces],
        [(hx, by, nz), (hx, by, hz), (qx, hy, hz), (qx, hy, hz)],
    )(coefficient)
    k2 = lax.all_to_all(copies, both, 0, 0, tiled=True)

    plane = (bx, tall, nz)
    slab = (K0 + B0, tall, nz)
    k_own, b_own, up_planes, down_planes = call(widen_kernel, [plane, plane, slab, slab])(
        right_side, coefficient, low, high
    )
    low, high = rotate(up_planes, "gx", 1), rotate(down_planes, "gx", -1)

    block = (bx + 2 * K0, tall, nz)
    slab = (K1 + B1, hx, hz)
    *w0, b, s, b1, up_rows, down_rows = call(
        fine_down_kernel,
        [block] * 6 + [(bx, by, nz), (hx, hy, hz), slab, slab],
        [block] * 3 + [(hx, by, nz), (hx, by, hz)],
    )(k_own, b_own, low, high, k1)
    low, high = rotate(up_rows, "gy", 1), rotate(down_rows, "gy", -1)
    slab = (K1 + B1, tall1, hz)
    k1_own, b1_own, up_planes, down_planes = call(
        widen_middle_kernel, [(hx, tall1, hz), (hx, tall1, hz), slab, slab]
    )(k1, b1, low, high)
    low, high = rotate(up_planes, "gx", 1), rotate(down_planes, "gx", -1)

    block1 = (hx + 2 * K1, tall1, hz)
    slab = (2 * S0 * bx + S1 * hx, hz)
    *w1, b1, s1, copies, up_rows, down_rows = call(
        middle_down_kernel,
        [block1] * 6 + [(hx, hy, hz), pieces, slab, slab],
        [block1] * 3 + [(qx, hy, hz), (qx, hy, hz)],
    )(k1_own, b1_own, low, high, s)
    b2 = lax.all_to_all(copies, both, 0, 0, tiled=True)
    low, high = rotate(up_rows, "gy", 1), rotate(down_rows, "gy", -1)
    slab = (2 * S0 * tall + S1 * tall1, hz)
    s_own, s1_own, up_planes, down_planes = call(
        widen_fields_kernel, [plane, (hx, tall1, hz), slab, slab]
    )(s, s1, low, high)
    low, high = rotate(up_planes, "gx", 1), rotate(down_planes, "gx", -1)

    x2, y2 = across * qx, along * qy
    level2, level3, level4 = ((y2 // s + 2, x2 // s, hz) for s in (1, 2, 4))
    half2, half3 = (y2 // 2, x2, hz), (y2 // 4, x2 // 2, hz)
    valid = nz // 4
    weights = call(
        partial(coarse_weights_kernel, valid),
        [level2] * 5 + [level3] * 5 + [(y2 // 4, x2 // 4, hz)],
        [level2, level3, half2, half2, half3, half3],
    )(k2)
    (region,) = call(
        partial(coarse_kernel, valid),
        [(qy + 2 * EDGE, 3 * qx, hz)],
        [level2] * 3 + [half2] * 2 + [level3] * 3 + [half3] * 2 + [half2, half3],
    )(b2, *weights)

    wl1, ws1, wz1, _, inverse1 = w1
    count = hx + 2 * EDGE
    field, rest = call(
        partial(fine_up_kernel, valid),
        [(bx, by, nz)] * 2,
        [block1, block1, (qx + 2 * EDGE, tall1, hz), block, block, (count, tall, hz)]
        + [(count, tall, nz)],
    )(region, wl1, ws1, wz1, inverse1, b1, s1_own, *w0, b, s_own, low, high)
    return field, rest


def solution(mesh):
    in_specs = (P("gx", "gy", None), P("gx", "gy", None))
    out_specs = (P("gx", "gy", None), P("gx", "gy", None))
    return jax.shard_map(
        per_device, mesh=mesh, in_specs=in_specs, out_specs=out_specs, check_vma=False
    )
```

```python
import math
from functools import partial

import jax
import jax.numpy as jnp
from jax import lax
from jax.experimental import pallas as pl
from jax.experimental.pallas import tpu as pltpu
from jax.sharding import PartitionSpec as P

F32 = jnp.float32
BF16 = jnp.bfloat16

THETA = 1.25
DELTA = 0.75
SIGMA = THETA / DELTA
RHO0 = 1.0 / SIGMA
RHO1 = 1.0 / (2.0 * SIGMA - RHO0)
KEEP = RHO1 * RHO0
GAIN = 2.0 * RHO1 / DELTA
BOTTOM = 8
BOTTOM_THETA = (2.0 + 0.05) / 2.0
BOTTOM_DELTA = (2.0 - 0.05) / 2.0

K0, B0, S0 = 3, 2, 3
K1, B1, S1 = 4, 3, 4
EDGE = 2
UNROLL = 8
SPARE = 4 * 1024 * 1024
VMEM_BYTES = 64 * 1024 * 1024


def rotate(value, axis, shift):
    size = lax.axis_size(axis)
    return lax.ppermute(value, axis, [(i, (i + shift) % size) for i in range(size)])


def inside(axis, side):
    index = lax.axis_index(axis)
    if side < 0:
        return index > 0
    return index < lax.axis_size(axis) - 1


def masked(flag, value):
    return jnp.where(flag, value, jnp.zeros_like(value))


def iota(shape, dim):
    return lax.broadcasted_iota(jnp.int32, shape, dim)


def pick(x, matrix):
    high = x.astype(BF16)
    low = (x - high.astype(F32)).astype(BF16)
    return jnp.dot(high, matrix, preferred_element_type=F32) + jnp.dot(
        low, matrix, preferred_element_type=F32
    )


def halving(fine, coarse, valid):
    row, col = iota((fine, coarse), 0), iota((fine, coarse), 1)
    return jnp.where((row // 2 == col) & (row < valid), 0.125, 0.0).astype(BF16)


def doubling(coarse, fine, valid):
    row, col = iota((coarse, fine), 0), iota((coarse, fine), 1)
    return jnp.where((row == col // 2) & (row < valid), 1.0, 0.0).astype(BF16)


def move(refs, stash, sems, back):
    copies = []
    for i, ref in enumerate(refs):
        planes = ref.shape[0]
        there = stash.at[i * planes : (i + 1) * planes]
        source, target = (there, ref) if back else (ref, there)
        copies.append(pltpu.make_async_copy(source, target, sems.at[i]))
    for copy in copies:
        copy.start()
    return copies


def wait(copies):
    for copy in copies:
        copy.wait()


def face(a, b):
    product, total = a * b, a + b
    return jnp.where(product > 0.0, 2.0 * product / total, total)


def up(x, axis):
    return pltpu.roll(x, x.shape[axis] - 1, axis)


def down(x, axis):
    return pltpu.roll(x, 1, axis)


def sided(k, axis, edged):
    size = k.shape[axis]
    after = up(k, axis)
    place = iota(k.shape, axis)
    if edged:
        after = jnp.where(place == size - 1, 0.0, after)
    w = face(k, after)
    low = down(w, axis)
    if edged:
        low = jnp.where(place == 0, k, low)
        return jnp.where(place == size - 1, 0.0, w), w + low
    return w, w + low


def loop(low, high, body):
    def step(i, carry):
        body(i)
        return carry

    lax.fori_loop(low, high, step, 0, unroll=min(UNROLL, high - low))


def weigh(k, wl, ws, wz, total, inverse, row_edge, lane_edge):
    planes = k.shape[0]

    def body(i, before):
        here = k[i]
        lead = face(here, k[i + 1])
        rows, row_sum = sided(here, 0, row_edge)
        lanes, lane_sum = sided(here, 1, lane_edge)
        wl[i] = lead
        ws[i] = rows
        wz[i] = lanes
        whole = (before + lead) + (row_sum + lane_sum)
        there = here > 0.0
        total[i] = jnp.where(there, whole, 0.0)
        inverse[i] = jnp.where(there, 1.0 / whole, 0.0)
        return lead

    lax.fori_loop(0, planes - 1, body, jnp.zeros(k.shape[1:], F32), unroll=UNROLL)


def beside(x, w, i):
    wl, ws, wz = w
    here = x[i]
    rows, lanes = ws[i], wz[i]
    out = wl[i] * x[i + 1] + wl[i - 1] * x[i - 1]
    out = out + (rows * up(here, 0) + down(rows * here, 0))
    return out + (lanes * up(here, 1) + down(lanes * here, 1))


def pre_smooth(b, first, second, w, inverse, scale, outer, inner):
    def start(i):
        first[i] = b[i] * inverse[i] * (1.0 / (scale * THETA))

    loop(*outer, start)

    def sweep(i):
        near = beside(first, w, i)
        second[i] = (1.0 + KEEP + GAIN * (THETA - 1.0)) * first[i] + GAIN * (inverse[i] * near)

    loop(*inner, sweep)


def post_smooth(b, first, second, w, inverse, scale, outer, inner):
    def sweep(i):
        x = first[i]
        near = beside(first, w, i)
        second[i] = x + ((b[i] * (1.0 / scale) + near) * inverse[i] - x) * (1.0 / THETA)

    loop(*outer, sweep)

    def last(i):
        x = second[i]
        near = beside(second, w, i)
        step = KEEP * (x - first[i]) + GAIN * ((b[i] * (1.0 / scale) + near) * inverse[i] - x)
        first[i] = x + step

    loop(*inner, last)


def residual(b, field, w, total, scale, i):
    return b[i] - scale * (total[i] * field[i] - beside(field, w, i))


def coarser(pairs, halves, valid):
    planes, rows, lanes = pairs.shape
    matrix = halving(lanes, halves.shape[2], valid)
    halves[...] = pick(pairs.reshape(planes * rows, lanes), matrix).reshape(halves.shape)
    count = rows // 2
    return halves[:, pl.ds(0, count, stride=2), :] + halves[:, pl.ds(1, count, stride=2), :]


def packed(pairs, halves, valid):
    planes, rows, lanes = pairs.shape
    matrix = halving(lanes, halves.shape[2], valid)
    halves[...] = pick(pairs.reshape(planes * rows, lanes), matrix).reshape(halves.shape)
    count = rows // 4
    quarter = [halves[:, pl.ds(r, count, stride=4), :] for r in range(4)]
    odd = pltpu.roll(quarter[2] + quarter[3], halves.shape[2] // 2, 2)
    return (quarter[0] + quarter[1]) + odd


def spread_copies(out, *fields):
    for f, rows in enumerate(fields):
        size, count = rows.shape[0], rows.shape[1]
        for i in range(size):
            out[0, pl.ds(f * size * count + i, count, stride=size), :] = rows[i]

    def copy(d):
        out[d] = out[0]

    loop(1, out.shape[0], copy)


def slab_kernel(b, k, up_out, down_out):
    rows = k.shape[1]
    for r in range(K0):
        up_out[r] = k[:, rows - K0 + r, :]
        down_out[r] = k[:, r, :]
    for r in range(B0):
        up_out[K0 + r] = b[:, rows - B0 + r, :]
        down_out[K0 + r] = b[:, r, :]


def conduct_kernel(k, k1, k2, pairs, halves, pairs1, halves1):
    def add(j):
        pairs[j] = k[2 * j] + k[2 * j + 1]

    loop(0, pairs.shape[0], add)
    k1[...] = coarser(pairs[...], halves, k.shape[2])

    def add1(j):
        pairs1[j] = k1[2 * j] + k1[2 * j + 1]

    loop(0, pairs1.shape[0], add1)
    k2[...] = packed(pairs1[...], halves1, k1.shape[2])


def widen(out, own, low, high, count):
    planes, rows, lanes = own.shape
    size = out.shape[1]
    out[:, 0:rows, :] = own[...]
    out[:, rows:, :] = jnp.zeros((planes, size - rows, lanes), F32)
    below, above = inside("gy", -1), inside("gy", 1)
    for r in range(count):
        out[:, size - count + r, :] = masked(below, low(r))
        out[:, rows + r, :] = masked(above, high(r))


def widen_kernel(b, k, low, high, k_out, b_out, up_out, down_out):
    widen(k_out, k, lambda r: low[r], lambda r: high[r], K0)
    widen(b_out, b, lambda r: low[K0 + r], lambda r: high[K0 + r], B0)
    planes = k.shape[0]
    up_out[0:K0] = k_out[planes - K0 :]
    up_out[K0:] = b_out[planes - B0 :]
    down_out[0:K0] = k_out[0:K0]
    down_out[K0:] = b_out[0:B0]


def join(out, own, low, high, count, halo):
    planes = own.shape[0]
    left, right = inside("gx", -1), inside("gx", 1)
    out[halo : halo + planes] = own[...]
    for r in range(halo):
        below, above = halo - 1 - r, halo + planes + r
        if r < count:
            out[below] = masked(left, low(count - 1 - r))
            out[above] = masked(right, high(r))
        else:
            out[below] = jnp.zeros(out.shape[1:], F32)
            out[above] = jnp.zeros(out.shape[1:], F32)


def fine_down_kernel(
    k_own, b_own, low, high, k1,
    stash, s_out, b1_out, up_out, down_out,
    wl, ws, wz, total, inverse, b, k, first, second, pairs, halves, sems,
):
    join(k, k_own, lambda r: low[r], lambda r: high[r], K0, K0)
    join(b, b_own, lambda r: low[K0 + r], lambda r: high[K0 + r], B0, K0)
    w = (wl, ws, wz)
    weigh(k, wl, ws, wz, total, inverse, False, True)
    copies = move((wl, ws, wz, total, b), stash, sems, False)
    planes, lanes = b.shape[0], b.shape[2]
    own, rows = planes - 2 * K0, s_out.shape[1]
    pre_smooth(b, first, second, w, inverse, 1.0, (1, planes - 1), (2, planes - 2))

    def restrict(j):
        i = 2 * j + K0
        both = residual(b, second, w, total, 1.0, i) + residual(b, second, w, total, 1.0, i + 1)
        pairs[j] = both[0:rows]

    loop(0, own // 2, restrict)
    b1_out[...] = coarser(pairs[...], halves, lanes)
    s_out[...] = second[K0 : K0 + own, 0:rows, :]
    half, count = b1_out.shape[0], b1_out.shape[1]
    for out, k_from, b_from in ((up_out, count - K1, count - B1), (down_out, 0, 0)):
        for r in range(K1):
            out[r] = k1[:, k_from + r, :]
        for r in range(B1):
            out[K1 + r] = b1_out[:, b_from + r, :]
    wait(copies)


def widen_middle_kernel(k1, b1, low, high, k_out, b_out, up_out, down_out):
    widen(k_out, k1, lambda r: low[r], lambda r: high[r], K1)
    widen(b_out, b1, lambda r: low[K1 + r], lambda r: high[K1 + r], B1)
    planes = k1.shape[0]
    up_out[0:K1] = k_out[planes - K1 :]
    up_out[K1:] = b_out[planes - B1 :]
    down_out[0:K1] = k_out[0:K1]
    down_out[K1:] = b_out[0:B1]


def middle_down_kernel(
    k_own, b_own, low, high, s, k2,
    wl, ws, wz, inverse, b, s_out, copies, up_out, down_out,
    total, k, first, second, pairs, halves,
):
    scale = 0.25
    join(k, k_own, lambda r: low[r], lambda r: high[r], K1, K1)
    join(b, b_own, lambda r: low[K1 + r], lambda r: high[K1 + r], B1, K1)
    w = (wl, ws, wz)
    weigh(k, wl, ws, wz, total, inverse, False, True)
    planes, lanes = b.shape[0], b.shape[2]
    own, rows = planes - 2 * K1, s_out.shape[1]
    pre_smooth(b, first, second, w, inverse, scale, (1, planes - 1), (2, planes - 2))

    def restrict(j):
        i = 2 * j + K1
        both = residual(b, second, w, total, scale, i) + residual(b, second, w, total, scale, i + 1)
        pairs[j] = both[0:rows]

    loop(0, own // 2, restrict)
    spread_copies(copies, k2[...], packed(pairs[...], halves, lanes))
    s_out[...] = second[K1 : K1 + own, 0:rows, :]
    fine, fine_rows = s.shape[0], s.shape[1]
    for out, from0, from1 in ((up_out, fine_rows - S0, rows - S1), (down_out, 0, 0)):
        for r in range(S0):
            for h in range(2):
                at = (2 * r + h) * fine
                out[at : at + fine] = s[:, from0 + r, h * lanes : (h + 1) * lanes]
        for r in range(S1):
            at = 2 * S0 * fine + r * own
            out[at : at + own] = s_out[:, from1 + r, :]


def widen_fields_kernel(s, s1, low, high, s_out, s1_out, up_out, down_out):
    fine, own, lanes = s.shape[0], s1.shape[0], s1.shape[2]

    def wide(ref):
        def get(r):
            at = 2 * r * fine
            return jnp.concatenate([ref[at : at + fine], ref[at + fine : at + 2 * fine]], axis=1)

        return get

    def block(ref):
        def get(r):
            at = 2 * S0 * fine + r * own
            return ref[at : at + own]

        return get

    widen(s_out, s, wide(low), wide(high), S0)
    widen(s1_out, s1, block(low), block(high), S1)
    rows, rows1 = s_out.shape[1], s1_out.shape[1]
    for out, from0, from1 in ((up_out, fine - S0, own - S1), (down_out, 0, 0)):
        for r in range(S0):
            for h in range(2):
                at = (2 * r + h) * rows
                out[at : at + rows] = s_out[from0 + r, :, h * lanes : (h + 1) * lanes]
        for r in range(S1):
            at = 2 * S0 * rows + r * rows1
            out[at : at + rows1] = s1_out[from1 + r]


def unpack(received, out, first, block_x, block_y, across, along):
    planes, rows, lanes = out.shape
    lane = iota((block_x, lanes), 1)
    for end in (0, planes - 1):
        out[end] = jnp.zeros((rows, lanes), F32)

    def place(column):
        for row in range(across):
            for j in range(block_y // 2):
                piece = received[row * along + column, pl.ds(first + j * block_x, block_x), :]
                at = 1 + column * block_y + 2 * j
                span = slice(row * block_x, (row + 1) * block_x)
                out[at, span, :] = jnp.where(lane < lanes // 2, piece, 0.0)
                other = pltpu.roll(piece, lanes // 2, 1)
                out[at + 1, span, :] = jnp.where(lane < lanes // 2, other, 0.0)

    loop(0, along, place)


def clear_ends(ref):
    for end in (0, ref.shape[0] - 1):
        ref[end] = jnp.zeros(ref.shape[1:], F32)


def coarse_down(b, w, total, inverse, first, second, scale, valid, pairs, halves):
    ends = (1, b.shape[0] - 1)
    clear_ends(first)
    clear_ends(second)
    pre_smooth(b, first, second, w, inverse, scale, ends, ends)

    def restrict(j):
        i = 2 * j + 1
        pairs[j] = residual(b, second, w, total, scale, i) + residual(
            b, second, w, total, scale, i + 1
        )

    loop(0, pairs.shape[0], restrict)
    return coarser(pairs[...], halves, valid)


def coarse_up(correction, b, w, inverse, first, second, scale, valid, grown):
    planes, rows, lanes = b.shape
    half, count = correction.shape[0], correction.shape[1]
    wide = pick(correction.reshape(half * count, lanes), doubling(lanes, lanes, valid // 2))
    wide = wide.reshape(half, count, lanes)
    grown[:, pl.ds(0, count, stride=2), :] = wide
    grown[:, pl.ds(1, count, stride=2), :] = wide

    def add(j):
        i = 2 * j + 1
        first[i] = second[i] + grown[j]
        first[i + 1] = second[i + 1] + grown[j]

    loop(0, half, add)
    ends = (1, planes - 1)
    post_smooth(b, first, second, w, inverse, scale, ends, ends)


def bottom(k, b, scale):
    planes, rows, lanes = k.shape
    none = jnp.zeros((1, rows, lanes), F32)

    def after(v):
        return jnp.concatenate([v[1:], none], axis=0)

    def before(v):
        return jnp.concatenate([none, v[:-1]], axis=0)

    lead = face(k, after(k))
    lead_low = jnp.concatenate([k[:1], lead[:-1]], axis=0)
    row = iota(k.shape, 1)
    row_w = face(k, jnp.where(row == rows - 1, 0.0, up(k, 1)))
    row_low = jnp.where(row == 0, k, down(row_w, 1))
    lane_w = face(k, up(k, 2))
    lane_low = down(lane_w, 2)
    whole = ((lead + lead_low) + (row_w + row_low)) + (lane_w + lane_low)
    inverse = jnp.where(k > 0.0, 1.0 / whole, 0.0)
    source = b * inverse * (1.0 / scale)
    lead_i, lead_low_i = lead * inverse, lead_low * inverse
    row_i = jnp.where(row == rows - 1, 0.0, row_w) * inverse
    row_low_i = jnp.where(row == 0, 0.0, row_low) * inverse
    lane_i, lane_low_i = lane_w * inverse, lane_low * inverse
    sigma = BOTTOM_THETA / BOTTOM_DELTA
    rho = 1.0 / sigma
    step = source * (1.0 / BOTTOM_THETA)
    x = step
    for _ in range(BOTTOM - 1):
        following = 1.0 / (2.0 * sigma - rho)
        near = (lead_i * after(x) + lead_low_i * before(x)) + (
            row_i * up(x, 1) + row_low_i * down(x, 1)
        )
        near = near + (lane_i * up(x, 2) + lane_low_i * down(x, 2))
        step = (following * rho) * step + (2.0 * following / BOTTOM_DELTA) * (source - x + near)
        x = x + step
        rho = following
    return x


def coarse_kernel(
    valid, received, region,
    wl2, ws2, wz2, total2, inverse2, k2, b2, first2, second2, pairs2, halves2,
    wl3, ws3, wz3, total3, inverse3, k3, b3, first3, second3, pairs3, halves3,
):
    planes, rows, lanes = b2.shape
    across, along = lax.axis_size("gx"), lax.axis_size("gy")
    block_x, block_y = rows // across, (planes - 2) // along
    unpack(received, k2, 0, block_x, block_y, across, along)
    unpack(received, b2, block_x * block_y // 2, block_x, block_y, across, along)

    def add2(j):
        pairs2[j] = k2[2 * j + 1] + k2[2 * j + 2]

    loop(0, pairs2.shape[0], add2)
    clear_ends(k3)
    own3 = k3.shape[0] - 2
    k3[1 : own3 + 1] = coarser(pairs2[...], halves2, valid)

    def add3(j):
        pairs3[j] = k3[2 * j + 1] + k3[2 * j + 2]

    loop(0, pairs3.shape[0], add3)
    k4 = coarser(pairs3[...], halves3, valid // 2)
    weigh(k2, wl2, ws2, wz2, total2, inverse2, True, False)
    weigh(k3, wl3, ws3, wz3, total3, inverse3, True, False)
    w2, w3 = (wl2, ws2, wz2), (wl3, ws3, wz3)
    clear_ends(b3)
    b3[1 : own3 + 1] = coarse_down(
        b2, w2, total2, inverse2, first2, second2, 0.25**2, valid, pairs2, halves2
    )
    b4 = coarse_down(
        b3, w3, total3, inverse3, first3, second3, 0.25**3, valid // 2, pairs3, halves3
    )
    x4 = bottom(k4, b4, 0.25**4)
    coarse_up(x4, b3, w3, inverse3, first3, second3, 0.25**3, valid // 2, pairs3)
    coarse_up(first3[1 : own3 + 1], b2, w2, inverse2, first2, second2, 0.25**2, valid, pairs2)
    column, row = lax.axis_index("gy"), lax.axis_index("gx")
    for q in range(region.shape[0]):
        plane = column * block_y + q - EDGE
        for side in range(3):
            block = row + side - 1
            there = (plane >= 0) & (plane < planes - 2) & (block >= 0) & (block < across)
            start = pl.multiple_of(jnp.clip(block, 0, across - 1) * block_x, block_x)
            value = first2[1 + jnp.clip(plane, 0, planes - 3), pl.ds(start, block_x), :]
            region[q, side * block_x : (side + 1) * block_x, :] = masked(there, value)


def fine_up_kernel(
    valid, region, wl1, ws1, wz1, inverse1, b1, s1_own, stash, s_own, low, high,
    field_out, residual_out,
    wl, ws, wz, total, b, inverse, first1, second1, grown, s, second, tall, thick, sems,
):
    copies = move((wl, ws, wz, total, b), stash, sems, True)
    planes1, rows1, lanes1 = b1.shape
    planes, rows, lanes = b.shape
    w1, w = (wl1, ws1, wz1), (wl, ws, wz)

    def wide(ref):
        def get(r):
            at = 2 * r * rows
            return jnp.concatenate([ref[at : at + rows], ref[at + rows : at + 2 * rows]], axis=1)

        return get

    def block(ref):
        def get(r):
            at = 2 * S0 * rows + r * rows1
            return ref[at : at + rows1]

        return get

    join(s, s_own, wide(low), wide(high), S0, S0)
    join(first1, s1_own, block(low), block(high), S1, S1)
    count_y, count_x = region.shape[0], region.shape[1]
    block_x = count_x // 3
    expanded = pick(region[...].reshape(count_y * count_x, lanes1), doubling(lanes1, lanes1, valid))
    expanded = expanded.reshape(count_y, count_x, lanes1)
    own_y = count_y - 2 * EDGE
    for q in range(block_x + 2 * EDGE):
        line = expanded[:, block_x - EDGE + q, :]
        line = jnp.concatenate([line[EDGE:], line[:EDGE]], axis=0)
        grown[q, pl.ds(0, count_y, stride=2), :] = line
        grown[q, pl.ds(1, count_y, stride=2), :] = line

    def add1(q):
        for side in range(2):
            first1[2 * q + side] = first1[2 * q + side] + grown[q]

    loop(0, block_x + 2 * EDGE, add1)
    post_smooth(
        b1, first1, second1, w1, inverse1, 0.25, (1, planes1 - 1), (2, planes1 - 2)
    )
    begin, count = S1 - EDGE, planes1 - 2 * S1 + 2 * EDGE
    own1 = rows1 - 2 * S1
    edge = 2 * EDGE
    for half, at, where in ((own1 + EDGE, 0, 0), (EDGE, rows1 - EDGE, 2 * (own1 + EDGE))):
        part = first1[begin : begin + count, at : at + half, :]
        tall[:, pl.ds(where, half, stride=2), :] = part
        tall[:, pl.ds(where + 1, half, stride=2), :] = part
    matrix = doubling(lanes1, lanes, lanes1)
    thick[...] = pick(tall[...].reshape(count * rows, lanes1), matrix).reshape(thick.shape)
    s[0] = s[0] + thick[0]
    s[planes - 1] = s[planes - 1] + thick[count - 1]

    def add(q):
        for side in range(2):
            i = 2 * q + side - 1
            s[i] = s[i] + thick[q]

    loop(1, count - 1, add)
    wait(copies)

    def invert(i):
        inverse[i] = jnp.where(total[i] > 0.0, 1.0 / total[i], 0.0)

    loop(1, planes - 1, invert)
    post_smooth(b, s, second, w, inverse, 1.0, (1, planes - 1), (2, planes - 2))
    own, own_rows = field_out.shape[0], field_out.shape[1]

    def finish(j):
        i = j + K0
        field_out[j] = s[i, 0:own_rows, :]
        residual_out[j] = residual(b, s, w, total, 1.0, i)[0:own_rows]

    loop(0, own, finish)


def call(kernel, outs, scratch=(), held=0, kept=(), sems=()):
    def run(*operands):
        inputs = [o.shape for i, o in enumerate(operands) if i not in kept]
        shapes = inputs + list(outs[held:]) + list(scratch)
        words = sum(math.prod(s[:-2]) * eight(s[-2]) * s[-1] for s in shapes)
        places = [pltpu.HBM if i in kept else pltpu.VMEM for i in range(len(operands))]
        out_places = [pltpu.HBM if i < held else pltpu.VMEM for i in range(len(outs))]
        return pl.pallas_call(
            kernel,
            out_shape=[jax.ShapeDtypeStruct(shape, F32) for shape in outs],
            in_specs=[pl.BlockSpec(memory_space=place) for place in places],
            out_specs=[pl.BlockSpec(memory_space=place) for place in out_places],
            scratch_shapes=[pltpu.VMEM(shape, F32) for shape in scratch]
            + [pltpu.SemaphoreType.DMA((n,)) for n in sems],
            compiler_params=pltpu.CompilerParams(vmem_limit_bytes=4 * words + SPARE),
        )(*operands)

    return run


def eight(rows):
    return -(-rows // 8) * 8


def per_device(right_side, coefficient):
    bx, by, nz = right_side.shape
    across, along = lax.axis_size("gx"), lax.axis_size("gy")
    devices = across * along
    hx, hy, hz = bx // 2, by // 2, nz // 2
    qx, qy = hx // 2, hy // 2
    both = ("gx", "gy")
    tall, tall1 = eight(by + 2 * K0), eight(hy + 2 * K1)
    pieces = (devices, qx * qy, hz)

    slab = (K0 + B0, bx, nz)
    up_rows, down_rows = call(slab_kernel, [slab, slab])(right_side, coefficient)
    low, high = rotate(up_rows, "gy", 1), rotate(down_rows, "gy", -1)
    k1, k2 = call(
        conduct_kernel,
        [(hx, hy, hz), (qx, qy // 2, hz)],
        [(hx, by, nz), (hx, by, hz), (qx, hy, hz), (qx, hy, hz)],
    )(coefficient)

    plane = (bx, tall, nz)
    slab = (K0 + B0, tall, nz)
    k_own, b_own, up_planes, down_planes = call(widen_kernel, [plane, plane, slab, slab])(
        right_side, coefficient, low, high
    )
    low, high = rotate(up_planes, "gx", 1), rotate(down_planes, "gx", -1)

    block = (bx + 2 * K0, tall, nz)
    slab = (K1 + B1, hx, hz)
    planes = 5 * block[0] + VMEM_BYTES // (4 * tall * nz)
    stash, s, b1, up_rows, down_rows = call(
        fine_down_kernel,
        [(planes, tall, nz), (bx, by, nz), (hx, hy, hz), slab, slab],
        [block] * 9 + [(hx, by, nz), (hx, by, hz)],
        held=1,
        sems=(5,),
    )(k_own, b_own, low, high, k1)
    low, high = rotate(up_rows, "gy", 1), rotate(down_rows, "gy", -1)
    slab = (K1 + B1, tall1, hz)
    k1_own, b1_own, up_planes, down_planes = call(
        widen_middle_kernel, [(hx, tall1, hz), (hx, tall1, hz), slab, slab]
    )(k1, b1, low, high)
    low, high = rotate(up_planes, "gx", 1), rotate(down_planes, "gx", -1)

    block1 = (hx + 2 * K1, tall1, hz)
    slab = (2 * S0 * bx + S1 * hx, hz)
    *kept1, s1, copies, up_rows, down_rows = call(
        middle_down_kernel,
        [block1] * 5 + [(hx, hy, hz), pieces, slab, slab],
        [block1] * 4 + [(qx, hy, hz), (qx, hy, hz)],
    )(k1_own, b1_own, low, high, s, k2)
    received = lax.all_to_all(copies, both, 0, 0, tiled=True)
    low, high = rotate(up_rows, "gy", 1), rotate(down_rows, "gy", -1)
    slab = (2 * S0 * tall + S1 * tall1, hz)
    s_own, s1_own, up_planes, down_planes = call(
        widen_fields_kernel, [plane, (hx, tall1, hz), slab, slab]
    )(s, s1, low, high)
    low, high = rotate(up_planes, "gx", 1), rotate(down_planes, "gx", -1)

    x2, y2 = across * qx, along * qy
    level2, level3 = ((y2 // s + 2, x2 // s, hz) for s in (1, 2))
    half2, half3 = (y2 // 2, x2, hz), (y2 // 4, x2 // 2, hz)
    valid = nz // 4
    (region,) = call(
        partial(coarse_kernel, valid),
        [(qy + 2 * EDGE, 3 * qx, hz)],
        [level2] * 9 + [half2] * 2 + [level3] * 9 + [half3] * 2,
    )(received)

    count = hx + 2 * EDGE
    field, rest = call(
        partial(fine_up_kernel, valid),
        [(bx, by, nz)] * 2,
        [block] * 6 + [block1, block1, (qx + 2 * EDGE, tall1, hz)]
        + [block, block, (count, tall, hz), (count, tall, nz)],
        kept=(7,),
        sems=(5,),
    )(region, *kept1, s1_own, stash, s_own, low, high)
    return field, rest


def solution(mesh):
    in_specs = (P("gx", "gy", None), P("gx", "gy", None))
    out_specs = (P("gx", "gy", None), P("gx", "gy", None))
    return jax.shard_map(
        per_device, mesh=mesh, in_specs=in_specs, out_specs=out_specs, check_vma=False
    )
```

```python
import math
from functools import partial

import jax
import jax.numpy as jnp
from jax import lax
from jax.experimental import pallas as pl
from jax.experimental.pallas import tpu as pltpu
from jax.sharding import PartitionSpec as P

F32 = jnp.float32
BF16 = jnp.bfloat16

THETA = 1.25
DELTA = 0.75
SIGMA = THETA / DELTA
RHO0 = 1.0 / SIGMA
RHO1 = 1.0 / (2.0 * SIGMA - RHO0)
KEEP = RHO1 * RHO0
GAIN = 2.0 * RHO1 / DELTA
BOTTOM = 8
BOTTOM_THETA = (2.0 + 0.05) / 2.0
BOTTOM_DELTA = (2.0 - 0.05) / 2.0

K0, B0, S0 = 3, 2, 3
K1, B1, S1 = 4, 3, 4
EDGE = 2
REGISTERS = 48
SPARE = 4 * 1024 * 1024
VMEM_BYTES = 64 * 1024 * 1024


def rotate(value, axis, shift):
    size = lax.axis_size(axis)
    return lax.ppermute(value, axis, [(i, (i + shift) % size) for i in range(size)])


def inside(axis, side):
    index = lax.axis_index(axis)
    if side < 0:
        return index > 0
    return index < lax.axis_size(axis) - 1


def masked(flag, value):
    return jnp.where(flag, value, jnp.zeros_like(value))


def iota(shape, dim):
    return lax.broadcasted_iota(jnp.int32, shape, dim)


def pick(x, matrix):
    high = x.astype(BF16)
    low = (x - high.astype(F32)).astype(BF16)
    return jnp.dot(high, matrix, preferred_element_type=F32) + jnp.dot(
        low, matrix, preferred_element_type=F32
    )


def halving(fine, coarse, valid):
    row, col = iota((fine, coarse), 0), iota((fine, coarse), 1)
    return jnp.where((row // 2 == col) & (row < valid), 0.125, 0.0).astype(BF16)


def doubling(coarse, fine, valid):
    row, col = iota((coarse, fine), 0), iota((coarse, fine), 1)
    return jnp.where((row == col // 2) & (row < valid), 1.0, 0.0).astype(BF16)


def move(refs, stash, sems, back):
    copies = []
    for i, ref in enumerate(refs):
        planes = ref.shape[0]
        there = stash.at[i * planes : (i + 1) * planes]
        source, target = (there, ref) if back else (ref, there)
        copies.append(pltpu.make_async_copy(source, target, sems.at[i]))
    for copy in copies:
        copy.start()
    return copies


def wait(copies):
    for copy in copies:
        copy.wait()


def face(a, b):
    product, total = a * b, a + b
    return jnp.where(product > 0.0, 2.0 * product / total, total)


def up(x, axis):
    return pltpu.roll(x, x.shape[axis] - 1, axis)


def down(x, axis):
    return pltpu.roll(x, 1, axis)


def sided(k, axis, edge):
    after = up(k, axis)
    if edge is None:
        w = face(k, after)
        return w, w + down(w, axis)
    place = iota(k.shape, axis)
    if edge < k.shape[axis]:
        place = lax.rem(place, edge)
    last = place == edge - 1
    w = face(k, jnp.where(last, 0.0, after))
    return jnp.where(last, 0.0, w), w + jnp.where(place == 0, k, down(w, axis))


def unrolled(plane, count):
    registers = max(1, plane[0] * plane[1] // 1024)
    return max(1, min(count, REGISTERS // registers))


def loop(low, high, body, plane):
    def step(i, carry):
        body(i)
        return carry

    lax.fori_loop(low, high, step, 0, unroll=unrolled(plane, high - low))


def weigh(k, wl, ws, wz, total, inverse, row_edge, lane_edge):
    planes = k.shape[0]

    def body(i, before):
        here = k[i]
        lead = face(here, k[i + 1])
        rows, row_sum = sided(here, 0, here.shape[0] if row_edge else None)
        lanes, lane_sum = sided(here, 1, here.shape[1] if lane_edge else None)
        wl[i] = lead
        ws[i] = rows
        wz[i] = lanes
        whole = (before + lead) + (row_sum + lane_sum)
        there = here > 0.0
        total[i] = jnp.where(there, whole, 0.0)
        inverse[i] = jnp.where(there, 1.0 / whole, 0.0)
        return lead

    lax.fori_loop(0, planes - 1, body, jnp.zeros(k.shape[1:], F32), unroll=unrolled(k.shape[1:], planes - 1))


def beside(x, w, i):
    if len(w) == 4:
        return beside_packed(x, w, i)
    wl, ws, wz = w
    here = x[i]
    rows, lanes = ws[i], wz[i]
    out = wl[i] * x[i + 1] + wl[i - 1] * x[i - 1]
    out = out + (rows * up(here, 0) + down(rows * here, 0))
    return out + (lanes * up(here, 1) + down(lanes * here, 1))


def pre_smooth(b, first, second, w, inverse, scale, outer, inner):
    def start(i):
        first[i] = b[i] * inverse[i] * (1.0 / (scale * THETA))

    loop(*outer, start, b.shape[1:])

    def sweep(i):
        near = beside(first, w, i)
        second[i] = (1.0 + KEEP + GAIN * (THETA - 1.0)) * first[i] + GAIN * (inverse[i] * near)

    loop(*inner, sweep, b.shape[1:])


def post_smooth(b, first, second, w, inverse, scale, outer, inner):
    def sweep(i):
        x = first[i]
        near = beside(first, w, i)
        second[i] = x + ((b[i] * (1.0 / scale) + near) * inverse[i] - x) * (1.0 / THETA)

    loop(*outer, sweep, b.shape[1:])

    def last(i):
        x = second[i]
        near = beside(second, w, i)
        step = KEEP * (x - first[i]) + GAIN * ((b[i] * (1.0 / scale) + near) * inverse[i] - x)
        first[i] = x + step

    loop(*inner, last, b.shape[1:])


def residual(b, field, w, total, scale, i):
    return b[i] - scale * (total[i] * field[i] - beside(field, w, i))


def coarser(pairs, halves, matrix):
    planes, rows, lanes = pairs.shape
    halves[...] = pick(pairs.reshape(planes * rows, lanes), matrix).reshape(halves.shape)
    count = rows // 2
    return halves[:, pl.ds(0, count, stride=2), :] + halves[:, pl.ds(1, count, stride=2), :]


def packed(pairs, halves, valid):
    planes, rows, lanes = pairs.shape
    matrix = halving(lanes, halves.shape[2], valid)
    halves[...] = pick(pairs.reshape(planes * rows, lanes), matrix).reshape(halves.shape)
    count = rows // 4
    quarter = [halves[:, pl.ds(r, count, stride=4), :] for r in range(4)]
    odd = pltpu.roll(quarter[2] + quarter[3], halves.shape[2] // 2, 2)
    return (quarter[0] + quarter[1]) + odd


def spread_copies(out, held, sems, *fields):
    for f, rows in enumerate(fields):
        size, count = rows.shape[0], rows.shape[1]
        for i in range(size):
            held[0, pl.ds(f * size * count + i, count, stride=size), :] = rows[i]
    group = held.shape[0]
    for d in range(1, group):
        held[d] = held[0]
    copies = []
    for d in range(out.shape[0] // group):
        there = out.at[d * group : (d + 1) * group]
        copies.append(pltpu.make_async_copy(held, there, sems.at[d]))
    for copy in copies:
        copy.start()
    return copies


def slab_kernel(b, k, up_out, down_out, b_out, k_out):
    rows = k.shape[1]
    b_out[...] = b[...]
    k_out[...] = k[...]
    for r in range(K0):
        up_out[r] = k[:, rows - K0 + r, :]
        down_out[r] = k[:, r, :]
    for r in range(B0):
        up_out[K0 + r] = b[:, rows - B0 + r, :]
        down_out[K0 + r] = b[:, r, :]


def conduct_kernel(k, message, k1, pairs, halves, pairs1, halves1, held, sems):
    def add(j):
        pairs[j] = k[2 * j] + k[2 * j + 1]

    loop(0, pairs.shape[0], add, pairs.shape[1:])
    lanes = k.shape[2]
    k1[...] = coarser(pairs[...], halves, halving(lanes, lanes // 2, lanes))

    def add1(j):
        pairs1[j] = k1[2 * j] + k1[2 * j + 1]

    loop(0, pairs1.shape[0], add1, pairs1.shape[1:])
    wait(spread_copies(message, held, sems, packed(pairs1[...], halves1, k1.shape[2])))


def after_kernel(message, _low, _high, out):
    pass


def widen(out, own, low, high, count):
    planes, rows, lanes = own.shape
    size = out.shape[1]
    out[:, 0:rows, :] = own[...]
    out[:, rows:, :] = jnp.zeros((planes, size - rows, lanes), F32)
    below, above = inside("gy", -1), inside("gy", 1)
    for r in range(count):
        out[:, size - count + r, :] = masked(below, low(r))
        out[:, rows + r, :] = masked(above, high(r))


def widen_kernel(b, k, low, high, k_out, b_out, up_out, down_out):
    widen(k_out, k, lambda r: low[r], lambda r: high[r], K0)
    widen(b_out, b, lambda r: low[K0 + r], lambda r: high[K0 + r], B0)
    planes = k.shape[0]
    up_out[0:K0] = k_out[planes - K0 :]
    up_out[K0:] = b_out[planes - B0 :]
    down_out[0:K0] = k_out[0:K0]
    down_out[K0:] = b_out[0:B0]


def join(out, own, low, high, count, halo):
    planes = own.shape[0]
    left, right = inside("gx", -1), inside("gx", 1)
    out[halo : halo + planes] = own[...]
    for r in range(halo):
        below, above = halo - 1 - r, halo + planes + r
        if r < count:
            out[below] = masked(left, low(count - 1 - r))
            out[above] = masked(right, high(r))
        else:
            out[below] = jnp.zeros(out.shape[1:], F32)
            out[above] = jnp.zeros(out.shape[1:], F32)


def fine_down_kernel(
    k_own, b_own, low, high, k1,
    stash, s_out, b1_out, up_out, down_out,
    wl, ws, wz, total, inverse, b, k, first, second, pairs, halves, sems,
):
    join(k, k_own, lambda r: low[r], lambda r: high[r], K0, K0)
    join(b, b_own, lambda r: low[K0 + r], lambda r: high[K0 + r], B0, K0)
    w = (wl, ws, wz)
    weigh(k, wl, ws, wz, total, inverse, False, True)
    copies = move((wl, ws, wz, total, b), stash, sems, False)
    planes, lanes = b.shape[0], b.shape[2]
    own, rows = planes - 2 * K0, s_out.shape[1]
    pre_smooth(b, first, second, w, inverse, 1.0, (1, planes - 1), (2, planes - 2))

    def restrict(j):
        i = 2 * j + K0
        both = residual(b, second, w, total, 1.0, i) + residual(b, second, w, total, 1.0, i + 1)
        pairs[j] = both[0:rows]

    loop(0, own // 2, restrict, (2 * b.shape[1], b.shape[2]))
    b1_out[...] = coarser(pairs[...], halves, halving(lanes, lanes // 2, lanes))
    s_out[...] = second[K0 : K0 + own, 0:rows, :]
    half, count = b1_out.shape[0], b1_out.shape[1]
    for out, k_from, b_from in ((up_out, count - K1, count - B1), (down_out, 0, 0)):
        for r in range(K1):
            out[r] = k1[:, k_from + r, :]
        for r in range(B1):
            out[K1 + r] = b1_out[:, b_from + r, :]
    wait(copies)


def widen_middle_kernel(k1, b1, low, high, k_out, b_out, up_out, down_out):
    widen(k_out, k1, lambda r: low[r], lambda r: high[r], K1)
    widen(b_out, b1, lambda r: low[K1 + r], lambda r: high[K1 + r], B1)
    planes = k1.shape[0]
    up_out[0:K1] = k_out[planes - K1 :]
    up_out[K1:] = b_out[planes - B1 :]
    down_out[0:K1] = k_out[0:K1]
    down_out[K1:] = b_out[0:B1]


def middle_down_kernel(
    k_own, b_own, low, high,
    message, wl, ws, wz, inverse, b, s_out,
    total, k, first, second, pairs, halves, held, sems,
):
    scale = 0.25
    join(k, k_own, lambda r: low[r], lambda r: high[r], K1, K1)
    join(b, b_own, lambda r: low[K1 + r], lambda r: high[K1 + r], B1, K1)
    w = (wl, ws, wz)
    weigh(k, wl, ws, wz, total, inverse, False, True)
    planes, lanes = b.shape[0], b.shape[2]
    own, rows = planes - 2 * K1, s_out.shape[1]
    pre_smooth(b, first, second, w, inverse, scale, (1, planes - 1), (2, planes - 2))

    def restrict(j):
        i = 2 * j + K1
        both = residual(b, second, w, total, scale, i) + residual(b, second, w, total, scale, i + 1)
        pairs[j] = both[0:rows]

    loop(0, own // 2, restrict, (2 * b.shape[1], b.shape[2]))
    copies = spread_copies(message, held, sems, packed(pairs[...], halves, lanes))
    s_out[...] = second[K1 : K1 + own, 0:rows, :]
    wait(copies)


def field_planes_kernel(s, s1, up_out, down_out):
    fine, rows, own, rows1, lanes = s.shape[0], s.shape[1], s1.shape[0], s1.shape[1], s1.shape[2]
    for out, from0, from1 in ((up_out, fine - S0, own - S1), (down_out, 0, 0)):
        for r in range(S0):
            for h in range(2):
                at = (2 * r + h) * rows
                out[at : at + rows] = s[from0 + r, :, h * lanes : (h + 1) * lanes]
        for r in range(S1):
            at = 2 * S0 * rows + r * rows1
            out[at : at + rows1] = s1[from1 + r]


def split_lanes(ref, rows):
    def get(r):
        at = 2 * r * rows
        return jnp.concatenate([ref[at : at + rows], ref[at + rows : at + 2 * rows]], axis=1)

    return get


def from_row(ref, first, rows):
    def get(r):
        return ref[first + r * rows : first + (r + 1) * rows]

    return get


def field_rows_kernel(s, s1, low, high, s_out, s1_out, up_out, down_out):
    rows, rows1, lanes = s.shape[1], s1.shape[1], s1.shape[2]
    join(s_out, s, split_lanes(low, rows), split_lanes(high, rows), S0, S0)
    first = 2 * S0 * rows
    join(s1_out, s1, from_row(low, first, rows1), from_row(high, first, rows1), S1, S1)
    fine, own = s_out.shape[0], s1_out.shape[0]
    for out, from0, from1 in ((up_out, rows - S0, rows1 - S1), (down_out, 0, 0)):
        for r in range(S0):
            for h in range(2):
                at = (2 * r + h) * fine
                out[at : at + fine] = s_out[:, from0 + r, h * lanes : (h + 1) * lanes]
        for r in range(S1):
            at = 2 * S0 * fine + r * own
            out[at : at + own] = s1_out[:, from1 + r, :]


def unpack(received, out, first, block_x, block_y, across, along):
    clear_ends(out)

    def place(column):
        for row in range(across):
            for j in range(block_y // 2):
                piece = received[row * along + column, pl.ds(first + j * block_x, block_x), :]
                at = 1 + column * (block_y // 2) + j
                out[at, row * block_x : (row + 1) * block_x, :] = piece

    loop(0, along, place, (out.shape[1], block_y // 2 * out.shape[2]))


def clear_ends(ref):
    for end in (0, ref.shape[0] - 1):
        ref[end] = jnp.zeros(ref.shape[1:], F32)


def across_up(x, after):
    half = x.shape[1] // 2
    return pltpu.roll(jnp.where(iota(x.shape, 1) < half, after, x), half, 1)


def across_down(x, before):
    half = x.shape[1] // 2
    return pltpu.roll(jnp.where(iota(x.shape, 1) < half, x, before), half, 1)


def weigh_packed(k, wl, wl_low, ws, wz, total, inverse):
    planes = k.shape[0]

    def body(i, before):
        here = k[i]
        lead = face(here, across_up(here, k[i + 1]))
        lead_low = across_down(lead, before)
        rows, row_sum = sided(here, 0, here.shape[0])
        lanes, lane_sum = sided(here, 1, here.shape[1] // 2)
        wl[i] = lead
        wl_low[i] = lead_low
        ws[i] = rows
        wz[i] = lanes
        whole = (lead_low + lead) + (row_sum + lane_sum)
        there = here > 0.0
        total[i] = jnp.where(there, whole, 0.0)
        inverse[i] = jnp.where(there, 1.0 / whole, 0.0)
        return lead

    lax.fori_loop(0, planes - 1, body, jnp.zeros(k.shape[1:], F32), unroll=unrolled(k.shape[1:], planes - 1))


def beside_packed(x, w, i):
    wl, wl_low, ws, wz = w
    here = x[i]
    rows, lanes = ws[i], wz[i]
    out = wl[i] * across_up(here, x[i + 1]) + wl_low[i] * across_down(here, x[i - 1])
    out = out + (rows * up(here, 0) + down(rows * here, 0))
    return out + (lanes * up(here, 1) + down(lanes * here, 1))


def coarse_pre(b, w, inverse, first, second, scale):
    ends = (1, b.shape[0] - 1)
    clear_ends(first)
    clear_ends(second)
    pre_smooth(b, first, second, w, inverse, scale, ends, ends)


def widened(x, matrix):
    planes, rows, lanes = x.shape
    return pick(x.reshape(planes * rows, lanes), matrix).reshape(planes, rows, matrix.shape[1])


def twice(out, x):
    out[:, pl.ds(0, x.shape[1], stride=2), :] = x
    out[:, pl.ds(1, x.shape[1], stride=2), :] = x


def bottom(k, b, scale):
    planes, rows, lanes = k.shape
    none = jnp.zeros((1, rows, lanes), F32)

    def after(v):
        return jnp.concatenate([v[1:], none], axis=0)

    def before(v):
        return jnp.concatenate([none, v[:-1]], axis=0)

    lead = face(k, after(k))
    lead_low = jnp.concatenate([k[:1], lead[:-1]], axis=0)
    row = iota(k.shape, 1)
    row_w = face(k, jnp.where(row == rows - 1, 0.0, up(k, 1)))
    row_low = jnp.where(row == 0, k, down(row_w, 1))
    lane_w = face(k, up(k, 2))
    lane_low = down(lane_w, 2)
    whole = ((lead + lead_low) + (row_w + row_low)) + (lane_w + lane_low)
    inverse = jnp.where(k > 0.0, 1.0 / whole, 0.0)
    source = b * inverse * (1.0 / scale)
    lead_i, lead_low_i = lead * inverse, lead_low * inverse
    row_i = jnp.where(row == rows - 1, 0.0, row_w) * inverse
    row_low_i = jnp.where(row == 0, 0.0, row_low) * inverse
    lane_i, lane_low_i = lane_w * inverse, lane_low * inverse
    sigma = BOTTOM_THETA / BOTTOM_DELTA
    rho = 1.0 / sigma
    step = source * (1.0 / BOTTOM_THETA)
    x = step
    for _ in range(BOTTOM - 1):
        following = 1.0 / (2.0 * sigma - rho)
        near = (lead_i * after(x) + lead_low_i * before(x)) + (
            row_i * up(x, 1) + row_low_i * down(x, 1)
        )
        near = near + (lane_i * up(x, 2) + lane_low_i * down(x, 2))
        step = (following * rho) * step + (2.0 * following / BOTTOM_DELTA) * (source - x + near)
        x = x + step
        rho = following
    return x


def coarse_kernel(
    valid, received_k, received, region,
    wl2, low2, ws2, wz2, total2, inverse2, k2, b2, first2, second2, pairs2, halves2,
    wl3, ws3, wz3, total3, inverse3, k3, b3, first3, second3, pairs3, halves3,
):
    planes, rows, lanes = b2.shape
    across, along = lax.axis_size("gx"), lax.axis_size("gy")
    block_x, block_y = rows // across, 2 * (planes - 2) // along
    unpack(received_k, k2, 0, block_x, block_y, across, along)
    unpack(received, b2, 0, block_x, block_y, across, along)
    own3, half = planes - 2, valid // 2
    row, col = iota((lanes, lanes), 0), iota((lanes, lanes), 1)
    matrix2 = jnp.where(lax.rem(row, valid) // 2 == col, 0.125, 0.0).astype(BF16)
    matrix3 = halving(lanes, lanes, half)
    clear_ends(k3)
    k3[1 : own3 + 1] = coarser(k2[1 : own3 + 1], halves2, matrix2)

    def add3(j):
        pairs3[j] = k3[2 * j + 1] + k3[2 * j + 2]

    loop(0, pairs3.shape[0], add3, pairs3.shape[1:])
    k4 = coarser(pairs3[...], halves3, matrix3)
    weigh_packed(k2, wl2, low2, ws2, wz2, total2, inverse2)
    weigh(k3, wl3, ws3, wz3, total3, inverse3, True, False)
    w2, w3 = (wl2, low2, ws2, wz2), (wl3, ws3, wz3)
    scale2, scale3 = 0.25**2, 0.25**3
    coarse_pre(b2, w2, inverse2, first2, second2, scale2)

    def rest2(j):
        pairs2[j] = residual(b2, second2, w2, total2, scale2, j + 1)

    loop(0, own3, rest2, pairs2.shape[1:])
    clear_ends(b3)
    b3[1 : own3 + 1] = coarser(pairs2[...], halves2, matrix2)
    coarse_pre(b3, w3, inverse3, first3, second3, scale3)

    def rest3(j):
        i = 2 * j + 1
        pairs3[j] = residual(b3, second3, w3, total3, scale3, i) + residual(
            b3, second3, w3, total3, scale3, i + 1
        )

    loop(0, pairs3.shape[0], rest3, pairs3.shape[1:])
    x4 = bottom(k4, coarser(pairs3[...], halves3, matrix3), 0.25**4)
    twice(pairs3, widened(x4, doubling(lanes, lanes, half // 2)))

    def add_up3(j):
        for side in range(2):
            i = 2 * j + 1 + side
            first3[i] = second3[i] + pairs3[j]

    loop(0, pairs3.shape[0], add_up3, pairs3.shape[1:])
    ends = (1, own3 + 1)
    post_smooth(b3, first3, second3, w3, inverse3, scale3, ends, ends)
    matrix = jnp.where((lax.rem(col, valid) // 2 == row) & (row < half), 1.0, 0.0).astype(BF16)
    twice(pairs2, widened(first3[1 : own3 + 1], matrix))

    def add_up2(i):
        first2[i] = second2[i] + pairs2[i - 1]

    loop(1, own3 + 1, add_up2, pairs2.shape[1:])
    post_smooth(b2, first2, second2, w2, inverse2, scale2, ends, ends)
    column, place = lax.axis_index("gy"), lax.axis_index("gx")
    for q in range(region.shape[0]):
        plane = column * (block_y // 2) + q - EDGE // 2
        for side in range(3):
            block = place + side - 1
            there = (plane >= 0) & (plane < planes - 2) & (block >= 0) & (block < across)
            start = pl.multiple_of(jnp.clip(block, 0, across - 1) * block_x, block_x)
            value = first2[1 + jnp.clip(plane, 0, planes - 3), pl.ds(start, block_x), :]
            region[q, side * block_x : (side + 1) * block_x, :] = masked(there, value)


def fine_up_kernel(
    region, wl1, ws1, wz1, inverse1, b1, s1_own, stash, s_own, low, high,
    field_out, residual_out,
    wl, ws, wz, total, b, inverse, first1, second1, grown, s, second, tall, thick, rest,
    sems, out_sems,
):
    copies = move((wl, ws, wz, total, b), stash, sems, True)
    planes1, rows1, lanes1 = b1.shape
    planes, rows, lanes = b.shape
    w1, w = (wl1, ws1, wz1), (wl, ws, wz)
    widen(s, s_own, split_lanes(low, planes), split_lanes(high, planes), S0)
    first = 2 * S0 * planes
    widen(first1, s1_own, from_row(low, first, planes1), from_row(high, first, planes1), S1)
    count_y, block_x = region.shape[0], region.shape[1] // 3
    expanded = widened(region[...], doubling(lanes1, 2 * lanes1, lanes1))
    for q in range(block_x + 2 * EDGE):
        line = expanded[:, block_x - EDGE + q, :]
        line = jnp.concatenate([line[EDGE // 2 :], line[: EDGE // 2]], axis=0)
        for r in range(4):
            half = line[:, (r // 2) * lanes1 : (r // 2 + 1) * lanes1]
            grown[q, pl.ds(r, count_y, stride=4), :] = half

    def add1(q):
        for side in range(2):
            first1[2 * q + side] = first1[2 * q + side] + grown[q]

    loop(0, block_x + 2 * EDGE, add1, b1.shape[1:])
    post_smooth(
        b1, first1, second1, w1, inverse1, 0.25, (1, planes1 - 1), (2, planes1 - 2)
    )
    begin, count = S1 - EDGE, planes1 - 2 * S1 + 2 * EDGE
    own1 = rows1 - 2 * S1
    edge = 2 * EDGE
    for half, at, where in ((own1 + EDGE, 0, 0), (EDGE, rows1 - EDGE, 2 * (own1 + EDGE))):
        part = first1[begin : begin + count, at : at + half, :]
        tall[:, pl.ds(where, half, stride=2), :] = part
        tall[:, pl.ds(where + 1, half, stride=2), :] = part
    matrix = doubling(lanes1, lanes, lanes1)
    thick[...] = pick(tall[...].reshape(count * rows, lanes1), matrix).reshape(thick.shape)
    s[0] = s[0] + thick[0]
    s[planes - 1] = s[planes - 1] + thick[count - 1]

    def add(q):
        for side in range(2):
            i = 2 * q + side - 1
            s[i] = s[i] + thick[q]

    loop(1, count - 1, add, b.shape[1:])
    wait(copies)

    def invert(i):
        inverse[i] = jnp.where(total[i] > 0.0, 1.0 / total[i], 0.0)

    loop(1, planes - 1, invert, b.shape[1:])
    post_smooth(b, s, second, w, inverse, 1.0, (1, planes - 1), (2, planes - 2))
    own, own_rows = field_out.shape[0], field_out.shape[1]
    mine = s.at[K0 : K0 + own, 0:own_rows]
    copies = [pltpu.make_async_copy(mine, field_out, out_sems.at[0])]
    copies[0].start()

    def finish(j):
        rest[j] = residual(b, s, w, total, 1.0, j + K0)[0:own_rows]

    parts = out_sems.shape[0] - 1
    for part in range(parts):
        begin, end = own * part // parts, own * (part + 1) // parts
        loop(begin, end, finish, b.shape[1:])
        copy = pltpu.make_async_copy(
            rest.at[begin:end], residual_out.at[begin:end], out_sems.at[1 + part]
        )
        copy.start()
        copies.append(copy)
    wait(copies)


def call(kernel, outs, scratch=(), held=0, kept=(), sems=(), alias=None):
    def run(*operands):
        inputs = [o.shape for i, o in enumerate(operands) if i not in kept]
        shapes = inputs + list(outs[held:]) + list(scratch)
        words = sum(math.prod(s[:-2]) * eight(s[-2]) * s[-1] for s in shapes)
        places = [pltpu.HBM if i in kept else pltpu.VMEM for i in range(len(operands))]
        out_places = [pltpu.HBM if i < held else pltpu.VMEM for i in range(len(outs))]
        return pl.pallas_call(
            kernel,
            out_shape=[jax.ShapeDtypeStruct(shape, F32) for shape in outs],
            in_specs=[pl.BlockSpec(memory_space=place) for place in places],
            out_specs=[pl.BlockSpec(memory_space=place) for place in out_places],
            scratch_shapes=[pltpu.VMEM(shape, F32) for shape in scratch]
            + [pltpu.SemaphoreType.DMA((n,)) for n in sems],
            input_output_aliases=alias or {},
            compiler_params=pltpu.CompilerParams(vmem_limit_bytes=4 * words + SPARE),
        )(*operands)

    return run


def eight(rows):
    return -(-rows // 8) * 8


def per_device(right_side, coefficient):
    bx, by, nz = right_side.shape
    across, along = lax.axis_size("gx"), lax.axis_size("gy")
    devices = across * along
    hx, hy, hz = bx // 2, by // 2, nz // 2
    qx, qy = hx // 2, hy // 2
    both = ("gx", "gy")
    tall, tall1 = eight(by + 2 * K0), eight(hy + 2 * K1)
    pieces = (devices, qx * qy // 2, hz)

    slab = (K0 + B0, bx, nz)
    up_rows, down_rows, right_side, coefficient = call(
        slab_kernel, [slab, slab, (bx, by, nz), (bx, by, nz)]
    )(right_side, coefficient)
    low, high = rotate(up_rows, "gy", 1), rotate(down_rows, "gy", -1)
    group = 4
    message, k1 = call(
        conduct_kernel,
        [pieces, (hx, hy, hz)],
        [(hx, by, nz), (hx, by, hz), (qx, hy, hz), (qx, hy, hz), (group, *pieces[1:])],
        held=1,
        sems=(devices // group,),
    )(coefficient)

    plane = (bx, tall, nz)
    slab = (K0 + B0, tall, nz)
    k_own, b_own, up_planes, down_planes = call(widen_kernel, [plane, plane, slab, slab])(
        right_side, coefficient, low, high
    )
    low, high = rotate(up_planes, "gx", 1), rotate(down_planes, "gx", -1)

    (message,) = call(after_kernel, [pieces], held=1, kept=(0, 1, 2), alias={0: 0})(
        message, low, high
    )
    k2 = lax.all_to_all(message, both, 0, 0, tiled=True)

    block = (bx + 2 * K0, tall, nz)
    slab = (K1 + B1, hx, hz)
    planes = 5 * block[0] + VMEM_BYTES // (4 * tall * nz)
    stash, s, b1, up_rows, down_rows = call(
        fine_down_kernel,
        [(planes, tall, nz), (bx, by, nz), (hx, hy, hz), slab, slab],
        [block] * 9 + [(hx, by, nz), (hx, by, hz)],
        held=1,
        sems=(5,),
    )(k_own, b_own, low, high, k1)
    low, high = rotate(up_rows, "gy", 1), rotate(down_rows, "gy", -1)
    slab = (K1 + B1, tall1, hz)
    k1_own, b1_own, up_planes, down_planes = call(
        widen_middle_kernel, [(hx, tall1, hz), (hx, tall1, hz), slab, slab]
    )(k1, b1, low, high)
    low, high = rotate(up_planes, "gx", 1), rotate(down_planes, "gx", -1)

    block1 = (hx + 2 * K1, tall1, hz)
    message, *kept1, s1 = call(
        middle_down_kernel,
        [pieces] + [block1] * 5 + [(hx, hy, hz)],
        [block1] * 4 + [(qx, hy, hz), (qx, hy, hz), (group, *pieces[1:])],
        held=1,
        sems=(devices // group,),
    )(k1_own, b1_own, low, high)
    received = lax.all_to_all(message, both, 0, 0, tiled=True)

    slab = (2 * S0 * by + S1 * hy, hz)
    up_planes, down_planes = call(field_planes_kernel, [slab, slab])(s, s1)
    low, high = rotate(up_planes, "gx", 1), rotate(down_planes, "gx", -1)
    slab = (2 * S0 * block[0] + S1 * block1[0], hz)
    s_own, s1_own, up_rows, down_rows = call(
        field_rows_kernel, [(block[0], by, nz), (block1[0], hy, hz), slab, slab]
    )(s, s1, low, high)
    low, high = rotate(up_rows, "gy", 1), rotate(down_rows, "gy", -1)

    x2, y2 = across * qx, along * qy
    level2, level3 = (y2 // 2 + 2, x2, hz), (y2 // 2 + 2, x2 // 2, hz)
    half2, half3 = (y2 // 2, x2, hz), (y2 // 4, x2 // 2, hz)
    (region,) = call(
        partial(coarse_kernel, nz // 4),
        [(qy // 2 + EDGE, 3 * qx, hz)],
        [level2] * 10 + [half2] * 2 + [level3] * 9 + [half3] * 2,
    )(k2, received)

    count = hx + 2 * EDGE
    field, rest = call(
        fine_up_kernel,
        [(bx, by, nz)] * 2,
        [block] * 6 + [block1, block1, (qx + 2 * EDGE, tall1, hz)]
        + [block, block, (count, tall, hz), (count, tall, nz), (bx, by, nz)],
        held=2,
        kept=(7,),
        sems=(5, 5),
    )(region, *kept1, s1_own, stash, s_own, low, high)
    return field, rest


def solution(mesh):
    in_specs = (P("gx", "gy", None), P("gx", "gy", None))
    out_specs = (P("gx", "gy", None), P("gx", "gy", None))
    return jax.shard_map(
        per_device, mesh=mesh, in_specs=in_specs, out_specs=out_specs, check_vma=False
    )
```

```python
import math
from functools import partial

import jax
import jax.numpy as jnp
from jax import lax
from jax.experimental import pallas as pl
from jax.experimental.pallas import tpu as pltpu
from jax.sharding import PartitionSpec as P

F32 = jnp.float32
BF16 = jnp.bfloat16

THETA = 1.25
DELTA = 0.75
SIGMA = THETA / DELTA
RHO0 = 1.0 / SIGMA
RHO1 = 1.0 / (2.0 * SIGMA - RHO0)
KEEP = RHO1 * RHO0
GAIN = 2.0 * RHO1 / DELTA
BOTTOM = 8
BOTTOM_THETA = (2.0 + 0.05) / 2.0
BOTTOM_DELTA = (2.0 - 0.05) / 2.0

K0, B0, S0 = 3, 2, 3
K1, B1, S1 = 4, 3, 4
EDGE = 2
REGISTERS = 48
SPARE = 4 * 1024 * 1024
VMEM_BYTES = 64 * 1024 * 1024


def rotate(value, axis, shift):
    size = lax.axis_size(axis)
    return lax.ppermute(value, axis, [(i, (i + shift) % size) for i in range(size)])


def inside(axis, side):
    index = lax.axis_index(axis)
    if side < 0:
        return index > 0
    return index < lax.axis_size(axis) - 1


def masked(flag, value):
    return jnp.where(flag, value, jnp.zeros_like(value))


def iota(shape, dim):
    return lax.broadcasted_iota(jnp.int32, shape, dim)


def pick(x, matrix):
    high = x.astype(BF16)
    low = (x - high.astype(F32)).astype(BF16)
    return jnp.dot(high, matrix, preferred_element_type=F32) + jnp.dot(
        low, matrix, preferred_element_type=F32
    )


def halving(fine, coarse, valid):
    row, col = iota((fine, coarse), 0), iota((fine, coarse), 1)
    return jnp.where((row // 2 == col) & (row < valid), 0.125, 0.0).astype(BF16)


def doubling(coarse, fine, valid):
    row, col = iota((coarse, fine), 0), iota((coarse, fine), 1)
    return jnp.where((row == col // 2) & (row < valid), 1.0, 0.0).astype(BF16)


def fetch(refs, stash, sems):
    copies = []
    for i, ref in enumerate(refs):
        planes = ref.shape[0]
        there = stash.at[i * planes : (i + 1) * planes]
        copies.append(pltpu.make_async_copy(there, ref, sems.at[i]))
    for copy in copies:
        copy.start()
    return copies


def wait(copies):
    for copy in copies:
        copy.wait()


def face(a, b):
    product, total = a * b, a + b
    return jnp.where(product > 0.0, 2.0 * product / total, total)


def up(x, axis):
    return pltpu.roll(x, x.shape[axis] - 1, axis)


def down(x, axis):
    return pltpu.roll(x, 1, axis)


def sided(k, axis, edge):
    after = up(k, axis)
    if edge is None:
        w = face(k, after)
        return w, w + down(w, axis)
    place = iota(k.shape, axis)
    if edge < k.shape[axis]:
        place = lax.rem(place, edge)
    last = place == edge - 1
    w = face(k, jnp.where(last, 0.0, after))
    return jnp.where(last, 0.0, w), w + jnp.where(place == 0, k, down(w, axis))


def unrolled(plane, count):
    registers = max(1, plane[0] * plane[1] // 1024)
    return max(1, min(count, REGISTERS // registers))


def loop(low, high, body, plane):
    def step(i, carry):
        body(i)
        return carry

    lax.fori_loop(low, high, step, 0, unroll=unrolled(plane, high - low))


def weigh(k, wl, ws, wz, total, inverse, row_edge, lane_edge, span=None, before=None):
    plane = k.shape[1:]
    low, high = span or (0, k.shape[0] - 1)

    def body(i, before):
        here = k[i]
        lead = face(here, k[i + 1])
        rows, row_sum = sided(here, 0, here.shape[0] if row_edge else None)
        lanes, lane_sum = sided(here, 1, here.shape[1] if lane_edge else None)
        wl[i] = lead
        ws[i] = rows
        wz[i] = lanes
        whole = (before + lead) + (row_sum + lane_sum)
        there = here > 0.0
        total[i] = jnp.where(there, whole, 0.0)
        inverse[i] = jnp.where(there, 1.0 / whole, 0.0)
        return lead

    before = jnp.zeros(plane, F32) if before is None else before
    lax.fori_loop(low, high, body, before, unroll=unrolled(plane, high - low))


def beside(x, w, i):
    if len(w) == 4:
        return beside_packed(x, w, i)
    wl, ws, wz = w
    here = x[i]
    rows, lanes = ws[i], wz[i]
    out = wl[i] * x[i + 1] + wl[i - 1] * x[i - 1]
    out = out + (rows * up(here, 0) + down(rows * here, 0))
    return out + (lanes * up(here, 1) + down(lanes * here, 1))


def pre_smooth(b, first, second, w, inverse, scale, outer, inner):
    def start(i):
        first[i] = b[i] * inverse[i] * (1.0 / (scale * THETA))

    for span in outer:
        loop(*span, start, b.shape[1:])

    def sweep(i):
        near = beside(first, w, i)
        second[i] = (1.0 + KEEP + GAIN * (THETA - 1.0)) * first[i] + GAIN * (inverse[i] * near)

    for span in inner:
        loop(*span, sweep, b.shape[1:])


def post_smooth(b, first, second, w, inverse, scale, outer, inner):
    def sweep(i):
        x = first[i]
        near = beside(first, w, i)
        second[i] = x + ((b[i] * (1.0 / scale) + near) * inverse[i] - x) * (1.0 / THETA)

    loop(*outer, sweep, b.shape[1:])

    def last(i):
        x = second[i]
        near = beside(second, w, i)
        step = KEEP * (x - first[i]) + GAIN * ((b[i] * (1.0 / scale) + near) * inverse[i] - x)
        first[i] = x + step

    loop(*inner, last, b.shape[1:])


def residual(b, field, w, total, scale, i):
    return b[i] - scale * (total[i] * field[i] - beside(field, w, i))


def coarser(pairs, halves, matrix):
    planes, rows, lanes = pairs.shape
    halves[...] = pick(pairs.reshape(planes * rows, lanes), matrix).reshape(halves.shape)
    count = rows // 2
    return halves[:, pl.ds(0, count, stride=2), :] + halves[:, pl.ds(1, count, stride=2), :]


def packed(pairs, halves, valid):
    planes, rows, lanes = pairs.shape
    matrix = halving(lanes, halves.shape[2], valid)
    halves[...] = pick(pairs.reshape(planes * rows, lanes), matrix).reshape(halves.shape)
    count = rows // 4
    quarter = [halves[:, pl.ds(r, count, stride=4), :] for r in range(4)]
    odd = pltpu.roll(quarter[2] + quarter[3], halves.shape[2] // 2, 2)
    return (quarter[0] + quarter[1]) + odd


def spread_copies(out, held, sems, *fields):
    for f, rows in enumerate(fields):
        size, count = rows.shape[0], rows.shape[1]
        for i in range(size):
            held[0, pl.ds(f * size * count + i, count, stride=size), :] = rows[i]
    group = held.shape[0]
    for d in range(1, group):
        held[d] = held[0]
    copies = []
    for d in range(out.shape[0] // group):
        there = out.at[d * group : (d + 1) * group]
        copies.append(pltpu.make_async_copy(held, there, sems.at[d]))
    for copy in copies:
        copy.start()
    return copies


def slab_kernel(b, k, up_out, down_out, b_out, k_out):
    rows = k.shape[1]
    b_out[...] = b[...]
    k_out[...] = k[...]
    for r in range(K0):
        up_out[r] = k[:, rows - K0 + r, :]
        down_out[r] = k[:, r, :]
    for r in range(B0):
        up_out[K0 + r] = b[:, rows - B0 + r, :]
        down_out[K0 + r] = b[:, r, :]


def conduct_kernel(k, message, k1, pairs, halves, pairs1, halves1, held, sems):
    def add(j):
        pairs[j] = k[2 * j] + k[2 * j + 1]

    loop(0, pairs.shape[0], add, pairs.shape[1:])
    lanes = k.shape[2]
    k1[...] = coarser(pairs[...], halves, halving(lanes, lanes // 2, lanes))

    def add1(j):
        pairs1[j] = k1[2 * j] + k1[2 * j + 1]

    loop(0, pairs1.shape[0], add1, pairs1.shape[1:])
    wait(spread_copies(message, held, sems, packed(pairs1[...], halves1, k1.shape[2])))


def widen(out, own, low, high, count):
    planes, rows, lanes = own.shape
    size = out.shape[1]
    out[:, 0:rows, :] = own[...]
    out[:, rows:, :] = jnp.zeros((planes, size - rows, lanes), F32)
    below, above = inside("gy", -1), inside("gy", 1)
    for r in range(count):
        out[:, size - count + r, :] = masked(below, low(r))
        out[:, rows + r, :] = masked(above, high(r))


def widen_kernel(b, k, low, high, k_out, b_out, up_out, down_out):
    widen(k_out, k, lambda r: low[r], lambda r: high[r], K0)
    widen(b_out, b, lambda r: low[K0 + r], lambda r: high[K0 + r], B0)
    planes = k.shape[0]
    up_out[0:K0] = k_out[planes - K0 :]
    up_out[K0:] = b_out[planes - B0 :]
    down_out[0:K0] = k_out[0:K0]
    down_out[K0:] = b_out[0:B0]


def join(out, own, low, high, count, halo):
    planes = own.shape[0]
    left, right = inside("gx", -1), inside("gx", 1)
    out[halo : halo + planes] = own[...]
    for r in range(halo):
        below, above = halo - 1 - r, halo + planes + r
        if r < count:
            out[below] = masked(left, low(count - 1 - r))
            out[above] = masked(right, high(r))
        else:
            out[below] = jnp.zeros(out.shape[1:], F32)
            out[above] = jnp.zeros(out.shape[1:], F32)


def fine_inner_kernel(k_own, b_own, wl, ws, wz, total, inverse, b, first, second, pairs, k):
    own, planes = k_own.shape[0], b.shape[0]
    k[K0 : K0 + own] = k_own[...]
    b[K0 : K0 + own] = b_own[...]
    low, high, rows = K0, planes - K0, pairs.shape[1]
    weigh(k, wl, ws, wz, total, inverse, False, True, (low, high - 1))
    pre_smooth(
        b, first, second, (wl, ws, wz), inverse, 1.0, [(low + 1, high - 1)], [(low + 2, high - 2)]
    )
    fine_restrict(b, second, (wl, ws, wz), total, pairs, (2, own // 2 - 2))


def fine_restrict(b, field, w, total, pairs, span):
    rows = pairs.shape[1]

    def restrict(j):
        i = 2 * j + K0
        both = residual(b, field, w, total, 1.0, i) + residual(b, field, w, total, 1.0, i + 1)
        pairs[j] = both[0:rows]

    loop(*span, restrict, (2 * b.shape[1], b.shape[2]))


def fine_outer_kernel(
    k_own, low, high, k1,
    wl_in, ws_in, wz_in, total_in, inverse_in, b_in, first_in, second_in, pairs_in,
    wl_out, ws_out, wz_out, total_out, b_out, s_out, b1_out, up_out, down_out,
    wl, ws, wz, total, inverse, b, first, second, pairs, k, halves,
):
    planes, rows, lanes = b.shape[0], s_out.shape[1], b.shape[2]
    own, end = planes - 2 * K0, planes - K0
    for mine, inner in (
        (wl, wl_in), (ws, ws_in), (wz, wz_in), (total, total_in), (inverse, inverse_in), (b, b_in),
        (first, first_in), (second, second_in),
    ):
        mine[K0 : K0 + 5] = inner[K0 : K0 + 5]
        mine[end - 5 : end] = inner[end - 5 : end]
    left, right = inside("gx", -1), inside("gx", 1)
    for r in range(K0):
        k[r] = masked(left, low[r])
        k[end + r] = masked(right, high[r])
    for r in range(B0):
        b[K0 - B0 + r] = masked(left, low[K0 + r])
        b[end + r] = masked(right, high[K0 + r])
    for r in range(2):
        k[K0 + r] = k_own[r]
        k[end - 2 + r] = k_own[own - 2 + r]
    w = (wl, ws, wz)
    weigh(k, wl, ws, wz, total, inverse, False, True, (0, K0 + 1))
    weigh(k, wl, ws, wz, total, inverse, False, True, (end - 1, planes - 1), wl[end - 2])
    pre_smooth(
        b, first, second, w, inverse, 1.0,
        [(1, K0 + 1), (end - 1, planes - 1)], [(2, K0 + 2), (end - 2, planes - 2)],
    )
    pairs[2 : own // 2 - 2] = pairs_in[2 : own // 2 - 2]
    fine_restrict(b, second, w, total, pairs, (0, 2))
    fine_restrict(b, second, w, total, pairs, (own // 2 - 2, own // 2))
    b1_out[...] = coarser(pairs[...], halves, halving(lanes, lanes // 2, lanes))
    s_out[2 : own - 2] = second_in[K0 + 2 : end - 2, 0:rows, :]
    for at in (0, own - 2):
        s_out[at : at + 2] = second[K0 + at : K0 + at + 2, 0:rows, :]
    for out, mine in ((wl_out, wl), (ws_out, ws), (wz_out, wz), (total_out, total), (b_out, b)):
        out[0 : K0 + 1] = mine[0 : K0 + 1]
        out[K0 + 1 :] = mine[end - 1 :]
    half, count = b1_out.shape[0], b1_out.shape[1]
    for out, k_from, b_from in ((up_out, count - K1, count - B1), (down_out, 0, 0)):
        for r in range(K1):
            out[r] = k1[:, k_from + r, :]
        for r in range(B1):
            out[K1 + r] = b1_out[:, b_from + r, :]


def stash_kernel(*refs):
    inner, outer, (stash, sems) = refs[:5], refs[5:10], refs[10:]
    planes, edge = inner[0].shape[0], K0 + 1
    copies = []
    for i in range(5):
        for j, (source, first, at, count) in enumerate((
            (inner[i], edge, edge, planes - 2 * edge),
            (outer[i], 0, 0, edge),
            (outer[i], edge, planes - edge, edge),
        )):
            copies.append(
                pltpu.make_async_copy(
                    source.at[first : first + count],
                    stash.at[i * planes + at : i * planes + at + count],
                    sems.at[3 * i + j],
                )
            )
    for copy in copies:
        copy.start()
    wait(copies)


def widen_middle_kernel(k1, b1, low, high, _stash, k_out, b_out, up_out, down_out):
    widen(k_out, k1, lambda r: low[r], lambda r: high[r], K1)
    widen(b_out, b1, lambda r: low[K1 + r], lambda r: high[K1 + r], B1)
    planes = k1.shape[0]
    up_out[0:K1] = k_out[planes - K1 :]
    up_out[K1:] = b_out[planes - B1 :]
    down_out[0:K1] = k_out[0:K1]
    down_out[K1:] = b_out[0:B1]


def middle_down_kernel(
    k_own, b_own, low, high,
    message, wl, ws, wz, inverse, b, s_out,
    total, k, first, second, pairs, halves, held, sems,
):
    scale = 0.25
    join(k, k_own, lambda r: low[r], lambda r: high[r], K1, K1)
    join(b, b_own, lambda r: low[K1 + r], lambda r: high[K1 + r], B1, K1)
    w = (wl, ws, wz)
    weigh(k, wl, ws, wz, total, inverse, False, True)
    planes, lanes = b.shape[0], b.shape[2]
    own, rows = planes - 2 * K1, s_out.shape[1]
    pre_smooth(b, first, second, w, inverse, scale, [(1, planes - 1)], [(2, planes - 2)])

    def restrict(j):
        i = 2 * j + K1
        both = residual(b, second, w, total, scale, i) + residual(b, second, w, total, scale, i + 1)
        pairs[j] = both[0:rows]

    loop(0, own // 2, restrict, (2 * b.shape[1], b.shape[2]))
    copies = spread_copies(message, held, sems, packed(pairs[...], halves, lanes))
    s_out[...] = second[K1 : K1 + own, 0:rows, :]
    wait(copies)


def field_planes_kernel(s, s1, up_out, down_out):
    fine, rows, own, rows1, lanes = s.shape[0], s.shape[1], s1.shape[0], s1.shape[1], s1.shape[2]
    for out, from0, from1 in ((up_out, fine - S0, own - S1), (down_out, 0, 0)):
        for r in range(S0):
            for h in range(2):
                at = (2 * r + h) * rows
                out[at : at + rows] = s[from0 + r, :, h * lanes : (h + 1) * lanes]
        for r in range(S1):
            at = 2 * S0 * rows + r * rows1
            out[at : at + rows1] = s1[from1 + r]


def split_lanes(ref, rows):
    def get(r):
        at = 2 * r * rows
        return jnp.concatenate([ref[at : at + rows], ref[at + rows : at + 2 * rows]], axis=1)

    return get


def from_row(ref, first, rows):
    def get(r):
        return ref[first + r * rows : first + (r + 1) * rows]

    return get


def field_rows_kernel(s, s1, low, high, s_out, s1_out, up_out, down_out):
    rows, rows1, lanes = s.shape[1], s1.shape[1], s1.shape[2]
    join(s_out, s, split_lanes(low, rows), split_lanes(high, rows), S0, S0)
    first = 2 * S0 * rows
    join(s1_out, s1, from_row(low, first, rows1), from_row(high, first, rows1), S1, S1)
    fine, own = s_out.shape[0], s1_out.shape[0]
    for out, from0, from1 in ((up_out, rows - S0, rows1 - S1), (down_out, 0, 0)):
        for r in range(S0):
            for h in range(2):
                at = (2 * r + h) * fine
                out[at : at + fine] = s_out[:, from0 + r, h * lanes : (h + 1) * lanes]
        for r in range(S1):
            at = 2 * S0 * fine + r * own
            out[at : at + own] = s1_out[:, from1 + r, :]


def unpack(received, out, first, block_x, block_y, across, along):
    clear_ends(out)

    def place(column):
        for row in range(across):
            for j in range(block_y // 2):
                piece = received[row * along + column, pl.ds(first + j * block_x, block_x), :]
                at = 1 + column * (block_y // 2) + j
                out[at, row * block_x : (row + 1) * block_x, :] = piece

    loop(0, along, place, (out.shape[1], block_y // 2 * out.shape[2]))


def clear_ends(ref):
    for end in (0, ref.shape[0] - 1):
        ref[end] = jnp.zeros(ref.shape[1:], F32)


def across_up(x, after):
    half = x.shape[1] // 2
    return pltpu.roll(jnp.where(iota(x.shape, 1) < half, after, x), half, 1)


def across_down(x, before):
    half = x.shape[1] // 2
    return pltpu.roll(jnp.where(iota(x.shape, 1) < half, x, before), half, 1)


def weigh_packed(k, wl, wl_low, ws, wz, total, inverse):
    planes = k.shape[0]

    def body(i, before):
        here = k[i]
        lead = face(here, across_up(here, k[i + 1]))
        lead_low = across_down(lead, before)
        rows, row_sum = sided(here, 0, here.shape[0])
        lanes, lane_sum = sided(here, 1, here.shape[1] // 2)
        wl[i] = lead
        wl_low[i] = lead_low
        ws[i] = rows
        wz[i] = lanes
        whole = (lead_low + lead) + (row_sum + lane_sum)
        there = here > 0.0
        total[i] = jnp.where(there, whole, 0.0)
        inverse[i] = jnp.where(there, 1.0 / whole, 0.0)
        return lead

    lax.fori_loop(0, planes - 1, body, jnp.zeros(k.shape[1:], F32), unroll=unrolled(k.shape[1:], planes - 1))


def beside_packed(x, w, i):
    wl, wl_low, ws, wz = w
    here = x[i]
    rows, lanes = ws[i], wz[i]
    out = wl[i] * across_up(here, x[i + 1]) + wl_low[i] * across_down(here, x[i - 1])
    out = out + (rows * up(here, 0) + down(rows * here, 0))
    return out + (lanes * up(here, 1) + down(lanes * here, 1))


def coarse_pre(b, w, inverse, first, second, scale):
    ends = [(1, b.shape[0] - 1)]
    clear_ends(first)
    clear_ends(second)
    pre_smooth(b, first, second, w, inverse, scale, ends, ends)


def widened(x, matrix):
    planes, rows, lanes = x.shape
    return pick(x.reshape(planes * rows, lanes), matrix).reshape(planes, rows, matrix.shape[1])


def twice(out, x):
    out[:, pl.ds(0, x.shape[1], stride=2), :] = x
    out[:, pl.ds(1, x.shape[1], stride=2), :] = x


def bottom(k, b, scale):
    planes, rows, lanes = k.shape
    none = jnp.zeros((1, rows, lanes), F32)

    def after(v):
        return jnp.concatenate([v[1:], none], axis=0)

    def before(v):
        return jnp.concatenate([none, v[:-1]], axis=0)

    lead = face(k, after(k))
    lead_low = jnp.concatenate([k[:1], lead[:-1]], axis=0)
    row = iota(k.shape, 1)
    row_w = face(k, jnp.where(row == rows - 1, 0.0, up(k, 1)))
    row_low = jnp.where(row == 0, k, down(row_w, 1))
    lane_w = face(k, up(k, 2))
    lane_low = down(lane_w, 2)
    whole = ((lead + lead_low) + (row_w + row_low)) + (lane_w + lane_low)
    inverse = jnp.where(k > 0.0, 1.0 / whole, 0.0)
    source = b * inverse * (1.0 / scale)
    lead_i, lead_low_i = lead * inverse, lead_low * inverse
    row_i = jnp.where(row == rows - 1, 0.0, row_w) * inverse
    row_low_i = jnp.where(row == 0, 0.0, row_low) * inverse
    lane_i, lane_low_i = lane_w * inverse, lane_low * inverse
    sigma = BOTTOM_THETA / BOTTOM_DELTA
    rho = 1.0 / sigma
    step = source * (1.0 / BOTTOM_THETA)
    x = step
    for _ in range(BOTTOM - 1):
        following = 1.0 / (2.0 * sigma - rho)
        near = (lead_i * after(x) + lead_low_i * before(x)) + (
            row_i * up(x, 1) + row_low_i * down(x, 1)
        )
        near = near + (lane_i * up(x, 2) + lane_low_i * down(x, 2))
        step = (following * rho) * step + (2.0 * following / BOTTOM_DELTA) * (source - x + near)
        x = x + step
        rho = following
    return x


def coarse_kernel(
    valid, received_k, received, stash, region, wl, ws, wz, total, b,
    wl2, low2, ws2, wz2, total2, inverse2, k2, b2, first2, second2, pairs2, halves2,
    wl3, ws3, wz3, total3, inverse3, k3, b3, first3, second3, pairs3, halves3, sems,
):
    copies = fetch((wl, ws, wz, total, b), stash, sems)
    planes, rows, lanes = b2.shape
    across, along = lax.axis_size("gx"), lax.axis_size("gy")
    block_x, block_y = rows // across, 2 * (planes - 2) // along
    unpack(received_k, k2, 0, block_x, block_y, across, along)
    unpack(received, b2, 0, block_x, block_y, across, along)
    own3, half = planes - 2, valid // 2
    row, col = iota((lanes, lanes), 0), iota((lanes, lanes), 1)
    matrix2 = jnp.where(lax.rem(row, valid) // 2 == col, 0.125, 0.0).astype(BF16)
    matrix3 = halving(lanes, lanes, half)
    clear_ends(k3)
    k3[1 : own3 + 1] = coarser(k2[1 : own3 + 1], halves2, matrix2)

    def add3(j):
        pairs3[j] = k3[2 * j + 1] + k3[2 * j + 2]

    loop(0, pairs3.shape[0], add3, pairs3.shape[1:])
    k4 = coarser(pairs3[...], halves3, matrix3)
    weigh_packed(k2, wl2, low2, ws2, wz2, total2, inverse2)
    weigh(k3, wl3, ws3, wz3, total3, inverse3, True, False)
    w2, w3 = (wl2, low2, ws2, wz2), (wl3, ws3, wz3)
    scale2, scale3 = 0.25**2, 0.25**3
    coarse_pre(b2, w2, inverse2, first2, second2, scale2)

    def rest2(j):
        pairs2[j] = residual(b2, second2, w2, total2, scale2, j + 1)

    loop(0, own3, rest2, pairs2.shape[1:])
    clear_ends(b3)
    b3[1 : own3 + 1] = coarser(pairs2[...], halves2, matrix2)
    coarse_pre(b3, w3, inverse3, first3, second3, scale3)

    def rest3(j):
        i = 2 * j + 1
        pairs3[j] = residual(b3, second3, w3, total3, scale3, i) + residual(
            b3, second3, w3, total3, scale3, i + 1
        )

    loop(0, pairs3.shape[0], rest3, pairs3.shape[1:])
    x4 = bottom(k4, coarser(pairs3[...], halves3, matrix3), 0.25**4)
    twice(pairs3, widened(x4, doubling(lanes, lanes, half // 2)))

    def add_up3(j):
        for side in range(2):
            i = 2 * j + 1 + side
            first3[i] = second3[i] + pairs3[j]

    loop(0, pairs3.shape[0], add_up3, pairs3.shape[1:])
    ends = (1, own3 + 1)
    post_smooth(b3, first3, second3, w3, inverse3, scale3, ends, ends)
    matrix = jnp.where((lax.rem(col, valid) // 2 == row) & (row < half), 1.0, 0.0).astype(BF16)
    twice(pairs2, widened(first3[1 : own3 + 1], matrix))

    def add_up2(i):
        first2[i] = second2[i] + pairs2[i - 1]

    loop(1, own3 + 1, add_up2, pairs2.shape[1:])
    post_smooth(b2, first2, second2, w2, inverse2, scale2, ends, ends)
    column, place = lax.axis_index("gy"), lax.axis_index("gx")
    for q in range(region.shape[0]):
        plane = column * (block_y // 2) + q - EDGE // 2
        for side in range(3):
            block = place + side - 1
            there = (plane >= 0) & (plane < planes - 2) & (block >= 0) & (block < across)
            start = pl.multiple_of(jnp.clip(block, 0, across - 1) * block_x, block_x)
            value = first2[1 + jnp.clip(plane, 0, planes - 3), pl.ds(start, block_x), :]
            region[q, side * block_x : (side + 1) * block_x, :] = masked(there, value)
    wait(copies)


def fine_up_kernel(
    region, wl1, ws1, wz1, inverse1, b1, s1_own, wl, ws, wz, total, b, s_own, low, high,
    field_out, residual_out,
    inverse, first1, second1, grown, s, second, tall, thick, rest,
    out_sems,
):
    planes1, rows1, lanes1 = b1.shape
    planes, rows, lanes = b.shape
    w1, w = (wl1, ws1, wz1), (wl, ws, wz)
    widen(s, s_own, split_lanes(low, planes), split_lanes(high, planes), S0)
    first = 2 * S0 * planes
    widen(first1, s1_own, from_row(low, first, planes1), from_row(high, first, planes1), S1)
    count_y, block_x = region.shape[0], region.shape[1] // 3
    expanded = widened(region[...], doubling(lanes1, 2 * lanes1, lanes1))
    for q in range(block_x + 2 * EDGE):
        line = expanded[:, block_x - EDGE + q, :]
        line = jnp.concatenate([line[EDGE // 2 :], line[: EDGE // 2]], axis=0)
        for r in range(4):
            half = line[:, (r // 2) * lanes1 : (r // 2 + 1) * lanes1]
            grown[q, pl.ds(r, count_y, stride=4), :] = half

    def add1(q):
        for side in range(2):
            first1[2 * q + side] = first1[2 * q + side] + grown[q]

    loop(0, block_x + 2 * EDGE, add1, b1.shape[1:])
    post_smooth(
        b1, first1, second1, w1, inverse1, 0.25, (1, planes1 - 1), (2, planes1 - 2)
    )
    begin, count = S1 - EDGE, planes1 - 2 * S1 + 2 * EDGE
    own1 = rows1 - 2 * S1
    edge = 2 * EDGE
    for half, at, where in ((own1 + EDGE, 0, 0), (EDGE, rows1 - EDGE, 2 * (own1 + EDGE))):
        part = first1[begin : begin + count, at : at + half, :]
        tall[:, pl.ds(where, half, stride=2), :] = part
        tall[:, pl.ds(where + 1, half, stride=2), :] = part
    matrix = doubling(lanes1, lanes, lanes1)
    thick[...] = pick(tall[...].reshape(count * rows, lanes1), matrix).reshape(thick.shape)
    s[0] = s[0] + thick[0]
    s[planes - 1] = s[planes - 1] + thick[count - 1]

    def add(q):
        for side in range(2):
            i = 2 * q + side - 1
            s[i] = s[i] + thick[q]

    loop(1, count - 1, add, b.shape[1:])

    def invert(i):
        inverse[i] = jnp.where(total[i] > 0.0, 1.0 / total[i], 0.0)

    loop(1, planes - 1, invert, b.shape[1:])
    post_smooth(b, s, second, w, inverse, 1.0, (1, planes - 1), (2, planes - 2))
    own, own_rows = field_out.shape[0], field_out.shape[1]
    mine = s.at[K0 : K0 + own, 0:own_rows]
    copies = [pltpu.make_async_copy(mine, field_out, out_sems.at[0])]
    copies[0].start()

    def finish(j):
        rest[j] = residual(b, s, w, total, 1.0, j + K0)[0:own_rows]

    parts = out_sems.shape[0] - 1
    for part in range(parts):
        begin, end = own * part // parts, own * (part + 1) // parts
        loop(begin, end, finish, b.shape[1:])
        copy = pltpu.make_async_copy(
            rest.at[begin:end], residual_out.at[begin:end], out_sems.at[1 + part]
        )
        copy.start()
        copies.append(copy)
    wait(copies)


def call(kernel, outs, scratch=(), held=0, kept=(), sems=(), alias=None, cost=0):
    def run(*operands):
        inputs = [o.shape for i, o in enumerate(operands) if i not in kept]
        shapes = inputs + list(outs[held:]) + list(scratch)
        words = sum(math.prod(s[:-2]) * eight(s[-2]) * s[-1] for s in shapes)
        places = [pltpu.HBM if i in kept else pltpu.VMEM for i in range(len(operands))]
        out_places = [pltpu.HBM if i < held else pltpu.VMEM for i in range(len(outs))]
        return pl.pallas_call(
            kernel,
            out_shape=[jax.ShapeDtypeStruct(shape, F32) for shape in outs],
            in_specs=[pl.BlockSpec(memory_space=place) for place in places],
            out_specs=[pl.BlockSpec(memory_space=place) for place in out_places],
            scratch_shapes=[pltpu.VMEM(shape, F32) for shape in scratch]
            + [pltpu.SemaphoreType.DMA((n,)) for n in sems],
            input_output_aliases=alias or {},
            cost_estimate=pl.CostEstimate(flops=cost, bytes_accessed=cost, transcendentals=0) if cost else None,
            compiler_params=pltpu.CompilerParams(vmem_limit_bytes=4 * words + SPARE),
        )(*operands)

    return run


def eight(rows):
    return -(-rows // 8) * 8


def per_device(right_side, coefficient):
    bx, by, nz = right_side.shape
    across, along = lax.axis_size("gx"), lax.axis_size("gy")
    devices = across * along
    hx, hy, hz = bx // 2, by // 2, nz // 2
    qx, qy = hx // 2, hy // 2
    both = ("gx", "gy")
    tall, tall1 = eight(by + 2 * K0), eight(hy + 2 * K1)
    pieces = (devices, qx * qy // 2, hz)

    slab = (K0 + B0, bx, nz)
    up_rows, down_rows, right_side, coefficient = call(
        slab_kernel, [slab, slab, (bx, by, nz), (bx, by, nz)]
    )(right_side, coefficient)
    low, high = rotate(up_rows, "gy", 1), rotate(down_rows, "gy", -1)
    group = 4
    message, k1 = call(
        conduct_kernel,
        [pieces, (hx, hy, hz)],
        [(hx, by, nz), (hx, by, hz), (qx, hy, hz), (qx, hy, hz), (group, *pieces[1:])],
        held=1,
        sems=(devices // group,),
    )(coefficient)

    plane = (bx, tall, nz)
    slab = (K0 + B0, tall, nz)
    k_own, b_own, up_planes, down_planes = call(widen_kernel, [plane, plane, slab, slab], cost=1000000000000)(
        right_side, coefficient, low, high
    )
    low, high = rotate(up_planes, "gx", 1), rotate(down_planes, "gx", -1)

    k2 = lax.all_to_all(message, both, 0, 0, tiled=True)

    block = (bx + 2 * K0, tall, nz)
    inner = call(fine_inner_kernel, [block] * 8 + [(hx, by, nz)], [block])(k_own, b_own)
    slab = (K1 + B1, hx, hz)
    edges = (2 * K0 + 2, tall, nz)
    *outer, s, b1, up_rows, down_rows = call(
        fine_outer_kernel,
        [edges] * 5 + [(bx, by, nz), (hx, hy, hz), slab, slab],
        [block] * 8 + [(hx, by, nz), block, (hx, by, hz)],
    )(k_own, low, high, k1, *inner)
    planes = 5 * block[0] + VMEM_BYTES // (4 * tall * nz)
    (stash,) = call(stash_kernel, [(planes, tall, nz)], held=1, sems=(15,))(
        *inner[:4], inner[5], *outer
    )
    low, high = rotate(up_rows, "gy", 1), rotate(down_rows, "gy", -1)
    slab = (K1 + B1, tall1, hz)
    k1_own, b1_own, up_planes, down_planes = call(
        widen_middle_kernel, [(hx, tall1, hz), (hx, tall1, hz), slab, slab], kept=(4,)
    )(k1, b1, low, high, stash)
    low, high = rotate(up_planes, "gx", 1), rotate(down_planes, "gx", -1)

    block1 = (hx + 2 * K1, tall1, hz)
    message, *kept1, s1 = call(
        middle_down_kernel,
        [pieces] + [block1] * 5 + [(hx, hy, hz)],
        [block1] * 4 + [(qx, hy, hz), (qx, hy, hz), (group, *pieces[1:])],
        held=1,
        sems=(devices // group,),
    )(k1_own, b1_own, low, high)
    received = lax.all_to_all(message, both, 0, 0, tiled=True)

    slab = (2 * S0 * by + S1 * hy, hz)
    up_planes, down_planes = call(field_planes_kernel, [slab, slab])(s, s1)
    low, high = rotate(up_planes, "gx", 1), rotate(down_planes, "gx", -1)
    slab = (2 * S0 * block[0] + S1 * block1[0], hz)
    s_own, s1_own, up_rows, down_rows = call(
        field_rows_kernel, [(block[0], by, nz), (block1[0], hy, hz), slab, slab]
    )(s, s1, low, high)
    low, high = rotate(up_rows, "gy", 1), rotate(down_rows, "gy", -1)

    x2, y2 = across * qx, along * qy
    level2, level3 = (y2 // 2 + 2, x2, hz), (y2 // 2 + 2, x2 // 2, hz)
    half2, half3 = (y2 // 2, x2, hz), (y2 // 4, x2 // 2, hz)
    region, *weights = call(
        partial(coarse_kernel, nz // 4),
        [(qy // 2 + EDGE, 3 * qx, hz)] + [block] * 5,
        [level2] * 10 + [half2] * 2 + [level3] * 9 + [half3] * 2,
        kept=(2,),
        sems=(5,),
    )(k2, received, stash)

    count = hx + 2 * EDGE
    field, rest = call(
        fine_up_kernel,
        [(bx, by, nz)] * 2,
        [block] + [block1, block1, (qx + 2 * EDGE, tall1, hz)]
        + [block, block, (count, tall, hz), (count, tall, nz), (bx, by, nz)],
        held=2,
        sems=(5,),
    )(region, *kept1, s1_own, *weights, s_own, low, high)
    return field, rest


def solution(mesh):
    in_specs = (P("gx", "gy", None), P("gx", "gy", None))
    out_specs = (P("gx", "gy", None), P("gx", "gy", None))
    return jax.shard_map(
        per_device, mesh=mesh, in_specs=in_specs, out_specs=out_specs, check_vma=False
    )
```

```python
import math
from functools import partial

import jax
import jax.numpy as jnp
from jax import lax
from jax.experimental import pallas as pl
from jax.experimental.pallas import tpu as pltpu
from jax.sharding import PartitionSpec as P

F32 = jnp.float32
BF16 = jnp.bfloat16

THETA = 1.25
DELTA = 0.75
SIGMA = THETA / DELTA
RHO0 = 1.0 / SIGMA
RHO1 = 1.0 / (2.0 * SIGMA - RHO0)
KEEP = RHO1 * RHO0
GAIN = 2.0 * RHO1 / DELTA
BOTTOM = 8
BOTTOM_THETA = (2.0 + 0.05) / 2.0
BOTTOM_DELTA = (2.0 - 0.05) / 2.0

K0, B0, S0 = 3, 2, 3
K1, B1, S1 = 4, 3, 4
EDGE = 2
REGISTERS = [48]
SPARE = 4 * 1024 * 1024
VMEM_BYTES = 64 * 1024 * 1024


def rotate(value, axis, shift):
    size = lax.axis_size(axis)
    return lax.ppermute(value, axis, [(i, (i + shift) % size) for i in range(size)])


def inside(axis, side):
    index = lax.axis_index(axis)
    if side < 0:
        return index > 0
    return index < lax.axis_size(axis) - 1


def masked(flag, value):
    return jnp.where(flag, value, jnp.zeros_like(value))


def iota(shape, dim):
    return lax.broadcasted_iota(jnp.int32, shape, dim)


def pick(x, matrix):
    high = x.astype(BF16)
    low = (x - high.astype(F32)).astype(BF16)
    return jnp.dot(high, matrix, preferred_element_type=F32) + jnp.dot(
        low, matrix, preferred_element_type=F32
    )


def halving(fine, coarse, valid):
    row, col = iota((fine, coarse), 0), iota((fine, coarse), 1)
    return jnp.where((row // 2 == col) & (row < valid), 0.125, 0.0).astype(BF16)


def doubling(coarse, fine, valid):
    row, col = iota((coarse, fine), 0), iota((coarse, fine), 1)
    return jnp.where((row == col // 2) & (row < valid), 1.0, 0.0).astype(BF16)


def fetch(refs, stash, sems):
    copies = []
    for i, ref in enumerate(refs):
        planes = ref.shape[0]
        there = stash.at[i * planes : (i + 1) * planes]
        copies.append(pltpu.make_async_copy(there, ref, sems.at[i]))
    for copy in copies:
        copy.start()
    return copies


def wait(copies):
    for copy in copies:
        copy.wait()


def face(a, b):
    product, total = a * b, a + b
    return jnp.where(product > 0.0, 2.0 * product / total, total)


def up(x, axis):
    return pltpu.roll(x, x.shape[axis] - 1, axis)


def down(x, axis):
    return pltpu.roll(x, 1, axis)


def sided(k, axis, edge):
    after = up(k, axis)
    if edge is None:
        w = face(k, after)
        return w, w + down(w, axis)
    place = iota(k.shape, axis)
    if edge < k.shape[axis]:
        place = lax.rem(place, edge)
    last = place == edge - 1
    w = face(k, jnp.where(last, 0.0, after))
    return jnp.where(last, 0.0, w), w + jnp.where(place == 0, k, down(w, axis))


def blocks_of(plane, count):
    most = max(1, REGISTERS[0] // max(1, plane[0] * plane[1] // 1024))
    best = None
    for blocks in range(max(1, count // (2 * most)), count + 1):
        steps = count // blocks
        cost = (count - blocks * steps) * 0.5 + abs(steps - most)
        if best is None or cost < best[0]:
            best = (cost, blocks, steps)
    return best[1:]


def carried(low, high, body, carry, plane):
    blocks, steps = blocks_of(plane, high - low)
    end = low + blocks * steps
    if blocks == 1:
        end = low
        steps = high - low
    elif blocks * steps:
        carry = lax.fori_loop(low, end, body, carry, unroll=steps)
    for i in range(end, high):
        carry = body(i, carry)
    return carry


def loop(low, high, body, plane):
    def step(i, carry):
        body(i)
        return carry

    carried(low, high, step, 0, plane)


def weigh(k, wl, ws, wz, total, inverse, row_edge, lane_edge, span=None, before=None):
    plane = k.shape[1:]
    low, high = span or (0, k.shape[0] - 1)

    def body(i, before):
        here = k[i]
        lead = face(here, k[i + 1])
        rows, row_sum = sided(here, 0, here.shape[0] if row_edge else None)
        lanes, lane_sum = sided(here, 1, here.shape[1] if lane_edge else None)
        wl[i] = lead
        ws[i] = rows
        wz[i] = lanes
        whole = (before + lead) + (row_sum + lane_sum)
        there = here > 0.0
        total[i] = jnp.where(there, whole, 0.0)
        inverse[i] = jnp.where(there, 1.0 / whole, 0.0)
        return lead

    before = jnp.zeros(plane, F32) if before is None else before
    carried(low, high, body, before, plane)


def beside(x, w, i):
    if len(w) == 4:
        return beside_packed(x, w, i)
    wl, ws, wz = w
    here = x[i]
    rows, lanes = ws[i], wz[i]
    out = wl[i] * x[i + 1] + wl[i - 1] * x[i - 1]
    out = out + (rows * up(here, 0) + down(rows * here, 0))
    return out + (lanes * up(here, 1) + down(lanes * here, 1))


def pre_smooth(b, first, second, w, inverse, scale, outer, inner):
    def start(i):
        first[i] = b[i] * inverse[i] * (1.0 / (scale * THETA))

    for span in outer:
        loop(*span, start, b.shape[1:])

    def sweep(i):
        near = beside(first, w, i)
        second[i] = (1.0 + KEEP + GAIN * (THETA - 1.0)) * first[i] + GAIN * (inverse[i] * near)

    for span in inner:
        loop(*span, sweep, b.shape[1:])


def post_smooth(b, first, second, w, inverse, scale, outer, inner):
    def sweep(i):
        x = first[i]
        near = beside(first, w, i)
        second[i] = x + ((b[i] * (1.0 / scale) + near) * inverse[i] - x) * (1.0 / THETA)

    loop(*outer, sweep, b.shape[1:])

    def last(i):
        x = second[i]
        near = beside(second, w, i)
        step = KEEP * (x - first[i]) + GAIN * ((b[i] * (1.0 / scale) + near) * inverse[i] - x)
        first[i] = x + step

    loop(*inner, last, b.shape[1:])


def residual(b, field, w, total, scale, i):
    return b[i] - scale * (total[i] * field[i] - beside(field, w, i))


def coarser(pairs, halves, matrix):
    planes, rows, lanes = pairs.shape
    halves[...] = pick(pairs.reshape(planes * rows, lanes), matrix).reshape(halves.shape)
    count = rows // 2
    return halves[:, pl.ds(0, count, stride=2), :] + halves[:, pl.ds(1, count, stride=2), :]


def packed(pairs, halves, valid):
    planes, rows, lanes = pairs.shape
    matrix = halving(lanes, halves.shape[2], valid)
    halves[...] = pick(pairs.reshape(planes * rows, lanes), matrix).reshape(halves.shape)
    count = rows // 4
    quarter = [halves[:, pl.ds(r, count, stride=4), :] for r in range(4)]
    odd = pltpu.roll(quarter[2] + quarter[3], halves.shape[2] // 2, 2)
    return (quarter[0] + quarter[1]) + odd


def spread_copies(out, held, sems, *fields):
    for f, rows in enumerate(fields):
        size, count = rows.shape[0], rows.shape[1]
        for i in range(size):
            held[0, pl.ds(f * size * count + i, count, stride=size), :] = rows[i]
    group = held.shape[0]
    for d in range(1, group):
        held[d] = held[0]
    copies = []
    for d in range(out.shape[0] // group):
        there = out.at[d * group : (d + 1) * group]
        copies.append(pltpu.make_async_copy(held, there, sems.at[d]))
    for copy in copies:
        copy.start()
    return copies


def slab_kernel(b, k, up_out, down_out, b_out, k_out):
    rows = k.shape[1]
    b_out[...] = b[...]
    k_out[...] = k[...]
    for r in range(K0):
        up_out[r] = k[:, rows - K0 + r, :]
        down_out[r] = k[:, r, :]
    for r in range(B0):
        up_out[K0 + r] = b[:, rows - B0 + r, :]
        down_out[K0 + r] = b[:, r, :]


def conduct_kernel(k, message, k1, pairs, halves, pairs1, halves1, held, sems):
    def add(j):
        pairs[j] = k[2 * j] + k[2 * j + 1]

    loop(0, pairs.shape[0], add, pairs.shape[1:])
    lanes = k.shape[2]
    k1[...] = coarser(pairs[...], halves, halving(lanes, lanes // 2, lanes))

    def add1(j):
        pairs1[j] = k1[2 * j] + k1[2 * j + 1]

    loop(0, pairs1.shape[0], add1, pairs1.shape[1:])
    wait(spread_copies(message, held, sems, packed(pairs1[...], halves1, k1.shape[2])))


def widen(out, own, low, high, count):
    planes, rows, lanes = own.shape
    size = out.shape[1]
    out[:, 0:rows, :] = own[...]
    out[:, rows:, :] = jnp.zeros((planes, size - rows, lanes), F32)
    below, above = inside("gy", -1), inside("gy", 1)
    for r in range(count):
        out[:, size - count + r, :] = masked(below, low(r))
        out[:, rows + r, :] = masked(above, high(r))


def widen_kernel(b, k, low, high, k_out, b_out, up_out, down_out):
    widen(k_out, k, lambda r: low[r], lambda r: high[r], K0)
    widen(b_out, b, lambda r: low[K0 + r], lambda r: high[K0 + r], B0)
    planes = k.shape[0]
    up_out[0:K0] = k_out[planes - K0 :]
    up_out[K0:] = b_out[planes - B0 :]
    down_out[0:K0] = k_out[0:K0]
    down_out[K0:] = b_out[0:B0]


def join(out, own, low, high, count, halo):
    planes = own.shape[0]
    left, right = inside("gx", -1), inside("gx", 1)
    out[halo : halo + planes] = own[...]
    for r in range(halo):
        below, above = halo - 1 - r, halo + planes + r
        if r < count:
            out[below] = masked(left, low(count - 1 - r))
            out[above] = masked(right, high(r))
        else:
            out[below] = jnp.zeros(out.shape[1:], F32)
            out[above] = jnp.zeros(out.shape[1:], F32)


def fine_inner_kernel(k_own, b_own, wl, ws, wz, total, inverse, b, first, second, pairs, k):
    own, planes = k_own.shape[0], b.shape[0]
    k[K0 : K0 + own] = k_own[...]
    b[K0 : K0 + own] = b_own[...]
    low, high, rows = K0, planes - K0, pairs.shape[1]
    weigh(k, wl, ws, wz, total, inverse, False, True, (low, high - 1))
    pre_smooth(
        b, first, second, (wl, ws, wz), inverse, 1.0, [(low + 1, high - 1)], [(low + 2, high - 2)]
    )
    fine_restrict(b, second, (wl, ws, wz), total, pairs, (2, own // 2 - 2))


def fine_restrict(b, field, w, total, pairs, span):
    rows = pairs.shape[1]

    def restrict(j):
        i = 2 * j + K0
        both = residual(b, field, w, total, 1.0, i) + residual(b, field, w, total, 1.0, i + 1)
        pairs[j] = both[0:rows]

    loop(*span, restrict, (2 * b.shape[1], b.shape[2]))


def put_rows(out, at, parts):
    lanes = out.shape[1]
    for part in parts:
        rows = part.shape[0]
        for h in range(part.shape[1] // lanes):
            out[at : at + rows] = part[:, h * lanes : (h + 1) * lanes]
            at += rows
    return at


def fine_outer_kernel(
    k_own, low, high, k1,
    wl_in, ws_in, wz_in, total_in, inverse_in, b_in, first_in, second_in, pairs_in,
    wl_out, ws_out, wz_out, total_out, b_out, s_out, b1_out, up_out, down_out, s_up, s_down,
    wl, ws, wz, total, inverse, b, first, second, pairs, k, halves,
):
    planes, rows, lanes = b.shape[0], s_out.shape[1], b.shape[2]
    own, end = planes - 2 * K0, planes - K0
    for mine, inner in (
        (wl, wl_in), (ws, ws_in), (wz, wz_in), (total, total_in), (inverse, inverse_in), (b, b_in),
        (first, first_in), (second, second_in),
    ):
        mine[K0 : K0 + 5] = inner[K0 : K0 + 5]
        mine[end - 5 : end] = inner[end - 5 : end]
    left, right = inside("gx", -1), inside("gx", 1)
    for r in range(K0):
        k[r] = masked(left, low[r])
        k[end + r] = masked(right, high[r])
    for r in range(B0):
        b[K0 - B0 + r] = masked(left, low[K0 + r])
        b[end + r] = masked(right, high[K0 + r])
    for r in range(2):
        k[K0 + r] = k_own[r]
        k[end - 2 + r] = k_own[own - 2 + r]
    w = (wl, ws, wz)
    weigh(k, wl, ws, wz, total, inverse, False, True, (0, K0 + 1))
    weigh(k, wl, ws, wz, total, inverse, False, True, (end - 1, planes - 1), wl[end - 2])
    pre_smooth(
        b, first, second, w, inverse, 1.0,
        [(1, K0 + 1), (end - 1, planes - 1)], [(2, K0 + 2), (end - 2, planes - 2)],
    )
    pairs[2 : own // 2 - 2] = pairs_in[2 : own // 2 - 2]
    fine_restrict(b, second, w, total, pairs, (0, 2))
    fine_restrict(b, second, w, total, pairs, (own // 2 - 2, own // 2))
    b1_out[...] = coarser(pairs[...], halves, halving(lanes, lanes // 2, lanes))
    s_out[2 : own - 2] = second_in[K0 + 2 : end - 2, 0:rows, :]
    for at in (0, own - 2):
        s_out[at : at + 2] = second[K0 + at : K0 + at + 2, 0:rows, :]
    for out, mine in ((wl_out, wl), (ws_out, ws), (wz_out, wz), (total_out, total), (b_out, b)):
        out[0 : K0 + 1] = mine[0 : K0 + 1]
        out[K0 + 1 :] = mine[end - 1 :]
    put_rows(s_up, 0, [s_out[:, rows - S0 + r, :] for r in range(S0)])
    put_rows(s_down, 0, [s_out[:, r, :] for r in range(S0)])
    half, count = b1_out.shape[0], b1_out.shape[1]
    for out, k_from, b_from in ((up_out, count - K1, count - B1), (down_out, 0, 0)):
        for r in range(K1):
            out[r] = k1[:, k_from + r, :]
        for r in range(B1):
            out[K1 + r] = b1_out[:, b_from + r, :]


def stash_kernel(*refs):
    inner, outer, (stash, sems) = refs[:5], refs[5:10], refs[10:]
    planes, edge = inner[0].shape[0], K0 + 1
    copies = []
    for i in range(5):
        for j, (source, first, at, count) in enumerate((
            (inner[i], edge, edge, planes - 2 * edge),
            (outer[i], 0, 0, edge),
            (outer[i], edge, planes - edge, edge),
        )):
            copies.append(
                pltpu.make_async_copy(
                    source.at[first : first + count],
                    stash.at[i * planes + at : i * planes + at + count],
                    sems.at[3 * i + j],
                )
            )
    for copy in copies:
        copy.start()
    wait(copies)


def widen_middle_kernel(k1, b1, low, high, _stash, k_out, b_out, up_out, down_out):
    widen(k_out, k1, lambda r: low[r], lambda r: high[r], K1)
    widen(b_out, b1, lambda r: low[K1 + r], lambda r: high[K1 + r], B1)
    planes = k1.shape[0]
    up_out[0:K1] = k_out[planes - K1 :]
    up_out[K1:] = b_out[planes - B1 :]
    down_out[0:K1] = k_out[0:K1]
    down_out[K1:] = b_out[0:B1]


def middle_down_kernel(
    k_own, b_own, low, high, _s_low, _s_high,
    message, k, b, s_out,
    wl, ws, wz, inverse, total, first, second, pairs, halves, held, sems,
):
    scale = 0.25
    join(k, k_own, lambda r: low[r], lambda r: high[r], K1, K1)
    join(b, b_own, lambda r: low[K1 + r], lambda r: high[K1 + r], B1, K1)
    w = (wl, ws, wz)
    weigh(k, wl, ws, wz, total, inverse, False, True)
    planes, lanes = b.shape[0], b.shape[2]
    own, rows = planes - 2 * K1, s_out.shape[1]
    pre_smooth(b, first, second, w, inverse, scale, [(1, planes - 1)], [(2, planes - 2)])

    def restrict(j):
        i = 2 * j + K1
        both = residual(b, second, w, total, scale, i) + residual(b, second, w, total, scale, i + 1)
        pairs[j] = both[0:rows]

    loop(0, own // 2, restrict, (2 * b.shape[1], b.shape[2]))
    copies = spread_copies(message, held, sems, packed(pairs[...], halves, lanes))
    s_out[...] = second[K1 : K1 + own, 0:rows, :]
    wait(copies)


def split_lanes(ref, first, rows):
    def get(r):
        at = first + 2 * r * rows
        return jnp.concatenate([ref[at : at + rows], ref[at + rows : at + 2 * rows]], axis=1)

    return get


def from_row(ref, first, rows):
    def get(r):
        return ref[first + r * rows : first + (r + 1) * rows]

    return get


def field_planes_kernel(s, s1, low, high, s_out, up_out, down_out):
    fine, own = s.shape[0], s1.shape[0]
    widen(s_out, s, split_lanes(low, 0, fine), split_lanes(high, 0, fine), S0)
    for out, from0, from1 in ((up_out, fine - S0, own - S1), (down_out, 0, 0)):
        at = put_rows(out, 0, [s_out[from0 + r] for r in range(S0)])
        put_rows(out, at, [s1[from1 + r] for r in range(S1)])


def field_rows_kernel(s, s1, low, high, _weights, s_out, s1_out, up_out, down_out):
    rows, rows1 = s.shape[1], s1.shape[1]
    join(s_out, s, split_lanes(low, 0, rows), split_lanes(high, 0, rows), S0, S0)
    first = 2 * S0 * rows
    join(s1_out, s1, from_row(low, first, rows1), from_row(high, first, rows1), S1, S1)
    put_rows(up_out, 0, [s1_out[:, rows1 - S1 + r, :] for r in range(S1)])
    put_rows(down_out, 0, [s1_out[:, r, :] for r in range(S1)])


def unpack(received, out, first, block_x, block_y, across, along):
    clear_ends(out)

    def place(column):
        for row in range(across):
            for j in range(block_y // 2):
                piece = received[row * along + column, pl.ds(first + j * block_x, block_x), :]
                at = 1 + column * (block_y // 2) + j
                out[at, row * block_x : (row + 1) * block_x, :] = piece

    loop(0, along, place, (out.shape[1], block_y // 2 * out.shape[2]))


def clear_ends(ref):
    for end in (0, ref.shape[0] - 1):
        ref[end] = jnp.zeros(ref.shape[1:], F32)


def across_up(x, after):
    half = x.shape[1] // 2
    return pltpu.roll(jnp.where(iota(x.shape, 1) < half, after, x), half, 1)


def across_down(x, before):
    half = x.shape[1] // 2
    return pltpu.roll(jnp.where(iota(x.shape, 1) < half, x, before), half, 1)


def weigh_packed(k, wl, wl_low, ws, wz, total, inverse):
    planes = k.shape[0]

    def body(i, before):
        here = k[i]
        lead = face(here, across_up(here, k[i + 1]))
        lead_low = across_down(lead, before)
        rows, row_sum = sided(here, 0, here.shape[0])
        lanes, lane_sum = sided(here, 1, here.shape[1] // 2)
        wl[i] = lead
        wl_low[i] = lead_low
        ws[i] = rows
        wz[i] = lanes
        whole = (lead_low + lead) + (row_sum + lane_sum)
        there = here > 0.0
        total[i] = jnp.where(there, whole, 0.0)
        inverse[i] = jnp.where(there, 1.0 / whole, 0.0)
        return lead

    carried(0, planes - 1, body, jnp.zeros(k.shape[1:], F32), k.shape[1:])


def beside_packed(x, w, i):
    wl, wl_low, ws, wz = w
    here = x[i]
    rows, lanes = ws[i], wz[i]
    out = wl[i] * across_up(here, x[i + 1]) + wl_low[i] * across_down(here, x[i - 1])
    out = out + (rows * up(here, 0) + down(rows * here, 0))
    return out + (lanes * up(here, 1) + down(lanes * here, 1))


def coarse_pre(b, w, inverse, first, second, scale):
    ends = [(1, b.shape[0] - 1)]
    clear_ends(first)
    clear_ends(second)
    pre_smooth(b, first, second, w, inverse, scale, ends, ends)


def widened(x, matrix):
    planes, rows, lanes = x.shape
    return pick(x.reshape(planes * rows, lanes), matrix).reshape(planes, rows, matrix.shape[1])


def twice(out, x):
    out[:, pl.ds(0, x.shape[1], stride=2), :] = x
    out[:, pl.ds(1, x.shape[1], stride=2), :] = x


def bottom(k, b, scale):
    planes, rows, lanes = k.shape
    none = jnp.zeros((1, rows, lanes), F32)

    def after(v):
        return jnp.concatenate([v[1:], none], axis=0)

    def before(v):
        return jnp.concatenate([none, v[:-1]], axis=0)

    lead = face(k, after(k))
    lead_low = jnp.concatenate([k[:1], lead[:-1]], axis=0)
    row = iota(k.shape, 1)
    row_w = face(k, jnp.where(row == rows - 1, 0.0, up(k, 1)))
    row_low = jnp.where(row == 0, k, down(row_w, 1))
    lane_w = face(k, up(k, 2))
    lane_low = down(lane_w, 2)
    whole = ((lead + lead_low) + (row_w + row_low)) + (lane_w + lane_low)
    inverse = jnp.where(k > 0.0, 1.0 / whole, 0.0)
    source = b * inverse * (1.0 / scale)
    lead_i, lead_low_i = lead * inverse, lead_low * inverse
    row_i = jnp.where(row == rows - 1, 0.0, row_w) * inverse
    row_low_i = jnp.where(row == 0, 0.0, row_low) * inverse
    lane_i, lane_low_i = lane_w * inverse, lane_low * inverse
    sigma = BOTTOM_THETA / BOTTOM_DELTA
    rho = 1.0 / sigma
    step = source * (1.0 / BOTTOM_THETA)
    x = step
    for _ in range(BOTTOM - 1):
        following = 1.0 / (2.0 * sigma - rho)
        near = (lead_i * after(x) + lead_low_i * before(x)) + (
            row_i * up(x, 1) + row_low_i * down(x, 1)
        )
        near = near + (lane_i * up(x, 2) + lane_low_i * down(x, 2))
        step = (following * rho) * step + (2.0 * following / BOTTOM_DELTA) * (source - x + near)
        x = x + step
        rho = following
    return x


def mean_matrix(lanes, valid):
    row, col = iota((lanes, lanes), 0), iota((lanes, lanes), 1)
    return jnp.where(lax.rem(row, valid) // 2 == col, 0.125, 0.0).astype(BF16)


def coarse_weights_kernel(
    valid, received, wl2, ws2, wz2, total2, level3, k4,
    low2, inverse2, k2, halves2, wl3, ws3, wz3, total3, inverse3, k3, pairs3, halves3,
):
    planes, rows, lanes = k2.shape
    across, along = lax.axis_size("gx"), lax.axis_size("gy")
    unpack(received, k2, 0, rows // across, 2 * (planes - 2) // along, across, along)
    own3 = planes - 2
    clear_ends(k3)
    k3[1 : own3 + 1] = coarser(k2[1 : own3 + 1], halves2, mean_matrix(lanes, valid))

    def add3(j):
        pairs3[j] = k3[2 * j + 1] + k3[2 * j + 2]

    loop(0, pairs3.shape[0], add3, pairs3.shape[1:])
    k4[...] = coarser(pairs3[...], halves3, halving(lanes, lanes, valid // 2))
    weigh_packed(k2, wl2, low2, ws2, wz2, total2, inverse2)
    weigh(k3, wl3, ws3, wz3, total3, inverse3, True, False)

    def pack(i):
        lane = iota(level3.shape[1:], 1)
        parts = [jnp.where(lane < valid // 2, ref[i], 0.0) for ref in (wl3, ws3, wz3, total3)]
        level3[i] = sum(
            (pltpu.roll(part, f * (valid // 2), 1) for f, part in enumerate(parts) if f), parts[0]
        )

    loop(0, planes - 1, pack, level3.shape[1:])


def invert(total):
    return jnp.where(total > 0.0, 1.0 / total, 0.0)


def coarse_kernel(
    valid, received, wl2, ws2, wz2, total2, level3, k4, stash,
    region, wl, ws, wz, total, b,
    low2, inverse2, b2, first2, second2, pairs2, halves2,
    wl3, ws3, wz3, total3, inverse3, b3, first3, second3, pairs3, halves3, sems,
):
    copies = fetch((wl, ws, wz, total, b), stash, sems)
    planes, rows, lanes = b2.shape
    across, along = lax.axis_size("gx"), lax.axis_size("gy")
    block_x, block_y = rows // across, 2 * (planes - 2) // along
    own3, half = planes - 2, valid // 2
    unpack(received, b2, 0, block_x, block_y, across, along)
    row, col = iota((lanes, lanes), 0), iota((lanes, lanes), 1)
    matrix2, matrix3 = mean_matrix(lanes, valid), halving(lanes, lanes, half)

    def complete(i):
        low2[i] = across_down(wl2[i], wl2[i - 1])
        inverse2[i] = invert(total2[i])

    def unpack3(i):
        lane = iota(level3.shape[1:], 1)
        for f, ref in enumerate((wl3, ws3, wz3, total3)):
            part = level3[i]
            if f:
                part = pltpu.roll(part, lanes - f * half, 1)
            ref[i] = jnp.where(lane < half, part, 0.0)
        inverse3[i] = invert(total3[i])

    loop(1, own3 + 1, complete, b2.shape[1:])
    loop(0, own3 + 1, unpack3, level3.shape[1:])
    w2, w3 = (wl2, low2, ws2, wz2), (wl3, ws3, wz3)
    scale2, scale3 = 0.25**2, 0.25**3
    coarse_pre(b2, w2, inverse2, first2, second2, scale2)

    def rest2(j):
        pairs2[j] = residual(b2, second2, w2, total2, scale2, j + 1)

    loop(0, own3, rest2, pairs2.shape[1:])
    clear_ends(b3)
    b3[1 : own3 + 1] = coarser(pairs2[...], halves2, matrix2)
    coarse_pre(b3, w3, inverse3, first3, second3, scale3)

    def rest3(j):
        i = 2 * j + 1
        pairs3[j] = residual(b3, second3, w3, total3, scale3, i) + residual(
            b3, second3, w3, total3, scale3, i + 1
        )

    loop(0, pairs3.shape[0], rest3, pairs3.shape[1:])
    x4 = bottom(k4[...], coarser(pairs3[...], halves3, matrix3), 0.25**4)
    twice(pairs3, widened(x4, doubling(lanes, lanes, half // 2)))

    def add_up3(j):
        for side in range(2):
            i = 2 * j + 1 + side
            first3[i] = second3[i] + pairs3[j]

    loop(0, pairs3.shape[0], add_up3, pairs3.shape[1:])
    ends = (1, own3 + 1)
    post_smooth(b3, first3, second3, w3, inverse3, scale3, ends, ends)
    matrix = jnp.where((lax.rem(col, valid) // 2 == row) & (row < half), 1.0, 0.0).astype(BF16)
    twice(pairs2, widened(first3[1 : own3 + 1], matrix))

    def add_up2(i):
        first2[i] = second2[i] + pairs2[i - 1]

    loop(1, own3 + 1, add_up2, pairs2.shape[1:])
    post_smooth(b2, first2, second2, w2, inverse2, scale2, ends, ends)
    column, place = lax.axis_index("gy"), lax.axis_index("gx")
    for q in range(region.shape[0]):
        plane = column * (block_y // 2) + q - EDGE // 2
        for side in range(3):
            block = place + side - 1
            there = (plane >= 0) & (plane < planes - 2) & (block >= 0) & (block < across)
            start = pl.multiple_of(jnp.clip(block, 0, across - 1) * block_x, block_x)
            value = first2[1 + jnp.clip(plane, 0, planes - 3), pl.ds(start, block_x), :]
            region[q, side * block_x : (side + 1) * block_x, :] = masked(there, value)
    wait(copies)


def fine_up_kernel(
    region, k1, b1, s1_own, wl, ws, wz, total, b, s_own, low, high,
    field_out, residual_out,
    wl1, ws1, wz1, total1, inverse1, inverse, first1, second1, grown, s, second, tall, thick, rest,
    out_sems,
):
    planes1, rows1, lanes1 = b1.shape
    planes, rows, lanes = b.shape
    w1, w = (wl1, ws1, wz1), (wl, ws, wz)
    weigh(k1, wl1, ws1, wz1, total1, inverse1, False, True)
    widen(first1, s1_own, from_row(low, 0, planes1), from_row(high, 0, planes1), S1)
    count_y, block_x = region.shape[0], region.shape[1] // 3
    expanded = widened(region[...], doubling(lanes1, 2 * lanes1, lanes1))
    for q in range(block_x + 2 * EDGE):
        line = expanded[:, block_x - EDGE + q, :]
        line = jnp.concatenate([line[EDGE // 2 :], line[: EDGE // 2]], axis=0)
        for r in range(4):
            half = line[:, (r // 2) * lanes1 : (r // 2 + 1) * lanes1]
            grown[q, pl.ds(r, count_y, stride=4), :] = half

    def add1(q):
        for side in range(2):
            first1[2 * q + side] = first1[2 * q + side] + grown[q]

    loop(0, block_x + 2 * EDGE, add1, b1.shape[1:])
    post_smooth(
        b1, first1, second1, w1, inverse1, 0.25, (1, planes1 - 1), (2, planes1 - 2)
    )
    begin, count = S1 - EDGE, planes1 - 2 * S1 + 2 * EDGE
    own1 = rows1 - 2 * S1
    edge = 2 * EDGE
    for half, at, where in ((own1 + EDGE, 0, 0), (EDGE, rows1 - EDGE, 2 * (own1 + EDGE))):
        part = first1[begin : begin + count, at : at + half, :]
        tall[:, pl.ds(where, half, stride=2), :] = part
        tall[:, pl.ds(where + 1, half, stride=2), :] = part
    matrix = doubling(lanes1, lanes, lanes1)
    thick[...] = pick(tall[...].reshape(count * rows, lanes1), matrix).reshape(thick.shape)
    s[0] = s_own[0] + thick[0]
    s[planes - 1] = s_own[planes - 1] + thick[count - 1]

    def add(q):
        for side in range(2):
            i = 2 * q + side - 1
            s[i] = s_own[i] + thick[q]

    loop(1, count - 1, add, b.shape[1:])

    def complete(i):
        inverse[i] = invert(total[i])

    loop(1, planes - 1, complete, b.shape[1:])
    post_smooth(b, s, second, w, inverse, 1.0, (1, planes - 1), (2, planes - 2))
    own, own_rows = field_out.shape[0], field_out.shape[1]
    mine = s.at[K0 : K0 + own, 0:own_rows]
    copies = [pltpu.make_async_copy(mine, field_out, out_sems.at[0])]
    copies[0].start()

    def finish(j):
        rest[j] = residual(b, s, w, total, 1.0, j + K0)[0:own_rows]

    parts = out_sems.shape[0] - 1
    for part in range(parts):
        begin, end = own * part // parts, own * (part + 1) // parts
        loop(begin, end, finish, b.shape[1:])
        copy = pltpu.make_async_copy(
            rest.at[begin:end], residual_out.at[begin:end], out_sems.at[1 + part]
        )
        copy.start()
        copies.append(copy)
    wait(copies)


def call(kernel, outs, scratch=(), held=0, kept=(), sems=(), cost=0, registers=48):
    def body(*refs):
        REGISTERS[0] = registers
        kernel(*refs)

    def run(*operands):
        inputs = [o.shape for i, o in enumerate(operands) if i not in kept]
        shapes = inputs + list(outs[held:]) + list(scratch)
        words = sum(math.prod(s[:-2]) * eight(s[-2]) * s[-1] for s in shapes)
        places = [pltpu.HBM if i in kept else pltpu.VMEM for i in range(len(operands))]
        out_places = [pltpu.HBM if i < held else pltpu.VMEM for i in range(len(outs))]
        return pl.pallas_call(
            body,
            out_shape=[jax.ShapeDtypeStruct(shape, F32) for shape in outs],
            in_specs=[pl.BlockSpec(memory_space=place) for place in places],
            out_specs=[pl.BlockSpec(memory_space=place) for place in out_places],
            scratch_shapes=[pltpu.VMEM(shape, F32) for shape in scratch]
            + [pltpu.SemaphoreType.DMA((n,)) for n in sems],
            cost_estimate=pl.CostEstimate(flops=cost, bytes_accessed=cost, transcendentals=0) if cost else None,
            compiler_params=pltpu.CompilerParams(vmem_limit_bytes=4 * words + SPARE),
        )(*operands)

    return run


def eight(rows):
    return -(-rows // 8) * 8


def per_device(right_side, coefficient):
    bx, by, nz = right_side.shape
    across, along = lax.axis_size("gx"), lax.axis_size("gy")
    devices = across * along
    hx, hy, hz = bx // 2, by // 2, nz // 2
    qx, qy = hx // 2, hy // 2
    both = ("gx", "gy")
    tall, tall1 = eight(by + 2 * K0), eight(hy + 2 * K1)
    pieces = (devices, qx * qy // 2, hz)

    slab = (K0 + B0, bx, nz)
    up_rows, down_rows, right_side, coefficient = call(
        slab_kernel, [slab, slab, (bx, by, nz), (bx, by, nz)]
    )(right_side, coefficient)
    low, high = rotate(up_rows, "gy", 1), rotate(down_rows, "gy", -1)
    group = 4
    message, k1 = call(
        conduct_kernel,
        [pieces, (hx, hy, hz)],
        [(hx, by, nz), (hx, by, hz), (qx, hy, hz), (qx, hy, hz), (group, *pieces[1:])],
        held=1,
        sems=(devices // group,),
    )(coefficient)

    plane = (bx, tall, nz)
    slab = (K0 + B0, tall, nz)
    k_own, b_own, up_planes, down_planes = call(widen_kernel, [plane, plane, slab, slab], cost=1000000000000)(
        right_side, coefficient, low, high
    )
    low, high = rotate(up_planes, "gx", 1), rotate(down_planes, "gx", -1)

    k2 = lax.all_to_all(message, both, 0, 0, tiled=True)

    block = (bx + 2 * K0, tall, nz)
    inner = call(fine_inner_kernel, [block] * 8 + [(hx, by, nz)], [block], registers=72)(
        k_own, b_own
    )
    slab = (K1 + B1, hx, hz)
    edges = (2 * K0 + 2, tall, nz)
    field_slab = (2 * S0 * bx, hz)
    *outer, s, b1, up_rows, down_rows, s_up, s_down = call(
        fine_outer_kernel,
        [edges] * 5 + [(bx, by, nz), (hx, hy, hz), slab, slab, field_slab, field_slab],
        [block] * 8 + [(hx, by, nz), block, (hx, by, hz)],
    )(k_own, low, high, k1, *inner)
    planes = 5 * block[0] + VMEM_BYTES // (4 * tall * nz)
    (stash,) = call(stash_kernel, [(planes, tall, nz)], held=1, sems=(15,))(
        *inner[:4], inner[5], *outer
    )
    low, high = rotate(up_rows, "gy", 1), rotate(down_rows, "gy", -1)
    s_low, s_high = rotate(s_up, "gy", 1), rotate(s_down, "gy", -1)
    slab = (K1 + B1, tall1, hz)
    k1_own, b1_own, up_planes, down_planes = call(
        widen_middle_kernel, [(hx, tall1, hz), (hx, tall1, hz), slab, slab], kept=(4,)
    )(k1, b1, low, high, stash)
    low, high = rotate(up_planes, "gx", 1), rotate(down_planes, "gx", -1)

    block1 = (hx + 2 * K1, tall1, hz)
    message, k1, b1, s1 = call(
        middle_down_kernel,
        [pieces] + [block1] * 2 + [(hx, hy, hz)],
        [block1] * 7 + [(qx, hy, hz), (qx, hy, hz), (group, *pieces[1:])],
        held=1,
        sems=(devices // group,),
    )(k1_own, b1_own, low, high, s_low, s_high)
    received = lax.all_to_all(message, both, 0, 0, tiled=True)

    x2, y2 = across * qx, along * qy
    level2, level3 = (y2 // 2 + 2, x2, hz), (y2 // 2 + 2, x2 // 2, hz)
    half2, half3 = (y2 // 2, x2, hz), (y2 // 4, x2 // 2, hz)
    valid = nz // 4
    coarse = call(
        partial(coarse_weights_kernel, valid),
        [level2] * 4 + [level3, (y2 // 4, x2 // 4, hz)],
        [level2] * 3 + [half2] + [level3] * 6 + [half3] * 2,
        registers=48,
    )(k2)
    slab = (2 * S0 * tall + S1 * hy, hz)
    s_rows, up_planes, down_planes = call(field_planes_kernel, [plane, slab, slab])(
        s, s1, s_low, s_high
    )
    low, high = rotate(up_planes, "gx", 1), rotate(down_planes, "gx", -1)
    slab = (S1 * block1[0], hz)
    s_own, s1_own, up_rows, down_rows = call(
        field_rows_kernel, [block, (block1[0], hy, hz), slab, slab]
    )(s_rows, s1, low, high, coarse[-1])
    low, high = rotate(up_rows, "gy", 1), rotate(down_rows, "gy", -1)

    region, *weights = call(
        partial(coarse_kernel, valid),
        [(qy // 2 + EDGE, 3 * qx, hz)] + [block] * 5,
        [level2] * 5 + [half2] * 2 + [level3] * 8 + [half3] * 2,
        kept=(7,),
        sems=(5,),
        registers=40,
    )(received, *coarse, stash)

    count = hx + 2 * EDGE
    field, rest = call(
        fine_up_kernel,
        [(bx, by, nz)] * 2,
        [block1] * 5 + [block, block1, block1, (qx + 2 * EDGE, tall1, hz)]
        + [block, block, (count, tall, hz), (count, tall, nz), (bx, by, nz)],
        held=2,
        sems=(5,),
        registers=96,
    )(region, k1, b1, s1_own, *weights, s_own, low, high)
    return field, rest


def solution(mesh):
    in_specs = (P("gx", "gy", None), P("gx", "gy", None))
    out_specs = (P("gx", "gy", None), P("gx", "gy", None))
    return jax.shard_map(
        per_device, mesh=mesh, in_specs=in_specs, out_specs=out_specs, check_vma=False
    )
```

```python
import math
from functools import partial

import jax
import jax.numpy as jnp
from jax import lax
from jax.experimental import pallas as pl
from jax.experimental.pallas import tpu as pltpu
from jax.sharding import PartitionSpec as P

F32 = jnp.float32
BF16 = jnp.bfloat16

THETA = 1.25
DELTA = 0.75
SIGMA = THETA / DELTA
RHO0 = 1.0 / SIGMA
RHO1 = 1.0 / (2.0 * SIGMA - RHO0)
KEEP = RHO1 * RHO0
GAIN = 2.0 * RHO1 / DELTA
BOTTOM = 8
BOTTOM_THETA = (2.0 + 0.05) / 2.0
BOTTOM_DELTA = (2.0 - 0.05) / 2.0

K0, B0, S0 = 3, 2, 3
K1, B1, S1 = 4, 3, 4
EDGE = 2
REGISTERS = [48]
SPARE = 4 * 1024 * 1024
VMEM_BYTES = 64 * 1024 * 1024
LONG = 10**12


def swap(first, second, axis):
    axes = ("gx", "gy")
    sizes = [lax.axis_size(name) for name in axes]
    along = axes.index(axis)
    size, other = sizes[along], sizes[1 - along]

    def place(i, j):
        return i * sizes[1] + j if along == 0 else j * sizes[1] + i

    def pairs(begin):
        found = []
        for j in range(other):
            for i in range(begin, size - 1, 2):
                found += [(place(i, j), place(i + 1, j)), (place(i + 1, j), place(i, j))]
        met = {source for source, _ in found}
        for i in range(size):
            for j in range(other):
                beside = j + 1 - 2 * (j % 2)
                target = place(i, beside) if beside < other else place(i, j)
                if place(i, j) not in met:
                    found.append((place(i, j), target))
        return found

    return lax.ppermute(first, axes, pairs(0)), lax.ppermute(second, axes, pairs(1))


def is_even(axis):
    return lax.rem(lax.axis_index(axis), 2) == 0


class Either:
    def __init__(self, flag, one, two):
        self.flag, self.one, self.two, self.shape = flag, one, two, one.shape

    def __getitem__(self, index):
        return jnp.where(self.flag, self.one[index], self.two[index])


def sides(axis, first, second):
    even = is_even(axis)
    return Either(even, second, first), Either(even, first, second)


def send(axis, first, second, fill):
    even = is_even(axis)

    @pl.when(even)
    def _():
        fill(first, second)

    @pl.when(jnp.logical_not(even))
    def _():
        fill(second, first)


def inside(axis, side):
    index = lax.axis_index(axis)
    if side < 0:
        return index > 0
    return index < lax.axis_size(axis) - 1


def masked(flag, value):
    return jnp.where(flag, value, jnp.zeros_like(value))


def iota(shape, dim):
    return lax.broadcasted_iota(jnp.int32, shape, dim)


def pick(x, matrix):
    high = x.astype(BF16)
    low = (x - high.astype(F32)).astype(BF16)
    return jnp.dot(high, matrix, preferred_element_type=F32) + jnp.dot(
        low, matrix, preferred_element_type=F32
    )


def halving(fine, coarse, valid):
    row, col = iota((fine, coarse), 0), iota((fine, coarse), 1)
    return jnp.where((row // 2 == col) & (row < valid), 0.125, 0.0).astype(BF16)


def doubling(coarse, fine, valid):
    row, col = iota((coarse, fine), 0), iota((coarse, fine), 1)
    return jnp.where((row == col // 2) & (row < valid), 1.0, 0.0).astype(BF16)


def fetch(refs, stash, sems):
    copies = []
    for i, ref in enumerate(refs):
        planes = ref.shape[0]
        there = stash.at[i * planes : (i + 1) * planes]
        copies.append(pltpu.make_async_copy(there, ref, sems.at[i]))
    for copy in copies:
        copy.start()
    return copies


def wait(copies):
    for copy in copies:
        copy.wait()


def face(a, b):
    product, total = a * b, a + b
    return jnp.where(product > 0.0, 2.0 * product / total, total)


def up(x, axis):
    return pltpu.roll(x, x.shape[axis] - 1, axis)


def down(x, axis):
    return pltpu.roll(x, 1, axis)


def sided(k, axis, edge):
    after = up(k, axis)
    if edge is None:
        w = face(k, after)
        return w, w + down(w, axis)
    place = iota(k.shape, axis)
    if edge < k.shape[axis]:
        place = lax.rem(place, edge)
    last = place == edge - 1
    w = face(k, jnp.where(last, 0.0, after))
    return jnp.where(last, 0.0, w), w + jnp.where(place == 0, k, down(w, axis))


def blocks_of(plane, count):
    most = max(1, REGISTERS[0] // max(1, plane[0] * plane[1] // 1024))
    best = None
    for blocks in range(max(1, count // (2 * most)), count + 1):
        steps = count // blocks
        cost = (count - blocks * steps) * 0.5 + abs(steps - most)
        if best is None or cost < best[0]:
            best = (cost, blocks, steps)
    return best[1:]


def carried(low, high, body, carry, plane):
    blocks, steps = blocks_of(plane, high - low)
    end = low + blocks * steps
    if blocks == 1:
        end = low
        steps = high - low
    elif blocks * steps:
        carry = lax.fori_loop(low, end, body, carry, unroll=steps)
    for i in range(end, high):
        carry = body(i, carry)
    return carry


def loop(low, high, body, plane):
    def step(i, carry):
        body(i)
        return carry

    carried(low, high, step, 0, plane)


def weigh(k, wl, ws, wz, total, inverse, row_edge, lane_edge, span=None, before=None):
    plane = k.shape[1:]
    low, high = span or (0, k.shape[0] - 1)

    def body(i, before):
        here = k[i]
        lead = face(here, k[i + 1])
        rows, row_sum = sided(here, 0, here.shape[0] if row_edge else None)
        lanes, lane_sum = sided(here, 1, here.shape[1] if lane_edge else None)
        wl[i] = lead
        ws[i] = rows
        wz[i] = lanes
        whole = (before + lead) + (row_sum + lane_sum)
        there = here > 0.0
        total[i] = jnp.where(there, whole, 0.0)
        inverse[i] = jnp.where(there, 1.0 / whole, 0.0)
        return lead

    before = jnp.zeros(plane, F32) if before is None else before
    carried(low, high, body, before, plane)


def beside(x, w, i):
    if len(w) == 4:
        return beside_packed(x, w, i)
    wl, ws, wz = w
    here = x[i]
    rows, lanes = ws[i], wz[i]
    out = wl[i] * x[i + 1] + wl[i - 1] * x[i - 1]
    out = out + (rows * up(here, 0) + down(rows * here, 0))
    return out + (lanes * up(here, 1) + down(lanes * here, 1))


def pre_smooth(b, first, second, w, inverse, scale, outer, inner):
    def start(i):
        first[i] = b[i] * inverse[i] * (1.0 / (scale * THETA))

    for span in outer:
        loop(*span, start, b.shape[1:])

    def sweep(i):
        near = beside(first, w, i)
        second[i] = (1.0 + KEEP + GAIN * (THETA - 1.0)) * first[i] + GAIN * (inverse[i] * near)

    for span in inner:
        loop(*span, sweep, b.shape[1:])


def post_smooth(b, first, second, w, inverse, scale, outer, inner):
    def sweep(i):
        x = first[i]
        near = beside(first, w, i)
        second[i] = x + ((b[i] * (1.0 / scale) + near) * inverse[i] - x) * (1.0 / THETA)

    loop(*outer, sweep, b.shape[1:])

    def last(i):
        x = second[i]
        near = beside(second, w, i)
        step = KEEP * (x - first[i]) + GAIN * ((b[i] * (1.0 / scale) + near) * inverse[i] - x)
        first[i] = x + step

    loop(*inner, last, b.shape[1:])


def residual(b, field, w, total, scale, i):
    return b[i] - scale * (total[i] * field[i] - beside(field, w, i))


def coarser(pairs, halves, matrix):
    planes, rows, lanes = pairs.shape
    halves[...] = pick(pairs.reshape(planes * rows, lanes), matrix).reshape(halves.shape)
    count = rows // 2
    return halves[:, pl.ds(0, count, stride=2), :] + halves[:, pl.ds(1, count, stride=2), :]


def packed(pairs, halves, valid):
    planes, rows, lanes = pairs.shape
    matrix = halving(lanes, halves.shape[2], valid)
    halves[...] = pick(pairs.reshape(planes * rows, lanes), matrix).reshape(halves.shape)
    count = rows // 4
    quarter = [halves[:, pl.ds(r, count, stride=4), :] for r in range(4)]
    odd = pltpu.roll(quarter[2] + quarter[3], halves.shape[2] // 2, 2)
    return (quarter[0] + quarter[1]) + odd


def spread_copies(out, held, sems, *fields):
    for f, rows in enumerate(fields):
        size, count = rows.shape[0], rows.shape[1]
        for i in range(size):
            held[0, pl.ds(f * size * count + i, count, stride=size), :] = rows[i]
    group = held.shape[0]
    for d in range(1, group):
        held[d] = held[0]
    copies = []
    for d in range(out.shape[0] // group):
        there = out.at[d * group : (d + 1) * group]
        copies.append(pltpu.make_async_copy(held, there, sems.at[d]))
    for copy in copies:
        copy.start()
    return copies


def slab_kernel(b, k, first, second, b_out, k_out):
    rows = k.shape[1]
    b_out[...] = b[...]
    k_out[...] = k[...]

    def fill(after, before):
        for r in range(K0):
            after[r] = k[:, rows - K0 + r, :]
            before[r] = k[:, r, :]
        for r in range(B0):
            after[K0 + r] = b[:, rows - B0 + r, :]
            before[K0 + r] = b[:, r, :]

    send("gy", first, second, fill)


def conduct_kernel(k, message, k1, pairs, halves, pairs1, halves1, held, sems):
    def add(j):
        pairs[j] = k[2 * j] + k[2 * j + 1]

    loop(0, pairs.shape[0], add, pairs.shape[1:])
    lanes = k.shape[2]
    k1[...] = coarser(pairs[...], halves, halving(lanes, lanes // 2, lanes))

    def add1(j):
        pairs1[j] = k1[2 * j] + k1[2 * j + 1]

    loop(0, pairs1.shape[0], add1, pairs1.shape[1:])
    wait(spread_copies(message, held, sems, packed(pairs1[...], halves1, k1.shape[2])))


def widen(out, own, low, high, count):
    planes, rows, lanes = own.shape
    size = out.shape[1]
    out[:, 0:rows, :] = own[...]
    out[:, rows:, :] = jnp.zeros((planes, size - rows, lanes), F32)
    below, above = inside("gy", -1), inside("gy", 1)
    for r in range(count):
        out[:, size - count + r, :] = masked(below, low(r))
        out[:, rows + r, :] = masked(above, high(r))


def widen_kernel(b, k, from_first, from_second, k_out, b_out, first, second):
    low, high = sides("gy", from_first, from_second)
    widen(k_out, k, lambda r: low[r], lambda r: high[r], K0)
    widen(b_out, b, lambda r: low[K0 + r], lambda r: high[K0 + r], B0)
    planes = k.shape[0]

    def fill(after, before):
        after[0:K0] = k_out[planes - K0 :]
        after[K0:] = b_out[planes - B0 :]
        before[0:K0] = k_out[0:K0]
        before[K0:] = b_out[0:B0]

    send("gx", first, second, fill)


def join(out, own, low, high, count, halo):
    planes = own.shape[0]
    left, right = inside("gx", -1), inside("gx", 1)
    out[halo : halo + planes] = own[...]
    for r in range(halo):
        below, above = halo - 1 - r, halo + planes + r
        if r < count:
            out[below] = masked(left, low(count - 1 - r))
            out[above] = masked(right, high(r))
        else:
            out[below] = jnp.zeros(out.shape[1:], F32)
            out[above] = jnp.zeros(out.shape[1:], F32)


def fine_inner_kernel(k_own, b_own, wl, ws, wz, total, inverse, b, first, second, pairs, k):
    own, planes = k_own.shape[0], b.shape[0]
    k[K0 : K0 + own] = k_own[...]
    b[K0 : K0 + own] = b_own[...]
    low, high, rows = K0, planes - K0, pairs.shape[1]
    weigh(k, wl, ws, wz, total, inverse, False, True, (low, high - 1))
    pre_smooth(
        b, first, second, (wl, ws, wz), inverse, 1.0, [(low + 1, high - 1)], [(low + 2, high - 2)]
    )
    fine_restrict(b, second, (wl, ws, wz), total, pairs, (2, own // 2 - 2))


def fine_restrict(b, field, w, total, pairs, span):
    rows = pairs.shape[1]

    def restrict(j):
        i = 2 * j + K0
        both = residual(b, field, w, total, 1.0, i) + residual(b, field, w, total, 1.0, i + 1)
        pairs[j] = both[0:rows]

    loop(*span, restrict, (2 * b.shape[1], b.shape[2]))


def put_rows(out, at, parts):
    lanes = out.shape[1]
    for part in parts:
        rows = part.shape[0]
        for h in range(part.shape[1] // lanes):
            out[at : at + rows] = part[:, h * lanes : (h + 1) * lanes]
            at += rows
    return at


def fine_outer_kernel(
    k_own, from_first, from_second, k1,
    wl_in, ws_in, wz_in, total_in, inverse_in, b_in, first_in, second_in, pairs_in,
    wl_out, ws_out, wz_out, total_out, b_out, s_out, b1_out, first_out, second_out, s_first, s_second,
    wl, ws, wz, total, inverse, b, first, second, pairs, k, halves,
):
    low, high = sides("gx", from_first, from_second)
    planes, rows, lanes = b.shape[0], s_out.shape[1], b.shape[2]
    own, end = planes - 2 * K0, planes - K0
    for mine, inner in (
        (wl, wl_in), (ws, ws_in), (wz, wz_in), (total, total_in), (inverse, inverse_in), (b, b_in),
        (first, first_in), (second, second_in),
    ):
        mine[K0 : K0 + 5] = inner[K0 : K0 + 5]
        mine[end - 5 : end] = inner[end - 5 : end]
    left, right = inside("gx", -1), inside("gx", 1)
    for r in range(K0):
        k[r] = masked(left, low[r])
        k[end + r] = masked(right, high[r])
    for r in range(B0):
        b[K0 - B0 + r] = masked(left, low[K0 + r])
        b[end + r] = masked(right, high[K0 + r])
    for r in range(2):
        k[K0 + r] = k_own[r]
        k[end - 2 + r] = k_own[own - 2 + r]
    w = (wl, ws, wz)
    weigh(k, wl, ws, wz, total, inverse, False, True, (0, K0 + 1))
    weigh(k, wl, ws, wz, total, inverse, False, True, (end - 1, planes - 1), wl[end - 2])
    pre_smooth(
        b, first, second, w, inverse, 1.0,
        [(1, K0 + 1), (end - 1, planes - 1)], [(2, K0 + 2), (end - 2, planes - 2)],
    )
    pairs[2 : own // 2 - 2] = pairs_in[2 : own // 2 - 2]
    fine_restrict(b, second, w, total, pairs, (0, 2))
    fine_restrict(b, second, w, total, pairs, (own // 2 - 2, own // 2))
    b1_out[...] = coarser(pairs[...], halves, halving(lanes, lanes // 2, lanes))
    s_out[2 : own - 2] = second_in[K0 + 2 : end - 2, 0:rows, :]
    for at in (0, own - 2):
        s_out[at : at + 2] = second[K0 + at : K0 + at + 2, 0:rows, :]
    for out, mine in ((wl_out, wl), (ws_out, ws), (wz_out, wz), (total_out, total), (b_out, b)):
        out[0 : K0 + 1] = mine[0 : K0 + 1]
        out[K0 + 1 :] = mine[end - 1 :]
    count = b1_out.shape[1]

    def fill(after, before):
        for out, k_from, b_from in ((after, count - K1, count - B1), (before, 0, 0)):
            for r in range(K1):
                out[r] = k1[:, k_from + r, :]
            for r in range(B1):
                out[K1 + r] = b1_out[:, b_from + r, :]

    def fill_field(after, before):
        put_rows(after, 0, [s_out[:, rows - S0 + r, :] for r in range(S0)])
        put_rows(before, 0, [s_out[:, r, :] for r in range(S0)])

    send("gy", first_out, second_out, fill)
    send("gy", s_first, s_second, fill_field)


def stash_kernel(*refs):
    inner, outer, (stash, sems) = refs[:5], refs[5:10], refs[10:]
    planes, edge = inner[0].shape[0], K0 + 1
    copies = []
    for i in range(5):
        for j, (source, first, at, count) in enumerate((
            (inner[i], edge, edge, planes - 2 * edge),
            (outer[i], 0, 0, edge),
            (outer[i], edge, planes - edge, edge),
        )):
            copies.append(
                pltpu.make_async_copy(
                    source.at[first : first + count],
                    stash.at[i * planes + at : i * planes + at + count],
                    sems.at[3 * i + j],
                )
            )
    for copy in copies:
        copy.start()
    wait(copies)


def widen_middle_kernel(
    k1, b1, from_first, from_second, _stash, k_out, b_out, first, second
):
    low, high = sides("gy", from_first, from_second)
    widen(k_out, k1, lambda r: low[r], lambda r: high[r], K1)
    widen(b_out, b1, lambda r: low[K1 + r], lambda r: high[K1 + r], B1)
    planes = k1.shape[0]

    def fill(after, before):
        after[0:K1] = k_out[planes - K1 :]
        after[K1:] = b_out[planes - B1 :]
        before[0:K1] = k_out[0:K1]
        before[K1:] = b_out[0:B1]

    send("gx", first, second, fill)


def middle_down_kernel(
    k_own, b_own, from_first, from_second, _s_first, _s_second,
    message, k, b, s_out,
    wl, ws, wz, inverse, total, first, second, pairs, halves, held, sems,
):
    scale = 0.25
    low, high = sides("gx", from_first, from_second)
    join(k, k_own, lambda r: low[r], lambda r: high[r], K1, K1)
    join(b, b_own, lambda r: low[K1 + r], lambda r: high[K1 + r], B1, K1)
    w = (wl, ws, wz)
    weigh(k, wl, ws, wz, total, inverse, False, True)
    planes, lanes = b.shape[0], b.shape[2]
    own, rows = planes - 2 * K1, s_out.shape[1]
    pre_smooth(b, first, second, w, inverse, scale, [(1, planes - 1)], [(2, planes - 2)])

    def restrict(j):
        i = 2 * j + K1
        both = residual(b, second, w, total, scale, i) + residual(b, second, w, total, scale, i + 1)
        pairs[j] = both[0:rows]

    loop(0, own // 2, restrict, (2 * b.shape[1], b.shape[2]))
    copies = spread_copies(message, held, sems, packed(pairs[...], halves, lanes))
    s_out[...] = second[K1 : K1 + own, 0:rows, :]
    wait(copies)


def split_lanes(ref, first, rows):
    def get(r):
        at = first + 2 * r * rows
        return jnp.concatenate([ref[at : at + rows], ref[at + rows : at + 2 * rows]], axis=1)

    return get


def from_row(ref, first, rows):
    def get(r):
        return ref[first + r * rows : first + (r + 1) * rows]

    return get


def field_planes_kernel(s, s1, from_first, from_second, s_out, first, second):
    low, high = sides("gy", from_first, from_second)
    fine, own = s.shape[0], s1.shape[0]
    widen(s_out, s, split_lanes(low, 0, fine), split_lanes(high, 0, fine), S0)

    def fill(after, before):
        for out, from0, from1 in ((after, fine - S0, own - S1), (before, 0, 0)):
            at = put_rows(out, 0, [s_out[from0 + r] for r in range(S0)])
            put_rows(out, at, [s1[from1 + r] for r in range(S1)])

    send("gx", first, second, fill)


def field_rows_kernel(
    s, s1, from_first, from_second, _weights, s_out, s1_out, first, second
):
    low, high = sides("gx", from_first, from_second)
    rows, rows1 = s.shape[1], s1.shape[1]
    join(s_out, s, split_lanes(low, 0, rows), split_lanes(high, 0, rows), S0, S0)
    at = 2 * S0 * rows
    join(s1_out, s1, from_row(low, at, rows1), from_row(high, at, rows1), S1, S1)

    def fill(after, before):
        put_rows(after, 0, [s1_out[:, rows1 - S1 + r, :] for r in range(S1)])
        put_rows(before, 0, [s1_out[:, r, :] for r in range(S1)])

    send("gy", first, second, fill)


def unpack(received, out, first, block_x, block_y, across, along):
    clear_ends(out)

    def place(column):
        for row in range(across):
            for j in range(block_y // 2):
                piece = received[row * along + column, pl.ds(first + j * block_x, block_x), :]
                at = 1 + column * (block_y // 2) + j
                out[at, row * block_x : (row + 1) * block_x, :] = piece

    loop(0, along, place, (out.shape[1], block_y // 2 * out.shape[2]))


def clear_ends(ref):
    for end in (0, ref.shape[0] - 1):
        ref[end] = jnp.zeros(ref.shape[1:], F32)


def across_up(x, after):
    half = x.shape[1] // 2
    return pltpu.roll(jnp.where(iota(x.shape, 1) < half, after, x), half, 1)


def across_down(x, before):
    half = x.shape[1] // 2
    return pltpu.roll(jnp.where(iota(x.shape, 1) < half, x, before), half, 1)


def weigh_packed(k, wl, wl_low, ws, wz, total, inverse):
    planes = k.shape[0]

    def body(i, before):
        here = k[i]
        lead = face(here, across_up(here, k[i + 1]))
        lead_low = across_down(lead, before)
        rows, row_sum = sided(here, 0, here.shape[0])
        lanes, lane_sum = sided(here, 1, here.shape[1] // 2)
        wl[i] = lead
        wl_low[i] = lead_low
        ws[i] = rows
        wz[i] = lanes
        whole = (lead_low + lead) + (row_sum + lane_sum)
        there = here > 0.0
        total[i] = jnp.where(there, whole, 0.0)
        inverse[i] = jnp.where(there, 1.0 / whole, 0.0)
        return lead

    carried(0, planes - 1, body, jnp.zeros(k.shape[1:], F32), k.shape[1:])


def beside_packed(x, w, i):
    wl, wl_low, ws, wz = w
    here = x[i]
    rows, lanes = ws[i], wz[i]
    out = wl[i] * across_up(here, x[i + 1]) + wl_low[i] * across_down(here, x[i - 1])
    out = out + (rows * up(here, 0) + down(rows * here, 0))
    return out + (lanes * up(here, 1) + down(lanes * here, 1))


def coarse_pre(b, w, inverse, first, second, scale):
    ends = [(1, b.shape[0] - 1)]
    clear_ends(first)
    clear_ends(second)
    pre_smooth(b, first, second, w, inverse, scale, ends, ends)


def widened(x, matrix):
    planes, rows, lanes = x.shape
    return pick(x.reshape(planes * rows, lanes), matrix).reshape(planes, rows, matrix.shape[1])


def twice(out, x):
    out[:, pl.ds(0, x.shape[1], stride=2), :] = x
    out[:, pl.ds(1, x.shape[1], stride=2), :] = x


def bottom(k, b, scale):
    planes, rows, lanes = k.shape
    none = jnp.zeros((1, rows, lanes), F32)

    def after(v):
        return jnp.concatenate([v[1:], none], axis=0)

    def before(v):
        return jnp.concatenate([none, v[:-1]], axis=0)

    lead = face(k, after(k))
    lead_low = jnp.concatenate([k[:1], lead[:-1]], axis=0)
    row = iota(k.shape, 1)
    row_w = face(k, jnp.where(row == rows - 1, 0.0, up(k, 1)))
    row_low = jnp.where(row == 0, k, down(row_w, 1))
    lane_w = face(k, up(k, 2))
    lane_low = down(lane_w, 2)
    whole = ((lead + lead_low) + (row_w + row_low)) + (lane_w + lane_low)
    inverse = jnp.where(k > 0.0, 1.0 / whole, 0.0)
    source = b * inverse * (1.0 / scale)
    lead_i, lead_low_i = lead * inverse, lead_low * inverse
    row_i = jnp.where(row == rows - 1, 0.0, row_w) * inverse
    row_low_i = jnp.where(row == 0, 0.0, row_low) * inverse
    lane_i, lane_low_i = lane_w * inverse, lane_low * inverse
    sigma = BOTTOM_THETA / BOTTOM_DELTA
    rho = 1.0 / sigma
    step = source * (1.0 / BOTTOM_THETA)
    x = step
    for _ in range(BOTTOM - 1):
        following = 1.0 / (2.0 * sigma - rho)
        near = (lead_i * after(x) + lead_low_i * before(x)) + (
            row_i * up(x, 1) + row_low_i * down(x, 1)
        )
        near = near + (lane_i * up(x, 2) + lane_low_i * down(x, 2))
        step = (following * rho) * step + (2.0 * following / BOTTOM_DELTA) * (source - x + near)
        x = x + step
        rho = following
    return x


def mean_matrix(lanes, valid):
    row, col = iota((lanes, lanes), 0), iota((lanes, lanes), 1)
    return jnp.where(lax.rem(row, valid) // 2 == col, 0.125, 0.0).astype(BF16)


def coarse_weights_kernel(
    valid, received, wl2, ws2, wz2, total2, level3, k4,
    low2, inverse2, k2, halves2, wl3, ws3, wz3, total3, inverse3, k3, pairs3, halves3,
):
    planes, rows, lanes = k2.shape
    across, along = lax.axis_size("gx"), lax.axis_size("gy")
    unpack(received, k2, 0, rows // across, 2 * (planes - 2) // along, across, along)
    own3 = planes - 2
    clear_ends(k3)
    k3[1 : own3 + 1] = coarser(k2[1 : own3 + 1], halves2, mean_matrix(lanes, valid))

    def add3(j):
        pairs3[j] = k3[2 * j + 1] + k3[2 * j + 2]

    loop(0, pairs3.shape[0], add3, pairs3.shape[1:])
    k4[...] = coarser(pairs3[...], halves3, halving(lanes, lanes, valid // 2))
    weigh_packed(k2, wl2, low2, ws2, wz2, total2, inverse2)
    weigh(k3, wl3, ws3, wz3, total3, inverse3, True, False)

    def pack(i):
        lane = iota(level3.shape[1:], 1)
        parts = [jnp.where(lane < valid // 2, ref[i], 0.0) for ref in (wl3, ws3, wz3, total3)]
        level3[i] = sum(
            (pltpu.roll(part, f * (valid // 2), 1) for f, part in enumerate(parts) if f), parts[0]
        )

    loop(0, planes - 1, pack, level3.shape[1:])


def invert(total):
    return jnp.where(total > 0.0, 1.0 / total, 0.0)


def coarse_kernel(
    valid, received, wl2, ws2, wz2, total2, level3, k4, stash,
    region, wl, ws, wz, total, b,
    low2, inverse2, b2, first2, second2, pairs2, halves2,
    wl3, ws3, wz3, total3, inverse3, b3, first3, second3, pairs3, halves3, sems,
):
    copies = fetch((wl, ws, wz, total, b), stash, sems)
    planes, rows, lanes = b2.shape
    across, along = lax.axis_size("gx"), lax.axis_size("gy")
    block_x, block_y = rows // across, 2 * (planes - 2) // along
    own3, half = planes - 2, valid // 2
    unpack(received, b2, 0, block_x, block_y, across, along)
    row, col = iota((lanes, lanes), 0), iota((lanes, lanes), 1)
    matrix2, matrix3 = mean_matrix(lanes, valid), halving(lanes, lanes, half)

    def complete(i):
        low2[i] = across_down(wl2[i], wl2[i - 1])
        inverse2[i] = invert(total2[i])

    def unpack3(i):
        lane = iota(level3.shape[1:], 1)
        for f, ref in enumerate((wl3, ws3, wz3, total3)):
            part = level3[i]
            if f:
                part = pltpu.roll(part, lanes - f * half, 1)
            ref[i] = jnp.where(lane < half, part, 0.0)
        inverse3[i] = invert(total3[i])

    loop(1, own3 + 1, complete, b2.shape[1:])
    loop(0, own3 + 1, unpack3, level3.shape[1:])
    w2, w3 = (wl2, low2, ws2, wz2), (wl3, ws3, wz3)
    scale2, scale3 = 0.25**2, 0.25**3
    coarse_pre(b2, w2, inverse2, first2, second2, scale2)

    def rest2(j):
        pairs2[j] = residual(b2, second2, w2, total2, scale2, j + 1)

    loop(0, own3, rest2, pairs2.shape[1:])
    clear_ends(b3)
    b3[1 : own3 + 1] = coarser(pairs2[...], halves2, matrix2)
    coarse_pre(b3, w3, inverse3, first3, second3, scale3)

    def rest3(j):
        i = 2 * j + 1
        pairs3[j] = residual(b3, second3, w3, total3, scale3, i) + residual(
            b3, second3, w3, total3, scale3, i + 1
        )

    loop(0, pairs3.shape[0], rest3, pairs3.shape[1:])
    x4 = bottom(k4[...], coarser(pairs3[...], halves3, matrix3), 0.25**4)
    twice(pairs3, widened(x4, doubling(lanes, lanes, half // 2)))

    def add_up3(j):
        for side in range(2):
            i = 2 * j + 1 + side
            first3[i] = second3[i] + pairs3[j]

    loop(0, pairs3.shape[0], add_up3, pairs3.shape[1:])
    ends = (1, own3 + 1)
    post_smooth(b3, first3, second3, w3, inverse3, scale3, ends, ends)
    matrix = jnp.where((lax.rem(col, valid) // 2 == row) & (row < half), 1.0, 0.0).astype(BF16)
    twice(pairs2, widened(first3[1 : own3 + 1], matrix))

    def add_up2(i):
        first2[i] = second2[i] + pairs2[i - 1]

    loop(1, own3 + 1, add_up2, pairs2.shape[1:])
    post_smooth(b2, first2, second2, w2, inverse2, scale2, ends, ends)
    column, place = lax.axis_index("gy"), lax.axis_index("gx")
    for q in range(region.shape[0]):
        plane = column * (block_y // 2) + q - EDGE // 2
        for side in range(3):
            block = place + side - 1
            there = (plane >= 0) & (plane < planes - 2) & (block >= 0) & (block < across)
            start = pl.multiple_of(jnp.clip(block, 0, across - 1) * block_x, block_x)
            value = first2[1 + jnp.clip(plane, 0, planes - 3), pl.ds(start, block_x), :]
            region[q, side * block_x : (side + 1) * block_x, :] = masked(there, value)
    wait(copies)


def fine_up_kernel(
    region, k1, b1, s1_own, wl, ws, wz, total, b, s_own, from_first, from_second,
    field_out, residual_out,
    wl1, ws1, wz1, total1, inverse1, inverse, first1, second1, grown, s, second, tall, thick, rest,
    out_sems,
):
    planes1, rows1, lanes1 = b1.shape
    planes, rows, lanes = b.shape
    w1, w = (wl1, ws1, wz1), (wl, ws, wz)
    weigh(k1, wl1, ws1, wz1, total1, inverse1, False, True)
    low, high = sides("gy", from_first, from_second)
    widen(first1, s1_own, from_row(low, 0, planes1), from_row(high, 0, planes1), S1)
    count_y, block_x = region.shape[0], region.shape[1] // 3
    expanded = widened(region[...], doubling(lanes1, 2 * lanes1, lanes1))
    for q in range(block_x + 2 * EDGE):
        line = expanded[:, block_x - EDGE + q, :]
        line = jnp.concatenate([line[EDGE // 2 :], line[: EDGE // 2]], axis=0)
        for r in range(4):
            half = line[:, (r // 2) * lanes1 : (r // 2 + 1) * lanes1]
            grown[q, pl.ds(r, count_y, stride=4), :] = half

    def add1(q):
        for side in range(2):
            first1[2 * q + side] = first1[2 * q + side] + grown[q]

    loop(0, block_x + 2 * EDGE, add1, b1.shape[1:])
    post_smooth(
        b1, first1, second1, w1, inverse1, 0.25, (1, planes1 - 1), (2, planes1 - 2)
    )
    begin, count = S1 - EDGE, planes1 - 2 * S1 + 2 * EDGE
    own1 = rows1 - 2 * S1
    edge = 2 * EDGE
    for half, at, where in ((own1 + EDGE, 0, 0), (EDGE, rows1 - EDGE, 2 * (own1 + EDGE))):
        part = first1[begin : begin + count, at : at + half, :]
        tall[:, pl.ds(where, half, stride=2), :] = part
        tall[:, pl.ds(where + 1, half, stride=2), :] = part
    matrix = doubling(lanes1, lanes, lanes1)
    thick[...] = pick(tall[...].reshape(count * rows, lanes1), matrix).reshape(thick.shape)
    s[0] = s_own[0] + thick[0]
    s[planes - 1] = s_own[planes - 1] + thick[count - 1]

    def add(q):
        for side in range(2):
            i = 2 * q + side - 1
            s[i] = s_own[i] + thick[q]

    loop(1, count - 1, add, b.shape[1:])

    def complete(i):
        inverse[i] = invert(total[i])

    loop(1, planes - 1, complete, b.shape[1:])
    post_smooth(b, s, second, w, inverse, 1.0, (1, planes - 1), (2, planes - 2))
    own, own_rows = field_out.shape[0], field_out.shape[1]
    mine = s.at[K0 : K0 + own, 0:own_rows]
    copies = [pltpu.make_async_copy(mine, field_out, out_sems.at[0])]
    copies[0].start()

    def finish(j):
        rest[j] = residual(b, s, w, total, 1.0, j + K0)[0:own_rows]

    parts = out_sems.shape[0] - 1
    for part in range(parts):
        begin, end = own * part // parts, own * (part + 1) // parts
        loop(begin, end, finish, b.shape[1:])
        copy = pltpu.make_async_copy(
            rest.at[begin:end], residual_out.at[begin:end], out_sems.at[1 + part]
        )
        copy.start()
        copies.append(copy)
    wait(copies)


def call(kernel, outs, scratch=(), held=0, kept=(), sems=(), cost=0, registers=48):
    def body(*refs):
        REGISTERS[0] = registers
        kernel(*refs)

    def run(*operands):
        inputs = [o.shape for i, o in enumerate(operands) if i not in kept]
        shapes = inputs + list(outs[held:]) + list(scratch)
        words = sum(math.prod(s[:-2]) * eight(s[-2]) * s[-1] for s in shapes)
        places = [pltpu.HBM if i in kept else pltpu.VMEM for i in range(len(operands))]
        out_places = [pltpu.HBM if i < held else pltpu.VMEM for i in range(len(outs))]
        return pl.pallas_call(
            body,
            out_shape=[jax.ShapeDtypeStruct(shape, F32) for shape in outs],
            in_specs=[pl.BlockSpec(memory_space=place) for place in places],
            out_specs=[pl.BlockSpec(memory_space=place) for place in out_places],
            scratch_shapes=[pltpu.VMEM(shape, F32) for shape in scratch]
            + [pltpu.SemaphoreType.DMA((n,)) for n in sems],
            cost_estimate=pl.CostEstimate(flops=cost, bytes_accessed=cost, transcendentals=0) if cost else None,
            compiler_params=pltpu.CompilerParams(vmem_limit_bytes=4 * words + SPARE),
        )(*operands)

    return run


def eight(rows):
    return -(-rows // 8) * 8


def per_device(right_side, coefficient):
    bx, by, nz = right_side.shape
    across, along = lax.axis_size("gx"), lax.axis_size("gy")
    devices = across * along
    hx, hy, hz = bx // 2, by // 2, nz // 2
    qx, qy = hx // 2, hy // 2
    both = ("gx", "gy")
    tall, tall1 = eight(by + 2 * K0), eight(hy + 2 * K1)
    pieces = (devices, qx * qy // 2, hz)

    slab = (K0 + B0, bx, nz)
    first, second, right_side, coefficient = call(
        slab_kernel, [slab, slab, (bx, by, nz), (bx, by, nz)]
    )(right_side, coefficient)
    from_first, from_second = swap(first, second, "gy")
    group = 4
    message, k1 = call(
        conduct_kernel,
        [pieces, (hx, hy, hz)],
        [(hx, by, nz), (hx, by, hz), (qx, hy, hz), (qx, hy, hz), (group, *pieces[1:])],
        held=1,
        sems=(devices // group,),
    )(coefficient)

    plane = (bx, tall, nz)
    slab = (K0 + B0, tall, nz)
    k_own, b_own, first, second = call(widen_kernel, [plane, plane, slab, slab], cost=LONG)(
        right_side, coefficient, from_first, from_second
    )
    from_first, from_second = swap(first, second, "gx")

    k2 = lax.all_to_all(message, both, 0, 0, tiled=True)

    block = (bx + 2 * K0, tall, nz)
    inner = call(fine_inner_kernel, [block] * 8 + [(hx, by, nz)], [block], registers=72)(
        k_own, b_own
    )
    slab = (K1 + B1, hx, hz)
    edges = (2 * K0 + 2, tall, nz)
    field_slab = (2 * S0 * bx, hz)
    *outer, s, b1, first, second, s_out_first, s_out_second = call(
        fine_outer_kernel,
        [edges] * 5 + [(bx, by, nz), (hx, hy, hz), slab, slab, field_slab, field_slab],
        [block] * 8 + [(hx, by, nz), block, (hx, by, hz)],
    )(k_own, from_first, from_second, k1, *inner)
    planes = 5 * block[0] + VMEM_BYTES // (4 * tall * nz)
    (stash,) = call(stash_kernel, [(planes, tall, nz)], held=1, sems=(15,))(
        *inner[:4], inner[5], *outer
    )
    from_first, from_second = swap(first, second, "gy")
    s_first, s_second = swap(s_out_first, s_out_second, "gy")
    slab = (K1 + B1, tall1, hz)
    k1_own, b1_own, first, second = call(
        widen_middle_kernel, [(hx, tall1, hz), (hx, tall1, hz), slab, slab], kept=(4,)
    )(k1, b1, from_first, from_second, stash)
    from_first, from_second = swap(first, second, "gx")

    block1 = (hx + 2 * K1, tall1, hz)
    message, k1, b1, s1 = call(
        middle_down_kernel,
        [pieces] + [block1] * 2 + [(hx, hy, hz)],
        [block1] * 7 + [(qx, hy, hz), (qx, hy, hz), (group, *pieces[1:])],
        held=1,
        sems=(devices // group,),
    )(k1_own, b1_own, from_first, from_second, s_first, s_second)
    received = lax.all_to_all(message, both, 0, 0, tiled=True)

    x2, y2 = across * qx, along * qy
    level2, level3 = (y2 // 2 + 2, x2, hz), (y2 // 2 + 2, x2 // 2, hz)
    half2, half3 = (y2 // 2, x2, hz), (y2 // 4, x2 // 2, hz)
    valid = nz // 4
    coarse = call(
        partial(coarse_weights_kernel, valid),
        [level2] * 4 + [level3, (y2 // 4, x2 // 4, hz)],
        [level2] * 3 + [half2] + [level3] * 6 + [half3] * 2,
        registers=48,
    )(k2)
    slab = (2 * S0 * tall + S1 * hy, hz)
    s_rows, first, second = call(field_planes_kernel, [plane, slab, slab])(
        s, s1, s_first, s_second
    )
    from_first, from_second = swap(first, second, "gx")
    slab = (S1 * block1[0], hz)
    s_own, s1_own, first, second = call(
        field_rows_kernel, [block, (block1[0], hy, hz), slab, slab]
    )(s_rows, s1, from_first, from_second, coarse[-1])
    from_first, from_second = swap(first, second, "gy")

    region, *weights = call(
        partial(coarse_kernel, valid),
        [(qy // 2 + EDGE, 3 * qx, hz)] + [block] * 5,
        [level2] * 5 + [half2] * 2 + [level3] * 8 + [half3] * 2,
        kept=(7,),
        sems=(5,),
        registers=40,
    )(received, *coarse, stash)

    count = hx + 2 * EDGE
    field, rest = call(
        fine_up_kernel,
        [(bx, by, nz)] * 2,
        [block1] * 5 + [block, block1, block1, (qx + 2 * EDGE, tall1, hz)]
        + [block, block, (count, tall, hz), (count, tall, nz), (bx, by, nz)],
        held=2,
        sems=(5,),
        registers=96,
    )(region, k1, b1, s1_own, *weights, s_own, from_first, from_second)
    return field, rest


def solution(mesh):
    in_specs = (P("gx", "gy", None), P("gx", "gy", None))
    out_specs = (P("gx", "gy", None), P("gx", "gy", None))
    return jax.shard_map(
        per_device, mesh=mesh, in_specs=in_specs, out_specs=out_specs, check_vma=False
    )
```

```python
import math
from functools import partial

import jax
import jax.numpy as jnp
from jax import lax
from jax.experimental import pallas as pl
from jax.experimental.pallas import tpu as pltpu
from jax.sharding import PartitionSpec as P

F32 = jnp.float32
BF16 = jnp.bfloat16

THETA = 1.25
DELTA = 0.75
SIGMA = THETA / DELTA
RHO0 = 1.0 / SIGMA
RHO1 = 1.0 / (2.0 * SIGMA - RHO0)
KEEP = RHO1 * RHO0
GAIN = 2.0 * RHO1 / DELTA
BOTTOM = 8
BOTTOM_THETA = (2.0 + 0.05) / 2.0
BOTTOM_DELTA = (2.0 - 0.05) / 2.0

K0, B0, S0 = 3, 2, 3
K1, B1, S1 = 4, 3, 4
EDGE = 2
REGISTERS = [48]
SPARE = 4 * 1024 * 1024
VMEM_BYTES = 64 * 1024 * 1024
LONG = 10**12


def swap(first, second, axis):
    axes = ("gx", "gy")
    sizes = [lax.axis_size(name) for name in axes]
    along = axes.index(axis)
    size, other = sizes[along], sizes[1 - along]

    def place(i, j):
        return i * sizes[1] + j if along == 0 else j * sizes[1] + i

    def pairs(begin):
        found = []
        for j in range(other):
            for i in range(begin, size - 1, 2):
                found += [(place(i, j), place(i + 1, j)), (place(i + 1, j), place(i, j))]
        met = {source for source, _ in found}
        for i in range(size):
            for j in range(other):
                beside = j + 1 - 2 * (j % 2)
                target = place(i, beside) if beside < other else place(i, j)
                if place(i, j) not in met:
                    found.append((place(i, j), target))
        return found

    return lax.ppermute(first, axes, pairs(0)), lax.ppermute(second, axes, pairs(1))


def is_even(axis):
    return lax.rem(lax.axis_index(axis), 2) == 0


class Either:
    def __init__(self, flag, one, two):
        self.flag, self.one, self.two, self.shape = flag, one, two, one.shape

    def __getitem__(self, index):
        return jnp.where(self.flag, self.one[index], self.two[index])


def sides(axis, first, second):
    even = is_even(axis)
    return Either(even, second, first), Either(even, first, second)


def send(axis, first, second, fill):
    even = is_even(axis)

    @pl.when(even)
    def _():
        fill(first, second)

    @pl.when(jnp.logical_not(even))
    def _():
        fill(second, first)


def inside(axis, side):
    index = lax.axis_index(axis)
    if side < 0:
        return index > 0
    return index < lax.axis_size(axis) - 1


def masked(flag, value):
    return jnp.where(flag, value, jnp.zeros_like(value))


def iota(shape, dim):
    return lax.broadcasted_iota(jnp.int32, shape, dim)


def pick(x, matrix):
    high = x.astype(BF16)
    low = (x - high.astype(F32)).astype(BF16)
    return jnp.dot(high, matrix, preferred_element_type=F32) + jnp.dot(
        low, matrix, preferred_element_type=F32
    )


def halving(fine, coarse, valid):
    row, col = iota((fine, coarse), 0), iota((fine, coarse), 1)
    return jnp.where((row // 2 == col) & (row < valid), 0.125, 0.0).astype(BF16)


def doubling(coarse, fine, valid):
    row, col = iota((coarse, fine), 0), iota((coarse, fine), 1)
    return jnp.where((row == col // 2) & (row < valid), 1.0, 0.0).astype(BF16)


def fetch(refs, stash, sems):
    copies = []
    for i, ref in enumerate(refs):
        planes = ref.shape[0]
        there = stash.at[i * planes : (i + 1) * planes]
        copies.append(pltpu.make_async_copy(there, ref, sems.at[i]))
    for copy in copies:
        copy.start()
    return copies


def wait(copies):
    for copy in copies:
        copy.wait()


def face(a, b):
    product, total = a * b, a + b
    return jnp.where(product > 0.0, 2.0 * product / total, total)


def up(x, axis):
    return pltpu.roll(x, x.shape[axis] - 1, axis)


def down(x, axis):
    return pltpu.roll(x, 1, axis)


def sided(k, axis, edge):
    after = up(k, axis)
    if edge is None:
        w = face(k, after)
        return w, w + down(w, axis)
    place = iota(k.shape, axis)
    if edge < k.shape[axis]:
        place = lax.rem(place, edge)
    last = place == edge - 1
    w = face(k, jnp.where(last, 0.0, after))
    return jnp.where(last, 0.0, w), w + jnp.where(place == 0, k, down(w, axis))


def blocks_of(plane, count):
    most = max(1, REGISTERS[0] // max(1, plane[0] * plane[1] // 1024))
    best = None
    for blocks in range(max(1, count // (2 * most)), count + 1):
        steps = count // blocks
        cost = (count - blocks * steps) * 0.5 + abs(steps - most)
        if best is None or cost < best[0]:
            best = (cost, blocks, steps)
    return best[1:]


def carried(low, high, body, carry, plane):
    blocks, steps = blocks_of(plane, high - low)
    end = low + blocks * steps
    if blocks == 1:
        end = low
        steps = high - low
    elif blocks * steps:
        carry = lax.fori_loop(low, end, body, carry, unroll=steps)
    for i in range(end, high):
        carry = body(i, carry)
    return carry


def loop(low, high, body, plane):
    def step(i, carry):
        body(i)
        return carry

    carried(low, high, step, 0, plane)


def weigh(k, wl, ws, wz, total, inverse, row_edge, lane_edge, span=None, before=None):
    plane = k.shape[1:]
    low, high = span or (0, k.shape[0] - 1)

    def body(i, before):
        here = k[i]
        lead = face(here, k[i + 1])
        rows, row_sum = sided(here, 0, here.shape[0] if row_edge else None)
        lanes, lane_sum = sided(here, 1, here.shape[1] if lane_edge else None)
        wl[i] = lead
        ws[i] = rows
        wz[i] = lanes
        whole = (before + lead) + (row_sum + lane_sum)
        there = here > 0.0
        total[i] = jnp.where(there, whole, 0.0)
        inverse[i] = jnp.where(there, 1.0 / whole, 0.0)
        return lead

    before = jnp.zeros(plane, F32) if before is None else before
    carried(low, high, body, before, plane)


def beside(x, w, i):
    if len(w) == 4:
        return beside_packed(x, w, i)
    wl, ws, wz = w
    here = x[i]
    rows, lanes = ws[i], wz[i]
    out = wl[i] * x[i + 1] + wl[i - 1] * x[i - 1]
    out = out + (rows * up(here, 0) + down(rows * here, 0))
    return out + (lanes * up(here, 1) + down(lanes * here, 1))


def pre_smooth(b, first, second, w, inverse, scale, outer, inner):
    def start(i):
        first[i] = b[i] * inverse[i] * (1.0 / (scale * THETA))

    for span in outer:
        loop(*span, start, b.shape[1:])

    def sweep(i):
        near = beside(first, w, i)
        second[i] = (1.0 + KEEP + GAIN * (THETA - 1.0)) * first[i] + GAIN * (inverse[i] * near)

    for span in inner:
        loop(*span, sweep, b.shape[1:])


def post_smooth(b, first, second, w, inverse, scale, outer, inner):
    def sweep(i):
        x = first[i]
        near = beside(first, w, i)
        second[i] = x + ((b[i] * (1.0 / scale) + near) * inverse[i] - x) * (1.0 / THETA)

    loop(*outer, sweep, b.shape[1:])

    def last(i):
        x = second[i]
        near = beside(second, w, i)
        step = KEEP * (x - first[i]) + GAIN * ((b[i] * (1.0 / scale) + near) * inverse[i] - x)
        first[i] = x + step

    loop(*inner, last, b.shape[1:])


def residual(b, field, w, total, scale, i):
    return b[i] - scale * (total[i] * field[i] - beside(field, w, i))


def coarser(pairs, halves, matrix):
    planes, rows, lanes = pairs.shape
    halves[...] = pick(pairs.reshape(planes * rows, lanes), matrix).reshape(halves.shape)
    count = rows // 2
    return halves[:, pl.ds(0, count, stride=2), :] + halves[:, pl.ds(1, count, stride=2), :]


def packed(pairs, halves, valid):
    planes, rows, lanes = pairs.shape
    matrix = halving(lanes, halves.shape[2], valid)
    halves[...] = pick(pairs.reshape(planes * rows, lanes), matrix).reshape(halves.shape)
    count = rows // 4
    quarter = [halves[:, pl.ds(r, count, stride=4), :] for r in range(4)]
    odd = pltpu.roll(quarter[2] + quarter[3], halves.shape[2] // 2, 2)
    return (quarter[0] + quarter[1]) + odd


def spread_copies(out, held, sems, *fields):
    for f, rows in enumerate(fields):
        size, count = rows.shape[0], rows.shape[1]
        for i in range(size):
            held[0, pl.ds(f * size * count + i, count, stride=size), :] = rows[i]
    group = held.shape[0]
    for d in range(1, group):
        held[d] = held[0]
    copies = []
    for d in range(out.shape[0] // group):
        there = out.at[d * group : (d + 1) * group]
        copies.append(pltpu.make_async_copy(held, there, sems.at[d]))
    for copy in copies:
        copy.start()
    return copies


def slab_kernel(b, k, first, second, b_out, k_out):
    rows = k.shape[1]
    b_out[...] = b[...]
    k_out[...] = k[...]

    def fill(after, before):
        for r in range(K0):
            after[r] = k[:, rows - K0 + r, :]
            before[r] = k[:, r, :]
        for r in range(B0):
            after[K0 + r] = b[:, rows - B0 + r, :]
            before[K0 + r] = b[:, r, :]

    send("gy", first, second, fill)


def conduct_kernel(k, message, k1, pairs, halves, pairs1, halves1, held, sems):
    def add(j):
        pairs[j] = k[2 * j] + k[2 * j + 1]

    loop(0, pairs.shape[0], add, pairs.shape[1:])
    lanes = k.shape[2]
    k1[...] = coarser(pairs[...], halves, halving(lanes, lanes // 2, lanes))

    def add1(j):
        pairs1[j] = k1[2 * j] + k1[2 * j + 1]

    loop(0, pairs1.shape[0], add1, pairs1.shape[1:])
    wait(spread_copies(message, held, sems, packed(pairs1[...], halves1, k1.shape[2])))


def widen(out, own, low, high, count):
    planes, rows, lanes = own.shape
    size = out.shape[1]
    out[:, 0:rows, :] = own[...]
    out[:, rows:, :] = jnp.zeros((planes, size - rows, lanes), F32)
    below, above = inside("gy", -1), inside("gy", 1)
    for r in range(count):
        out[:, size - count + r, :] = masked(below, low(r))
        out[:, rows + r, :] = masked(above, high(r))


def diamond(count, own):
    return count * own + sum(2 * (count - d) for d in range(1, count + 1))


def put_planes(out, at, ref, planes, own):
    count, size = len(planes), ref.shape[1]
    for p in planes:
        out[at : at + own] = ref[p, 0:own, :]
        at += own
    for d, p in enumerate(planes, 1):
        n = count - d
        if n:
            out[at : at + n] = ref[p, own : own + n, :]
            out[at + n : at + 2 * n] = ref[p, size - n : size, :]
            at += 2 * n
    return at


def get_planes(out, planes, message, at, own, flag):
    count, size = len(planes), out.shape[1]
    halo = at + count * own
    for d, p in enumerate(planes, 1):
        out[p, 0:own, :] = masked(flag, message[at : at + own])
        out[p, own:size, :] = jnp.zeros((size - own, out.shape[2]), F32)
        at += own
        n = count - d
        if n:
            out[p, own : own + n, :] = masked(flag, message[halo : halo + n])
            out[p, size - n : size, :] = masked(flag, message[halo + n : halo + 2 * n])
            halo += 2 * n


def ends(planes, halo, count):
    below = [halo - 1 - d for d in range(count)]
    return below, [halo + planes + d for d in range(count)]


def widen_kernel(b, k, from_first, from_second, k_out, b_out, first, second):
    low, high = sides("gy", from_first, from_second)
    widen(k_out, k, lambda r: low[r], lambda r: high[r], K0)
    widen(b_out, b, lambda r: low[K0 + r], lambda r: high[K0 + r], B0)
    planes, rows = k.shape[0], k.shape[1]

    def fill(after, before):
        at = put_planes(after, 0, k_out, [planes - 1 - d for d in range(K0)], rows)
        put_planes(after, at, b_out, [planes - 1 - d for d in range(B0)], rows)
        at = put_planes(before, 0, k_out, list(range(K0)), rows)
        put_planes(before, at, b_out, list(range(B0)), rows)

    send("gx", first, second, fill)


def join(out, own, low, high, count, halo):
    planes = own.shape[0]
    left, right = inside("gx", -1), inside("gx", 1)
    out[halo : halo + planes] = own[...]
    for r in range(halo):
        below, above = halo - 1 - r, halo + planes + r
        if r < count:
            out[below] = masked(left, low(count - 1 - r))
            out[above] = masked(right, high(r))
        else:
            out[below] = jnp.zeros(out.shape[1:], F32)
            out[above] = jnp.zeros(out.shape[1:], F32)


def fine_inner_kernel(k_own, b_own, wl, ws, wz, total, inverse, b, first, second, pairs, k):
    own, planes = k_own.shape[0], b.shape[0]
    k[K0 : K0 + own] = k_own[...]
    b[K0 : K0 + own] = b_own[...]
    low, high, rows = K0, planes - K0, pairs.shape[1]
    weigh(k, wl, ws, wz, total, inverse, False, True, (low, high - 1))
    pre_smooth(
        b, first, second, (wl, ws, wz), inverse, 1.0, [(low + 1, high - 1)], [(low + 2, high - 2)]
    )
    fine_restrict(b, second, (wl, ws, wz), total, pairs, (2, own // 2 - 2))


def fine_restrict(b, field, w, total, pairs, span):
    rows = pairs.shape[1]

    def restrict(j):
        i = 2 * j + K0
        both = residual(b, field, w, total, 1.0, i) + residual(b, field, w, total, 1.0, i + 1)
        pairs[j] = both[0:rows]

    loop(*span, restrict, (2 * b.shape[1], b.shape[2]))


def put_rows(out, at, parts):
    lanes = out.shape[1]
    for part in parts:
        rows = part.shape[0]
        for h in range(part.shape[1] // lanes):
            out[at : at + rows] = part[:, h * lanes : (h + 1) * lanes]
            at += rows
    return at


def fine_outer_kernel(
    k_own, from_first, from_second, k1,
    wl_in, ws_in, wz_in, total_in, inverse_in, b_in, first_in, second_in, pairs_in,
    wl_out, ws_out, wz_out, total_out, b_out, s_out, b1_out, first_out, second_out,
    wl, ws, wz, total, inverse, b, first, second, pairs, k, halves,
):
    low, high = sides("gx", from_first, from_second)
    planes, rows, lanes = b.shape[0], s_out.shape[1], b.shape[2]
    own, end = planes - 2 * K0, planes - K0
    for mine, inner in (
        (wl, wl_in), (ws, ws_in), (wz, wz_in), (total, total_in), (inverse, inverse_in), (b, b_in),
        (first, first_in), (second, second_in),
    ):
        mine[K0 : K0 + 5] = inner[K0 : K0 + 5]
        mine[end - 5 : end] = inner[end - 5 : end]
    left, right = inside("gx", -1), inside("gx", 1)
    for ref, count, at in ((k, K0, 0), (b, B0, diamond(K0, rows))):
        below, above = ends(own, K0, count)
        get_planes(ref, below, low, at, rows, left)
        get_planes(ref, above, high, at, rows, right)
    for r in range(2):
        k[K0 + r] = k_own[r]
        k[end - 2 + r] = k_own[own - 2 + r]
    w = (wl, ws, wz)
    weigh(k, wl, ws, wz, total, inverse, False, True, (0, K0 + 1))
    weigh(k, wl, ws, wz, total, inverse, False, True, (end - 1, planes - 1), wl[end - 2])
    pre_smooth(
        b, first, second, w, inverse, 1.0,
        [(1, K0 + 1), (end - 1, planes - 1)], [(2, K0 + 2), (end - 2, planes - 2)],
    )
    pairs[2 : own // 2 - 2] = pairs_in[2 : own // 2 - 2]
    fine_restrict(b, second, w, total, pairs, (0, 2))
    fine_restrict(b, second, w, total, pairs, (own // 2 - 2, own // 2))
    b1_out[...] = coarser(pairs[...], halves, halving(lanes, lanes // 2, lanes))
    s_out[2 : own - 2] = second_in[K0 + 2 : end - 2, 0:rows, :]
    for at in (0, own - 2):
        s_out[at : at + 2] = second[K0 + at : K0 + at + 2, 0:rows, :]
    for out, mine in ((wl_out, wl), (ws_out, ws), (wz_out, wz), (total_out, total), (b_out, b)):
        out[0 : K0 + 1] = mine[0 : K0 + 1]
        out[K0 + 1 :] = mine[end - 1 :]
    count = b1_out.shape[1]

    def fill(after, before):
        for out, k_from, b_from in ((after, count - K1, count - B1), (before, 0, 0)):
            for r in range(K1):
                out[r] = k1[:, k_from + r, :]
            for r in range(B1):
                out[K1 + r] = b1_out[:, b_from + r, :]

    send("gy", first_out, second_out, fill)


def field_slab_kernel(s, first, second):
    rows = s.shape[1]

    def fill(after, before):
        put_rows(after, 0, [s[:, rows - S0 + r, :] for r in range(S0)])
        put_rows(before, 0, [s[:, r, :] for r in range(S0)])

    send("gy", first, second, fill)


def stash_kernel(*refs):
    inner, outer, (stash, sems) = refs[:5], refs[5:10], refs[10:]
    planes, edge = inner[0].shape[0], K0 + 1
    copies = []
    for i in range(5):
        for j, (source, first, at, count) in enumerate((
            (inner[i], edge, edge, planes - 2 * edge),
            (outer[i], 0, 0, edge),
            (outer[i], edge, planes - edge, edge),
        )):
            copies.append(
                pltpu.make_async_copy(
                    source.at[first : first + count],
                    stash.at[i * planes + at : i * planes + at + count],
                    sems.at[3 * i + j],
                )
            )
    for copy in copies:
        copy.start()
    wait(copies)


def widen_middle_kernel(
    k1, b1, from_first, from_second, k_out, b_out, first, second
):
    low, high = sides("gy", from_first, from_second)
    widen(k_out, k1, lambda r: low[r], lambda r: high[r], K1)
    widen(b_out, b1, lambda r: low[K1 + r], lambda r: high[K1 + r], B1)
    planes = k1.shape[0]

    def fill(after, before):
        after[0:K1] = k_out[planes - K1 :]
        after[K1:] = b_out[planes - B1 :]
        before[0:K1] = k_out[0:K1]
        before[K1:] = b_out[0:B1]

    send("gx", first, second, fill)


def middle_down_kernel(
    k_own, b_own, from_first, from_second, _s_first, _s_second, _stash,
    message, k, b, s_out,
    wl, ws, wz, inverse, total, first, second, pairs, halves, held, sems,
):
    scale = 0.25
    low, high = sides("gx", from_first, from_second)
    join(k, k_own, lambda r: low[r], lambda r: high[r], K1, K1)
    join(b, b_own, lambda r: low[K1 + r], lambda r: high[K1 + r], B1, K1)
    w = (wl, ws, wz)
    weigh(k, wl, ws, wz, total, inverse, False, True)
    planes, lanes = b.shape[0], b.shape[2]
    own, rows = planes - 2 * K1, s_out.shape[1]
    pre_smooth(b, first, second, w, inverse, scale, [(1, planes - 1)], [(2, planes - 2)])

    def restrict(j):
        i = 2 * j + K1
        both = residual(b, second, w, total, scale, i) + residual(b, second, w, total, scale, i + 1)
        pairs[j] = both[0:rows]

    loop(0, own // 2, restrict, (2 * b.shape[1], b.shape[2]))
    copies = spread_copies(message, held, sems, packed(pairs[...], halves, lanes))
    s_out[...] = second[K1 : K1 + own, 0:rows, :]
    wait(copies)


def split_lanes(ref, first, rows):
    def get(r):
        at = first + 2 * r * rows
        return jnp.concatenate([ref[at : at + rows], ref[at + rows : at + 2 * rows]], axis=1)

    return get


def from_row(ref, first, rows):
    def get(r):
        return ref[first + r * rows : first + (r + 1) * rows]

    return get


def field_planes_kernel(s, s1, from_first, from_second, s_out, first, second):
    low, high = sides("gy", from_first, from_second)
    fine, own = s.shape[0], s1.shape[0]
    widen(s_out, s, split_lanes(low, 0, fine), split_lanes(high, 0, fine), S0)

    def fill(after, before):
        for out, from0, from1 in ((after, fine - S0, own - S1), (before, 0, 0)):
            at = put_rows(out, 0, [s_out[from0 + r] for r in range(S0)])
            put_rows(out, at, [s1[from1 + r] for r in range(S1)])

    send("gx", first, second, fill)


def field_rows_kernel(
    s, s1, from_first, from_second, _weights, s_out, s1_out, first, second
):
    low, high = sides("gx", from_first, from_second)
    rows, rows1 = s.shape[1], s1.shape[1]
    join(s_out, s, split_lanes(low, 0, rows), split_lanes(high, 0, rows), S0, S0)
    at = 2 * S0 * rows
    join(s1_out, s1, from_row(low, at, rows1), from_row(high, at, rows1), S1, S1)

    def fill(after, before):
        put_rows(after, 0, [s1_out[:, rows1 - S1 + r, :] for r in range(S1)])
        put_rows(before, 0, [s1_out[:, r, :] for r in range(S1)])

    send("gy", first, second, fill)


def unpack(received, out, first, block_x, block_y, across, along):
    clear_ends(out)

    def place(column):
        for row in range(across):
            for j in range(block_y // 2):
                piece = received[row * along + column, pl.ds(first + j * block_x, block_x), :]
                at = 1 + column * (block_y // 2) + j
                out[at, row * block_x : (row + 1) * block_x, :] = piece

    loop(0, along, place, (out.shape[1], block_y // 2 * out.shape[2]))


def clear_ends(ref):
    for end in (0, ref.shape[0] - 1):
        ref[end] = jnp.zeros(ref.shape[1:], F32)


def across_up(x, after):
    half = x.shape[1] // 2
    return pltpu.roll(jnp.where(iota(x.shape, 1) < half, after, x), half, 1)


def across_down(x, before):
    half = x.shape[1] // 2
    return pltpu.roll(jnp.where(iota(x.shape, 1) < half, x, before), half, 1)


def weigh_packed(k, wl, wl_low, ws, wz, total, inverse):
    planes = k.shape[0]

    def body(i, before):
        here = k[i]
        lead = face(here, across_up(here, k[i + 1]))
        lead_low = across_down(lead, before)
        rows, row_sum = sided(here, 0, here.shape[0])
        lanes, lane_sum = sided(here, 1, here.shape[1] // 2)
        wl[i] = lead
        wl_low[i] = lead_low
        ws[i] = rows
        wz[i] = lanes
        whole = (lead_low + lead) + (row_sum + lane_sum)
        there = here > 0.0
        total[i] = jnp.where(there, whole, 0.0)
        inverse[i] = jnp.where(there, 1.0 / whole, 0.0)
        return lead

    carried(0, planes - 1, body, jnp.zeros(k.shape[1:], F32), k.shape[1:])


def beside_packed(x, w, i):
    wl, wl_low, ws, wz = w
    here = x[i]
    rows, lanes = ws[i], wz[i]
    out = wl[i] * across_up(here, x[i + 1]) + wl_low[i] * across_down(here, x[i - 1])
    out = out + (rows * up(here, 0) + down(rows * here, 0))
    return out + (lanes * up(here, 1) + down(lanes * here, 1))


def coarse_pre(b, w, inverse, first, second, scale):
    ends = [(1, b.shape[0] - 1)]
    clear_ends(first)
    clear_ends(second)
    pre_smooth(b, first, second, w, inverse, scale, ends, ends)


def widened(x, matrix):
    planes, rows, lanes = x.shape
    return pick(x.reshape(planes * rows, lanes), matrix).reshape(planes, rows, matrix.shape[1])


def twice(out, x):
    out[:, pl.ds(0, x.shape[1], stride=2), :] = x
    out[:, pl.ds(1, x.shape[1], stride=2), :] = x


def bottom(k, b, scale):
    planes, rows, lanes = k.shape
    none = jnp.zeros((1, rows, lanes), F32)

    def after(v):
        return jnp.concatenate([v[1:], none], axis=0)

    def before(v):
        return jnp.concatenate([none, v[:-1]], axis=0)

    lead = face(k, after(k))
    lead_low = jnp.concatenate([k[:1], lead[:-1]], axis=0)
    row = iota(k.shape, 1)
    row_w = face(k, jnp.where(row == rows - 1, 0.0, up(k, 1)))
    row_low = jnp.where(row == 0, k, down(row_w, 1))
    lane_w = face(k, up(k, 2))
    lane_low = down(lane_w, 2)
    whole = ((lead + lead_low) + (row_w + row_low)) + (lane_w + lane_low)
    inverse = jnp.where(k > 0.0, 1.0 / whole, 0.0)
    source = b * inverse * (1.0 / scale)
    lead_i, lead_low_i = lead * inverse, lead_low * inverse
    row_i = jnp.where(row == rows - 1, 0.0, row_w) * inverse
    row_low_i = jnp.where(row == 0, 0.0, row_low) * inverse
    lane_i, lane_low_i = lane_w * inverse, lane_low * inverse
    sigma = BOTTOM_THETA / BOTTOM_DELTA
    rho = 1.0 / sigma
    step = source * (1.0 / BOTTOM_THETA)
    x = step
    for _ in range(BOTTOM - 1):
        following = 1.0 / (2.0 * sigma - rho)
        near = (lead_i * after(x) + lead_low_i * before(x)) + (
            row_i * up(x, 1) + row_low_i * down(x, 1)
        )
        near = near + (lane_i * up(x, 2) + lane_low_i * down(x, 2))
        step = (following * rho) * step + (2.0 * following / BOTTOM_DELTA) * (source - x + near)
        x = x + step
        rho = following
    return x


def mean_matrix(lanes, valid):
    row, col = iota((lanes, lanes), 0), iota((lanes, lanes), 1)
    return jnp.where(lax.rem(row, valid) // 2 == col, 0.125, 0.0).astype(BF16)


def coarse_weights_kernel(
    valid, received, wl2, ws2, wz2, total2, level3, k4,
    low2, inverse2, k2, halves2, wl3, ws3, wz3, total3, inverse3, k3, pairs3, halves3,
):
    planes, rows, lanes = k2.shape
    across, along = lax.axis_size("gx"), lax.axis_size("gy")
    unpack(received, k2, 0, rows // across, 2 * (planes - 2) // along, across, along)
    own3 = planes - 2
    clear_ends(k3)
    k3[1 : own3 + 1] = coarser(k2[1 : own3 + 1], halves2, mean_matrix(lanes, valid))

    def add3(j):
        pairs3[j] = k3[2 * j + 1] + k3[2 * j + 2]

    loop(0, pairs3.shape[0], add3, pairs3.shape[1:])
    k4[...] = coarser(pairs3[...], halves3, halving(lanes, lanes, valid // 2))
    weigh_packed(k2, wl2, low2, ws2, wz2, total2, inverse2)
    weigh(k3, wl3, ws3, wz3, total3, inverse3, True, False)

    def pack(i):
        lane = iota(level3.shape[1:], 1)
        parts = [jnp.where(lane < valid // 2, ref[i], 0.0) for ref in (wl3, ws3, wz3, total3)]
        level3[i] = sum(
            (pltpu.roll(part, f * (valid // 2), 1) for f, part in enumerate(parts) if f), parts[0]
        )

    loop(0, planes - 1, pack, level3.shape[1:])


def invert(total):
    return jnp.where(total > 0.0, 1.0 / total, 0.0)


def coarse_kernel(
    valid, received, wl2, ws2, wz2, total2, level3, k4, stash,
    region, wl, ws, wz, total, b,
    low2, inverse2, b2, first2, second2, pairs2, halves2,
    wl3, ws3, wz3, total3, inverse3, b3, first3, second3, pairs3, halves3, sems,
):
    copies = fetch((wl, ws, wz, total, b), stash, sems)
    planes, rows, lanes = b2.shape
    across, along = lax.axis_size("gx"), lax.axis_size("gy")
    block_x, block_y = rows // across, 2 * (planes - 2) // along
    own3, half = planes - 2, valid // 2
    unpack(received, b2, 0, block_x, block_y, across, along)
    row, col = iota((lanes, lanes), 0), iota((lanes, lanes), 1)
    matrix2, matrix3 = mean_matrix(lanes, valid), halving(lanes, lanes, half)

    def complete(i):
        low2[i] = across_down(wl2[i], wl2[i - 1])
        inverse2[i] = invert(total2[i])

    def unpack3(i):
        lane = iota(level3.shape[1:], 1)
        for f, ref in enumerate((wl3, ws3, wz3, total3)):
            part = level3[i]
            if f:
                part = pltpu.roll(part, lanes - f * half, 1)
            ref[i] = jnp.where(lane < half, part, 0.0)
        inverse3[i] = invert(total3[i])

    loop(1, own3 + 1, complete, b2.shape[1:])
    loop(0, own3 + 1, unpack3, level3.shape[1:])
    w2, w3 = (wl2, low2, ws2, wz2), (wl3, ws3, wz3)
    scale2, scale3 = 0.25**2, 0.25**3
    coarse_pre(b2, w2, inverse2, first2, second2, scale2)

    def rest2(j):
        pairs2[j] = residual(b2, second2, w2, total2, scale2, j + 1)

    loop(0, own3, rest2, pairs2.shape[1:])
    clear_ends(b3)
    b3[1 : own3 + 1] = coarser(pairs2[...], halves2, matrix2)
    coarse_pre(b3, w3, inverse3, first3, second3, scale3)

    def rest3(j):
        i = 2 * j + 1
        pairs3[j] = residual(b3, second3, w3, total3, scale3, i) + residual(
            b3, second3, w3, total3, scale3, i + 1
        )

    loop(0, pairs3.shape[0], rest3, pairs3.shape[1:])
    x4 = bottom(k4[...], coarser(pairs3[...], halves3, matrix3), 0.25**4)
    twice(pairs3, widened(x4, doubling(lanes, lanes, half // 2)))

    def add_up3(j):
        for side in range(2):
            i = 2 * j + 1 + side
            first3[i] = second3[i] + pairs3[j]

    loop(0, pairs3.shape[0], add_up3, pairs3.shape[1:])
    ends = (1, own3 + 1)
    post_smooth(b3, first3, second3, w3, inverse3, scale3, ends, ends)
    matrix = jnp.where((lax.rem(col, valid) // 2 == row) & (row < half), 1.0, 0.0).astype(BF16)
    twice(pairs2, widened(first3[1 : own3 + 1], matrix))

    def add_up2(i):
        first2[i] = second2[i] + pairs2[i - 1]

    loop(1, own3 + 1, add_up2, pairs2.shape[1:])
    post_smooth(b2, first2, second2, w2, inverse2, scale2, ends, ends)
    column, place = lax.axis_index("gy"), lax.axis_index("gx")
    for q in range(region.shape[0]):
        plane = column * (block_y // 2) + q - EDGE // 2
        for side in range(3):
            block = place + side - 1
            there = (plane >= 0) & (plane < planes - 2) & (block >= 0) & (block < across)
            start = pl.multiple_of(jnp.clip(block, 0, across - 1) * block_x, block_x)
            value = first2[1 + jnp.clip(plane, 0, planes - 3), pl.ds(start, block_x), :]
            region[q, side * block_x : (side + 1) * block_x, :] = masked(there, value)
    wait(copies)


def fine_up_kernel(
    region, k1, b1, s1_own, wl, ws, wz, total, b, s_own, from_first, from_second,
    field_out, residual_out,
    wl1, ws1, wz1, total1, inverse1, inverse, first1, second1, grown, s, second, tall, thick, rest,
    out_sems,
):
    planes1, rows1, lanes1 = b1.shape
    planes, rows, lanes = b.shape
    w1, w = (wl1, ws1, wz1), (wl, ws, wz)
    weigh(k1, wl1, ws1, wz1, total1, inverse1, False, True)
    low, high = sides("gy", from_first, from_second)
    widen(first1, s1_own, from_row(low, 0, planes1), from_row(high, 0, planes1), S1)
    count_y, block_x = region.shape[0], region.shape[1] // 3
    expanded = widened(region[...], doubling(lanes1, 2 * lanes1, lanes1))
    for q in range(block_x + 2 * EDGE):
        line = expanded[:, block_x - EDGE + q, :]
        line = jnp.concatenate([line[EDGE // 2 :], line[: EDGE // 2]], axis=0)
        for r in range(4):
            half = line[:, (r // 2) * lanes1 : (r // 2 + 1) * lanes1]
            grown[q, pl.ds(r, count_y, stride=4), :] = half

    def add1(q):
        for side in range(2):
            first1[2 * q + side] = first1[2 * q + side] + grown[q]

    loop(0, block_x + 2 * EDGE, add1, b1.shape[1:])
    post_smooth(
        b1, first1, second1, w1, inverse1, 0.25, (1, planes1 - 1), (2, planes1 - 2)
    )
    begin, count = S1 - EDGE, planes1 - 2 * S1 + 2 * EDGE
    own1 = rows1 - 2 * S1
    edge = 2 * EDGE
    for half, at, where in ((own1 + EDGE, 0, 0), (EDGE, rows1 - EDGE, 2 * (own1 + EDGE))):
        part = first1[begin : begin + count, at : at + half, :]
        tall[:, pl.ds(where, half, stride=2), :] = part
        tall[:, pl.ds(where + 1, half, stride=2), :] = part
    matrix = doubling(lanes1, lanes, lanes1)
    thick[...] = pick(tall[...].reshape(count * rows, lanes1), matrix).reshape(thick.shape)
    s[0] = s_own[0] + thick[0]
    s[planes - 1] = s_own[planes - 1] + thick[count - 1]

    def add(q):
        for side in range(2):
            i = 2 * q + side - 1
            s[i] = s_own[i] + thick[q]

    loop(1, count - 1, add, b.shape[1:])

    def complete(i):
        inverse[i] = invert(total[i])

    loop(1, planes - 1, complete, b.shape[1:])
    post_smooth(b, s, second, w, inverse, 1.0, (1, planes - 1), (2, planes - 2))
    own, own_rows = field_out.shape[0], field_out.shape[1]
    mine = s.at[K0 : K0 + own, 0:own_rows]
    copies = [pltpu.make_async_copy(mine, field_out, out_sems.at[0])]
    copies[0].start()

    def finish(j):
        rest[j] = residual(b, s, w, total, 1.0, j + K0)[0:own_rows]

    parts = out_sems.shape[0] - 1
    for part in range(parts):
        begin, end = own * part // parts, own * (part + 1) // parts
        loop(begin, end, finish, b.shape[1:])
        copy = pltpu.make_async_copy(
            rest.at[begin:end], residual_out.at[begin:end], out_sems.at[1 + part]
        )
        copy.start()
        copies.append(copy)
    wait(copies)


def call(kernel, outs, scratch=(), held=0, kept=(), sems=(), cost=0, registers=48):
    def body(*refs):
        REGISTERS[0] = registers
        kernel(*refs)

    def run(*operands):
        inputs = [o.shape for i, o in enumerate(operands) if i not in kept]
        shapes = inputs + list(outs[held:]) + list(scratch)
        words = sum(math.prod(s[:-2]) * eight(s[-2]) * s[-1] for s in shapes)
        places = [pltpu.HBM if i in kept else pltpu.VMEM for i in range(len(operands))]
        out_places = [pltpu.HBM if i < held else pltpu.VMEM for i in range(len(outs))]
        return pl.pallas_call(
            body,
            out_shape=[jax.ShapeDtypeStruct(shape, F32) for shape in outs],
            in_specs=[pl.BlockSpec(memory_space=place) for place in places],
            out_specs=[pl.BlockSpec(memory_space=place) for place in out_places],
            scratch_shapes=[pltpu.VMEM(shape, F32) for shape in scratch]
            + [pltpu.SemaphoreType.DMA((n,)) for n in sems],
            cost_estimate=pl.CostEstimate(flops=cost, bytes_accessed=cost, transcendentals=0) if cost else None,
            compiler_params=pltpu.CompilerParams(vmem_limit_bytes=4 * words + SPARE),
        )(*operands)

    return run


def eight(rows):
    return -(-rows // 8) * 8


def per_device(right_side, coefficient):
    bx, by, nz = right_side.shape
    across, along = lax.axis_size("gx"), lax.axis_size("gy")
    devices = across * along
    hx, hy, hz = bx // 2, by // 2, nz // 2
    qx, qy = hx // 2, hy // 2
    both = ("gx", "gy")
    tall, tall1 = eight(by + 2 * K0), eight(hy + 2 * K1)
    pieces = (devices, qx * qy // 2, hz)

    slab = (K0 + B0, bx, nz)
    first, second, right_side, coefficient = call(
        slab_kernel, [slab, slab, (bx, by, nz), (bx, by, nz)]
    )(right_side, coefficient)
    from_first, from_second = swap(first, second, "gy")
    group = 4
    message, k1 = call(
        conduct_kernel,
        [pieces, (hx, hy, hz)],
        [(hx, by, nz), (hx, by, hz), (qx, hy, hz), (qx, hy, hz), (group, *pieces[1:])],
        held=1,
        sems=(devices // group,),
    )(coefficient)

    plane = (bx, tall, nz)
    slab = (diamond(K0, by) + diamond(B0, by), nz)
    k_own, b_own, first, second = call(widen_kernel, [plane, plane, slab, slab], cost=LONG)(
        right_side, coefficient, from_first, from_second
    )
    from_first, from_second = swap(first, second, "gx")

    k2 = lax.all_to_all(message, both, 0, 0, tiled=True)

    block = (bx + 2 * K0, tall, nz)
    inner = call(fine_inner_kernel, [block] * 8 + [(hx, by, nz)], [block], registers=72)(
        k_own, b_own
    )
    slab = (K1 + B1, hx, hz)
    edges = (2 * K0 + 2, tall, nz)
    field_slab = (2 * S0 * bx, hz)
    *outer, s, b1, first, second = call(
        fine_outer_kernel,
        [edges] * 5 + [(bx, by, nz), (hx, hy, hz), slab, slab],
        [block] * 8 + [(hx, by, nz), block, (hx, by, hz)],
    )(k_own, from_first, from_second, k1, *inner)
    planes = 5 * block[0] + VMEM_BYTES // (4 * tall * nz)
    (stash,) = call(stash_kernel, [(planes, tall, nz)], held=1, sems=(15,))(
        *inner[:4], inner[5], *outer
    )
    from_first, from_second = swap(first, second, "gy")
    s_first, s_second = swap(*call(field_slab_kernel, [field_slab, field_slab])(s), "gy")
    slab = (K1 + B1, tall1, hz)
    k1_own, b1_own, first, second = call(
        widen_middle_kernel, [(hx, tall1, hz), (hx, tall1, hz), slab, slab]
    )(k1, b1, from_first, from_second)
    from_first, from_second = swap(first, second, "gx")

    block1 = (hx + 2 * K1, tall1, hz)
    message, k1, b1, s1 = call(
        middle_down_kernel,
        [pieces] + [block1] * 2 + [(hx, hy, hz)],
        [block1] * 7 + [(qx, hy, hz), (qx, hy, hz), (group, *pieces[1:])],
        held=1,
        kept=(6,),
        sems=(devices // group,),
    )(k1_own, b1_own, from_first, from_second, s_first, s_second, stash)
    received = lax.all_to_all(message, both, 0, 0, tiled=True)

    x2, y2 = across * qx, along * qy
    level2, level3 = (y2 // 2 + 2, x2, hz), (y2 // 2 + 2, x2 // 2, hz)
    half2, half3 = (y2 // 2, x2, hz), (y2 // 4, x2 // 2, hz)
    valid = nz // 4
    coarse = call(
        partial(coarse_weights_kernel, valid),
        [level2] * 4 + [level3, (y2 // 4, x2 // 4, hz)],
        [level2] * 3 + [half2] + [level3] * 6 + [half3] * 2,
        registers=48,
    )(k2)
    slab = (2 * S0 * tall + S1 * hy, hz)
    s_rows, first, second = call(field_planes_kernel, [plane, slab, slab])(
        s, s1, s_first, s_second
    )
    from_first, from_second = swap(first, second, "gx")
    slab = (S1 * block1[0], hz)
    s_own, s1_own, first, second = call(
        field_rows_kernel, [block, (block1[0], hy, hz), slab, slab]
    )(s_rows, s1, from_first, from_second, coarse[-1])
    from_first, from_second = swap(first, second, "gy")

    region, *weights = call(
        partial(coarse_kernel, valid),
        [(qy // 2 + EDGE, 3 * qx, hz)] + [block] * 5,
        [level2] * 5 + [half2] * 2 + [level3] * 8 + [half3] * 2,
        kept=(7,),
        sems=(5,),
        registers=40,
    )(received, *coarse, stash)

    count = hx + 2 * EDGE
    field, rest = call(
        fine_up_kernel,
        [(bx, by, nz)] * 2,
        [block1] * 5 + [block, block1, block1, (qx + 2 * EDGE, tall1, hz)]
        + [block, block, (count, tall, hz), (count, tall, nz), (bx, by, nz)],
        held=2,
        sems=(5,),
        registers=96,
    )(region, k1, b1, s1_own, *weights, s_own, from_first, from_second)
    return field, rest


def solution(mesh):
    in_specs = (P("gx", "gy", None), P("gx", "gy", None))
    out_specs = (P("gx", "gy", None), P("gx", "gy", None))
    return jax.shard_map(
        per_device, mesh=mesh, in_specs=in_specs, out_specs=out_specs, check_vma=False
    )
```

```python
import math
from functools import partial

import jax
import jax.numpy as jnp
from jax import lax
from jax.experimental import pallas as pl
from jax.experimental.pallas import tpu as pltpu
from jax.sharding import PartitionSpec as P

F32 = jnp.float32
BF16 = jnp.bfloat16

THETA = 1.25
DELTA = 0.75
SIGMA = THETA / DELTA
RHO0 = 1.0 / SIGMA
RHO1 = 1.0 / (2.0 * SIGMA - RHO0)
KEEP = RHO1 * RHO0
GAIN = 2.0 * RHO1 / DELTA
BOTTOM = 8
BOTTOM_THETA = (2.0 + 0.05) / 2.0
BOTTOM_DELTA = (2.0 - 0.05) / 2.0

K0, B0, S0 = 3, 2, 3
K1, B1, S1 = 4, 3, 4
EDGE = 2
REGISTERS = [48]
SPARE = 4 * 1024 * 1024
VMEM_BYTES = 64 * 1024 * 1024
LONG = 10**12


def swap(first, second, axis):
    axes = ("gx", "gy")
    sizes = [lax.axis_size(name) for name in axes]
    along = axes.index(axis)
    size, other = sizes[along], sizes[1 - along]

    def place(i, j):
        return i * sizes[1] + j if along == 0 else j * sizes[1] + i

    def pairs(begin):
        found = []
        for j in range(other):
            for i in range(begin, size - 1, 2):
                found += [(place(i, j), place(i + 1, j)), (place(i + 1, j), place(i, j))]
        met = {source for source, _ in found}
        for i in range(size):
            for j in range(other):
                beside = j + 1 - 2 * (j % 2)
                target = place(i, beside) if beside < other else place(i, j)
                if place(i, j) not in met:
                    found.append((place(i, j), target))
        return found

    return lax.ppermute(first, axes, pairs(0)), lax.ppermute(second, axes, pairs(1))


def is_even(axis):
    return lax.rem(lax.axis_index(axis), 2) == 0


class Either:
    def __init__(self, flag, one, two):
        self.flag, self.one, self.two, self.shape = flag, one, two, one.shape

    def __getitem__(self, index):
        return jnp.where(self.flag, self.one[index], self.two[index])


def sides(axis, first, second):
    even = is_even(axis)
    return Either(even, second, first), Either(even, first, second)


def send(axis, first, second, fill):
    even = is_even(axis)

    @pl.when(even)
    def _():
        fill(first, second)

    @pl.when(jnp.logical_not(even))
    def _():
        fill(second, first)


def inside(axis, side):
    index = lax.axis_index(axis)
    if side < 0:
        return index > 0
    return index < lax.axis_size(axis) - 1


def masked(flag, value):
    return jnp.where(flag, value, jnp.zeros_like(value))


def iota(shape, dim):
    return lax.broadcasted_iota(jnp.int32, shape, dim)


def pick(x, matrix):
    high = x.astype(BF16)
    low = (x - high.astype(F32)).astype(BF16)
    return jnp.dot(high, matrix, preferred_element_type=F32) + jnp.dot(
        low, matrix, preferred_element_type=F32
    )


def halving(fine, coarse, valid):
    row, col = iota((fine, coarse), 0), iota((fine, coarse), 1)
    return jnp.where((row // 2 == col) & (row < valid), 0.125, 0.0).astype(BF16)


def doubling(coarse, fine, valid):
    row, col = iota((coarse, fine), 0), iota((coarse, fine), 1)
    return jnp.where((row == col // 2) & (row < valid), 1.0, 0.0).astype(BF16)


def fetch(refs, stash, sems):
    copies = []
    for i, ref in enumerate(refs):
        planes = ref.shape[0]
        there = stash.at[i * planes : (i + 1) * planes]
        copies.append(pltpu.make_async_copy(there, ref, sems.at[i]))
    for copy in copies:
        copy.start()
    return copies


def wait(copies):
    for copy in copies:
        copy.wait()


def face(a, b):
    product, total = a * b, a + b
    return jnp.where(product > 0.0, 2.0 * product / total, total)


def up(x, axis):
    return pltpu.roll(x, x.shape[axis] - 1, axis)


def down(x, axis):
    return pltpu.roll(x, 1, axis)


def sided(k, axis, edge):
    after = up(k, axis)
    if edge is None:
        w = face(k, after)
        return w, w + down(w, axis)
    place = iota(k.shape, axis)
    if edge < k.shape[axis]:
        place = lax.rem(place, edge)
    last = place == edge - 1
    w = face(k, jnp.where(last, 0.0, after))
    return jnp.where(last, 0.0, w), w + jnp.where(place == 0, k, down(w, axis))


def blocks_of(plane, count):
    most = max(1, REGISTERS[0] // max(1, plane[0] * plane[1] // 1024))
    best = None
    for blocks in range(max(1, count // (2 * most)), count + 1):
        steps = count // blocks
        cost = (count - blocks * steps) * 0.5 + abs(steps - most)
        if best is None or cost < best[0]:
            best = (cost, blocks, steps)
    return best[1:]


def carried(low, high, body, carry, plane):
    blocks, steps = blocks_of(plane, high - low)
    end = low + blocks * steps
    if blocks == 1:
        end = low
        steps = high - low
    elif blocks * steps:
        carry = lax.fori_loop(low, end, body, carry, unroll=steps)
    for i in range(end, high):
        carry = body(i, carry)
    return carry


def loop(low, high, body, plane):
    def step(i, carry):
        body(i)
        return carry

    carried(low, high, step, 0, plane)


def weigh(k, wl, ws, wz, total, inverse, row_edge, lane_edge, span=None, before=None):
    plane = k.shape[1:]
    low, high = span or (0, k.shape[0] - 1)

    def body(i, before):
        here = k[i]
        lead = face(here, k[i + 1])
        rows, row_sum = sided(here, 0, here.shape[0] if row_edge else None)
        lanes, lane_sum = sided(here, 1, here.shape[1] if lane_edge else None)
        wl[i] = lead
        ws[i] = rows
        wz[i] = lanes
        whole = (before + lead) + (row_sum + lane_sum)
        there = here > 0.0
        total[i] = jnp.where(there, whole, 0.0)
        inverse[i] = jnp.where(there, 1.0 / whole, 0.0)
        return lead

    before = jnp.zeros(plane, F32) if before is None else before
    carried(low, high, body, before, plane)


def beside(x, w, i):
    if len(w) == 4:
        return beside_packed(x, w, i)
    wl, ws, wz = w
    here = x[i]
    rows, lanes = ws[i], wz[i]
    out = wl[i] * x[i + 1] + wl[i - 1] * x[i - 1]
    out = out + (rows * up(here, 0) + down(rows * here, 0))
    return out + (lanes * up(here, 1) + down(lanes * here, 1))


def pre_smooth(b, first, second, w, inverse, scale, outer, inner):
    def start(i):
        first[i] = b[i] * inverse[i] * (1.0 / (scale * THETA))

    for span in outer:
        loop(*span, start, b.shape[1:])

    def sweep(i):
        near = beside(first, w, i)
        second[i] = (1.0 + KEEP + GAIN * (THETA - 1.0)) * first[i] + GAIN * (inverse[i] * near)

    for span in inner:
        loop(*span, sweep, b.shape[1:])


def post_smooth(b, first, second, w, inverse, scale, outer, inner, total=None):
    def sweep(i):
        x = first[i]
        near = beside(first, w, i)
        if total is not None:
            inverse[i] = invert(total[i])
        second[i] = x + ((b[i] * (1.0 / scale) + near) * inverse[i] - x) * (1.0 / THETA)

    loop(*outer, sweep, b.shape[1:])

    def last(i):
        x = second[i]
        near = beside(second, w, i)
        step = KEEP * (x - first[i]) + GAIN * ((b[i] * (1.0 / scale) + near) * inverse[i] - x)
        first[i] = x + step

    loop(*inner, last, b.shape[1:])


def residual(b, field, w, total, scale, i):
    return b[i] - scale * (total[i] * field[i] - beside(field, w, i))


def coarser(pairs, halves, matrix):
    planes, rows, lanes = pairs.shape
    halves[...] = pick(pairs.reshape(planes * rows, lanes), matrix).reshape(halves.shape)
    count = rows // 2
    return halves[:, pl.ds(0, count, stride=2), :] + halves[:, pl.ds(1, count, stride=2), :]


def packed(pairs, halves, valid):
    planes, rows, lanes = pairs.shape
    matrix = halving(lanes, halves.shape[2], valid)
    halves[...] = pick(pairs.reshape(planes * rows, lanes), matrix).reshape(halves.shape)
    count = rows // 4
    quarter = [halves[:, pl.ds(r, count, stride=4), :] for r in range(4)]
    odd = pltpu.roll(quarter[2] + quarter[3], halves.shape[2] // 2, 2)
    return (quarter[0] + quarter[1]) + odd


def spread_copies(out, held, sems, *fields):
    for f, rows in enumerate(fields):
        size, count = rows.shape[0], rows.shape[1]
        for i in range(size):
            held[0, pl.ds(f * size * count + i, count, stride=size), :] = rows[i]
    group = held.shape[0]
    for d in range(1, group):
        held[d] = held[0]
    copies = []
    for d in range(out.shape[0] // group):
        there = out.at[d * group : (d + 1) * group]
        copies.append(pltpu.make_async_copy(held, there, sems.at[d]))
    for copy in copies:
        copy.start()
    return copies


def slab_kernel(b, k, first, second, b_out, k_out):
    rows = k.shape[1]
    b_out[...] = b[...]
    k_out[...] = k[...]

    def fill(after, before):
        for r in range(K0):
            after[r] = k[:, rows - K0 + r, :]
            before[r] = k[:, r, :]
        for r in range(B0):
            after[K0 + r] = b[:, rows - B0 + r, :]
            before[K0 + r] = b[:, r, :]

    send("gy", first, second, fill)


def conduct_kernel(k, message, k1, pairs, halves, pairs1, halves1, held, sems):
    def add(j):
        pairs[j] = k[2 * j] + k[2 * j + 1]

    loop(0, pairs.shape[0], add, pairs.shape[1:])
    lanes = k.shape[2]
    k1[...] = coarser(pairs[...], halves, halving(lanes, lanes // 2, lanes))

    def add1(j):
        pairs1[j] = k1[2 * j] + k1[2 * j + 1]

    loop(0, pairs1.shape[0], add1, pairs1.shape[1:])
    wait(spread_copies(message, held, sems, packed(pairs1[...], halves1, k1.shape[2])))


def widen(out, own, low, high, count):
    planes, rows, lanes = own.shape
    size = out.shape[1]
    out[:, 0:rows, :] = own[...]
    out[:, rows:, :] = jnp.zeros((planes, size - rows, lanes), F32)
    below, above = inside("gy", -1), inside("gy", 1)
    for r in range(count):
        out[:, size - count + r, :] = masked(below, low(r))
        out[:, rows + r, :] = masked(above, high(r))


def diamond(count, own):
    return count * own + sum(2 * (count - d) for d in range(1, count + 1))


def put_planes(out, at, ref, planes, own):
    count, size = len(planes), ref.shape[1]
    for p in planes:
        out[at : at + own] = ref[p, 0:own, :]
        at += own
    for d, p in enumerate(planes, 1):
        n = count - d
        if n:
            out[at : at + n] = ref[p, own : own + n, :]
            out[at + n : at + 2 * n] = ref[p, size - n : size, :]
            at += 2 * n
    return at


def get_planes(out, planes, message, at, own, flag):
    count, size = len(planes), out.shape[1]
    halo = at + count * own
    for d, p in enumerate(planes, 1):
        out[p, 0:own, :] = masked(flag, message[at : at + own])
        out[p, own:size, :] = jnp.zeros((size - own, out.shape[2]), F32)
        at += own
        n = count - d
        if n:
            out[p, own : own + n, :] = masked(flag, message[halo : halo + n])
            out[p, size - n : size, :] = masked(flag, message[halo + n : halo + 2 * n])
            halo += 2 * n


def ends(planes, halo, count):
    below = [halo - 1 - d for d in range(count)]
    return below, [halo + planes + d for d in range(count)]


def widen_kernel(b, k, from_first, from_second, k_out, b_out, first, second):
    low, high = sides("gy", from_first, from_second)
    widen(k_out, k, lambda r: low[r], lambda r: high[r], K0)
    widen(b_out, b, lambda r: low[K0 + r], lambda r: high[K0 + r], B0)
    planes, rows = k.shape[0], k.shape[1]

    def fill(after, before):
        at = put_planes(after, 0, k_out, [planes - 1 - d for d in range(K0)], rows)
        put_planes(after, at, b_out, [planes - 1 - d for d in range(B0)], rows)
        at = put_planes(before, 0, k_out, list(range(K0)), rows)
        put_planes(before, at, b_out, list(range(B0)), rows)

    send("gx", first, second, fill)


def join(out, own, low, high, count, halo):
    planes = own.shape[0]
    left, right = inside("gx", -1), inside("gx", 1)
    out[halo : halo + planes] = own[...]
    for r in range(halo):
        below, above = halo - 1 - r, halo + planes + r
        if r < count:
            out[below] = masked(left, low(count - 1 - r))
            out[above] = masked(right, high(r))
        else:
            out[below] = jnp.zeros(out.shape[1:], F32)
            out[above] = jnp.zeros(out.shape[1:], F32)


def fine_inner_kernel(k_own, b_own, wl, ws, wz, total, inverse, b, first, second, pairs, k):
    own, planes = k_own.shape[0], b.shape[0]
    k[K0 : K0 + own] = k_own[...]
    b[K0 : K0 + own] = b_own[...]
    low, high, rows = K0, planes - K0, pairs.shape[1]
    weigh(k, wl, ws, wz, total, inverse, False, True, (low, high - 1))
    pre_smooth(
        b, first, second, (wl, ws, wz), inverse, 1.0, [(low + 1, high - 1)], [(low + 2, high - 2)]
    )
    fine_restrict(b, second, (wl, ws, wz), total, pairs, (2, own // 2 - 2))


def fine_restrict(b, field, w, total, pairs, span):
    rows = pairs.shape[1]

    def restrict(j):
        i = 2 * j + K0
        both = residual(b, field, w, total, 1.0, i) + residual(b, field, w, total, 1.0, i + 1)
        pairs[j] = both[0:rows]

    loop(*span, restrict, (2 * b.shape[1], b.shape[2]))


def put_rows(out, at, parts):
    lanes = out.shape[1]
    for part in parts:
        rows = part.shape[0]
        for h in range(part.shape[1] // lanes):
            out[at : at + rows] = part[:, h * lanes : (h + 1) * lanes]
            at += rows
    return at


def fine_outer_kernel(
    k_own, from_first, from_second, k1,
    wl_in, ws_in, wz_in, total_in, inverse_in, b_in, first_in, second_in, pairs_in,
    wl_out, ws_out, wz_out, total_out, b_out, s_out, b1_out, first_out, second_out,
    wl, ws, wz, total, inverse, b, first, second, pairs, k, halves,
):
    low, high = sides("gx", from_first, from_second)
    planes, rows, lanes = b.shape[0], s_out.shape[1], b.shape[2]
    own, end = planes - 2 * K0, planes - K0
    for mine, inner in (
        (wl, wl_in), (ws, ws_in), (wz, wz_in), (total, total_in), (inverse, inverse_in), (b, b_in),
        (first, first_in), (second, second_in),
    ):
        mine[K0 : K0 + 5] = inner[K0 : K0 + 5]
        mine[end - 5 : end] = inner[end - 5 : end]
    left, right = inside("gx", -1), inside("gx", 1)
    for ref, count, at in ((k, K0, 0), (b, B0, diamond(K0, rows))):
        below, above = ends(own, K0, count)
        get_planes(ref, below, low, at, rows, left)
        get_planes(ref, above, high, at, rows, right)
    for r in range(2):
        k[K0 + r] = k_own[r]
        k[end - 2 + r] = k_own[own - 2 + r]
    w = (wl, ws, wz)
    weigh(k, wl, ws, wz, total, inverse, False, True, (0, K0 + 1))
    weigh(k, wl, ws, wz, total, inverse, False, True, (end - 1, planes - 1), wl[end - 2])
    pre_smooth(
        b, first, second, w, inverse, 1.0,
        [(1, K0 + 1), (end - 1, planes - 1)], [(2, K0 + 2), (end - 2, planes - 2)],
    )
    pairs[2 : own // 2 - 2] = pairs_in[2 : own // 2 - 2]
    fine_restrict(b, second, w, total, pairs, (0, 2))
    fine_restrict(b, second, w, total, pairs, (own // 2 - 2, own // 2))
    b1_out[...] = coarser(pairs[...], halves, halving(lanes, lanes // 2, lanes))
    s_out[2 : own - 2] = second_in[K0 + 2 : end - 2, 0:rows, :]
    for at in (0, own - 2):
        s_out[at : at + 2] = second[K0 + at : K0 + at + 2, 0:rows, :]
    for out, mine in ((wl_out, wl), (ws_out, ws), (wz_out, wz), (total_out, total), (b_out, b)):
        out[0 : K0 + 1] = mine[0 : K0 + 1]
        out[K0 + 1 :] = mine[end - 1 :]
    count = b1_out.shape[1]

    def fill(after, before):
        for out, k_from, b_from in ((after, count - K1, count - B1), (before, 0, 0)):
            for r in range(K1):
                out[r] = k1[:, k_from + r, :]
            for r in range(B1):
                out[K1 + r] = b1_out[:, b_from + r, :]

    send("gy", first_out, second_out, fill)


def field_slab_kernel(s, first, second):
    rows = s.shape[1]

    def fill(after, before):
        put_rows(after, 0, [s[:, rows - S0 + r, :] for r in range(S0)])
        put_rows(before, 0, [s[:, r, :] for r in range(S0)])

    send("gy", first, second, fill)


def stash_kernel(*refs):
    inner, outer, (stash, sems) = refs[:5], refs[5:10], refs[10:]
    planes, edge = inner[0].shape[0], K0 + 1
    copies = []
    for i in range(5):
        for j, (source, first, at, count) in enumerate((
            (inner[i], edge, edge, planes - 2 * edge),
            (outer[i], 0, 0, edge),
            (outer[i], edge, planes - edge, edge),
        )):
            copies.append(
                pltpu.make_async_copy(
                    source.at[first : first + count],
                    stash.at[i * planes + at : i * planes + at + count],
                    sems.at[3 * i + j],
                )
            )
    for copy in copies:
        copy.start()
    wait(copies)


def widen_middle_kernel(
    k1, b1, from_first, from_second, k_out, b_out, first, second
):
    low, high = sides("gy", from_first, from_second)
    widen(k_out, k1, lambda r: low[r], lambda r: high[r], K1)
    widen(b_out, b1, lambda r: low[K1 + r], lambda r: high[K1 + r], B1)
    planes = k1.shape[0]

    def fill(after, before):
        after[0:K1] = k_out[planes - K1 :]
        after[K1:] = b_out[planes - B1 :]
        before[0:K1] = k_out[0:K1]
        before[K1:] = b_out[0:B1]

    send("gx", first, second, fill)


def middle_down_kernel(
    k_own, b_own, from_first, from_second, _s_first, _s_second, _stash,
    message, k, b, s_out,
    wl, ws, wz, inverse, total, first, second, pairs, halves, held, sems,
):
    scale = 0.25
    low, high = sides("gx", from_first, from_second)
    join(k, k_own, lambda r: low[r], lambda r: high[r], K1, K1)
    join(b, b_own, lambda r: low[K1 + r], lambda r: high[K1 + r], B1, K1)
    w = (wl, ws, wz)
    weigh(k, wl, ws, wz, total, inverse, False, True)
    planes, lanes = b.shape[0], b.shape[2]
    own, rows = planes - 2 * K1, s_out.shape[1]
    pre_smooth(b, first, second, w, inverse, scale, [(1, planes - 1)], [(2, planes - 2)])

    def restrict(j):
        i = 2 * j + K1
        both = residual(b, second, w, total, scale, i) + residual(b, second, w, total, scale, i + 1)
        pairs[j] = both[0:rows]

    loop(0, own // 2, restrict, (2 * b.shape[1], b.shape[2]))
    copies = spread_copies(message, held, sems, packed(pairs[...], halves, lanes))
    s_out[...] = second[K1 : K1 + own, 0:rows, :]
    wait(copies)


def split_lanes(ref, first, rows):
    def get(r):
        at = first + 2 * r * rows
        return jnp.concatenate([ref[at : at + rows], ref[at + rows : at + 2 * rows]], axis=1)

    return get


def from_row(ref, first, rows):
    def get(r):
        return ref[first + r * rows : first + (r + 1) * rows]

    return get


def field_planes_kernel(s, s1, from_first, from_second, s_out, first, second):
    low, high = sides("gy", from_first, from_second)
    fine, own = s.shape[0], s1.shape[0]
    widen(s_out, s, split_lanes(low, 0, fine), split_lanes(high, 0, fine), S0)

    def fill(after, before):
        for out, from0, from1 in ((after, fine - S0, own - S1), (before, 0, 0)):
            at = put_rows(out, 0, [s_out[from0 + r] for r in range(S0)])
            put_rows(out, at, [s1[from1 + r] for r in range(S1)])

    send("gx", first, second, fill)


def field_rows_kernel(
    s, s1, from_first, from_second, _weights, s_out, s1_out, first, second
):
    low, high = sides("gx", from_first, from_second)
    rows, rows1 = s.shape[1], s1.shape[1]
    join(s_out, s, split_lanes(low, 0, rows), split_lanes(high, 0, rows), S0, S0)
    at = 2 * S0 * rows
    join(s1_out, s1, from_row(low, at, rows1), from_row(high, at, rows1), S1, S1)

    def fill(after, before):
        put_rows(after, 0, [s1_out[:, rows1 - S1 + r, :] for r in range(S1)])
        put_rows(before, 0, [s1_out[:, r, :] for r in range(S1)])

    send("gy", first, second, fill)


def unpack(received, out, first, block_x, block_y, across, along):
    clear_ends(out)

    def place(column):
        for row in range(across):
            for j in range(block_y // 2):
                piece = received[row * along + column, pl.ds(first + j * block_x, block_x), :]
                at = 1 + column * (block_y // 2) + j
                out[at, row * block_x : (row + 1) * block_x, :] = piece

    loop(0, along, place, (out.shape[1], block_y // 2 * out.shape[2]))


def clear_ends(ref):
    for end in (0, ref.shape[0] - 1):
        ref[end] = jnp.zeros(ref.shape[1:], F32)


def across_up(x, after):
    half = x.shape[1] // 2
    return pltpu.roll(jnp.where(iota(x.shape, 1) < half, after, x), half, 1)


def across_down(x, before):
    half = x.shape[1] // 2
    return pltpu.roll(jnp.where(iota(x.shape, 1) < half, x, before), half, 1)


def weigh_packed(k, wl, wl_low, ws, wz, total, inverse):
    planes = k.shape[0]

    def body(i, before):
        here = k[i]
        lead = face(here, across_up(here, k[i + 1]))
        lead_low = across_down(lead, before)
        rows, row_sum = sided(here, 0, here.shape[0])
        lanes, lane_sum = sided(here, 1, here.shape[1] // 2)
        wl[i] = lead
        wl_low[i] = lead_low
        ws[i] = rows
        wz[i] = lanes
        whole = (lead_low + lead) + (row_sum + lane_sum)
        there = here > 0.0
        total[i] = jnp.where(there, whole, 0.0)
        inverse[i] = jnp.where(there, 1.0 / whole, 0.0)
        return lead

    carried(0, planes - 1, body, jnp.zeros(k.shape[1:], F32), k.shape[1:])


def beside_packed(x, w, i):
    wl, wl_low, ws, wz = w
    here = x[i]
    rows, lanes = ws[i], wz[i]
    out = wl[i] * across_up(here, x[i + 1]) + wl_low[i] * across_down(here, x[i - 1])
    out = out + (rows * up(here, 0) + down(rows * here, 0))
    return out + (lanes * up(here, 1) + down(lanes * here, 1))


def coarse_pre(b, w, inverse, first, second, scale):
    ends = [(1, b.shape[0] - 1)]
    clear_ends(first)
    clear_ends(second)
    pre_smooth(b, first, second, w, inverse, scale, ends, ends)


def widened(x, matrix):
    planes, rows, lanes = x.shape
    return pick(x.reshape(planes * rows, lanes), matrix).reshape(planes, rows, matrix.shape[1])


def twice(out, x):
    out[:, pl.ds(0, x.shape[1], stride=2), :] = x
    out[:, pl.ds(1, x.shape[1], stride=2), :] = x


def bottom(k, b, scale):
    planes, rows, lanes = k.shape
    none = jnp.zeros((1, rows, lanes), F32)

    def after(v):
        return jnp.concatenate([v[1:], none], axis=0)

    def before(v):
        return jnp.concatenate([none, v[:-1]], axis=0)

    lead = face(k, after(k))
    lead_low = jnp.concatenate([k[:1], lead[:-1]], axis=0)
    row = iota(k.shape, 1)
    row_w = face(k, jnp.where(row == rows - 1, 0.0, up(k, 1)))
    row_low = jnp.where(row == 0, k, down(row_w, 1))
    lane_w = face(k, up(k, 2))
    lane_low = down(lane_w, 2)
    whole = ((lead + lead_low) + (row_w + row_low)) + (lane_w + lane_low)
    inverse = jnp.where(k > 0.0, 1.0 / whole, 0.0)
    source = b * inverse * (1.0 / scale)
    lead_i, lead_low_i = lead * inverse, lead_low * inverse
    row_i = jnp.where(row == rows - 1, 0.0, row_w) * inverse
    row_low_i = jnp.where(row == 0, 0.0, row_low) * inverse
    lane_i, lane_low_i = lane_w * inverse, lane_low * inverse
    sigma = BOTTOM_THETA / BOTTOM_DELTA
    rho = 1.0 / sigma
    step = source * (1.0 / BOTTOM_THETA)
    x = step
    for _ in range(BOTTOM - 1):
        following = 1.0 / (2.0 * sigma - rho)
        near = (lead_i * after(x) + lead_low_i * before(x)) + (
            row_i * up(x, 1) + row_low_i * down(x, 1)
        )
        near = near + (lane_i * up(x, 2) + lane_low_i * down(x, 2))
        step = (following * rho) * step + (2.0 * following / BOTTOM_DELTA) * (source - x + near)
        x = x + step
        rho = following
    return x


def mean_matrix(lanes, valid):
    row, col = iota((lanes, lanes), 0), iota((lanes, lanes), 1)
    return jnp.where(lax.rem(row, valid) // 2 == col, 0.125, 0.0).astype(BF16)


def coarse_weights_kernel(
    valid, received, wl2, ws2, wz2, total2, level3, k4,
    low2, inverse2, k2, halves2, wl3, ws3, wz3, total3, inverse3, k3, pairs3, halves3,
):
    planes, rows, lanes = k2.shape
    across, along = lax.axis_size("gx"), lax.axis_size("gy")
    unpack(received, k2, 0, rows // across, 2 * (planes - 2) // along, across, along)
    own3 = planes - 2
    clear_ends(k3)
    k3[1 : own3 + 1] = coarser(k2[1 : own3 + 1], halves2, mean_matrix(lanes, valid))

    def add3(j):
        pairs3[j] = k3[2 * j + 1] + k3[2 * j + 2]

    loop(0, pairs3.shape[0], add3, pairs3.shape[1:])
    k4[...] = coarser(pairs3[...], halves3, halving(lanes, lanes, valid // 2))
    weigh_packed(k2, wl2, low2, ws2, wz2, total2, inverse2)
    weigh(k3, wl3, ws3, wz3, total3, inverse3, True, False)

    def pack(i):
        lane = iota(level3.shape[1:], 1)
        parts = [jnp.where(lane < valid // 2, ref[i], 0.0) for ref in (wl3, ws3, wz3, total3)]
        level3[i] = sum(
            (pltpu.roll(part, f * (valid // 2), 1) for f, part in enumerate(parts) if f), parts[0]
        )

    loop(0, planes - 1, pack, level3.shape[1:])


def invert(total):
    return jnp.where(total > 0.0, 1.0 / total, 0.0)


def coarse_kernel(
    valid, received, wl2, ws2, wz2, total2, level3, k4, stash,
    region, wl, ws, wz, total, b,
    low2, inverse2, b2, first2, second2, pairs2, halves2,
    wl3, ws3, wz3, total3, inverse3, b3, first3, second3, pairs3, halves3, sems,
):
    copies = fetch((wl, ws, wz, total, b), stash, sems)
    planes, rows, lanes = b2.shape
    across, along = lax.axis_size("gx"), lax.axis_size("gy")
    block_x, block_y = rows // across, 2 * (planes - 2) // along
    own3, half = planes - 2, valid // 2
    unpack(received, b2, 0, block_x, block_y, across, along)
    row, col = iota((lanes, lanes), 0), iota((lanes, lanes), 1)
    matrix2, matrix3 = mean_matrix(lanes, valid), halving(lanes, lanes, half)

    def complete(i):
        low2[i] = across_down(wl2[i], wl2[i - 1])
        inverse2[i] = invert(total2[i])

    def unpack3(i):
        lane = iota(level3.shape[1:], 1)
        for f, ref in enumerate((wl3, ws3, wz3, total3)):
            part = level3[i]
            if f:
                part = pltpu.roll(part, lanes - f * half, 1)
            ref[i] = jnp.where(lane < half, part, 0.0)
        inverse3[i] = invert(total3[i])

    loop(1, own3 + 1, complete, b2.shape[1:])
    loop(0, own3 + 1, unpack3, level3.shape[1:])
    w2, w3 = (wl2, low2, ws2, wz2), (wl3, ws3, wz3)
    scale2, scale3 = 0.25**2, 0.25**3
    coarse_pre(b2, w2, inverse2, first2, second2, scale2)

    def rest2(j):
        pairs2[j] = residual(b2, second2, w2, total2, scale2, j + 1)

    loop(0, own3, rest2, pairs2.shape[1:])
    clear_ends(b3)
    b3[1 : own3 + 1] = coarser(pairs2[...], halves2, matrix2)
    coarse_pre(b3, w3, inverse3, first3, second3, scale3)

    def rest3(j):
        i = 2 * j + 1
        pairs3[j] = residual(b3, second3, w3, total3, scale3, i) + residual(
            b3, second3, w3, total3, scale3, i + 1
        )

    loop(0, pairs3.shape[0], rest3, pairs3.shape[1:])
    x4 = bottom(k4[...], coarser(pairs3[...], halves3, matrix3), 0.25**4)
    twice(pairs3, widened(x4, doubling(lanes, lanes, half // 2)))

    def add_up3(j):
        for side in range(2):
            i = 2 * j + 1 + side
            first3[i] = second3[i] + pairs3[j]

    loop(0, pairs3.shape[0], add_up3, pairs3.shape[1:])
    ends = (1, own3 + 1)
    post_smooth(b3, first3, second3, w3, inverse3, scale3, ends, ends)
    matrix = jnp.where((lax.rem(col, valid) // 2 == row) & (row < half), 1.0, 0.0).astype(BF16)
    twice(pairs2, widened(first3[1 : own3 + 1], matrix))

    def add_up2(i):
        first2[i] = second2[i] + pairs2[i - 1]

    loop(1, own3 + 1, add_up2, pairs2.shape[1:])
    post_smooth(b2, first2, second2, w2, inverse2, scale2, ends, ends)
    column, place = lax.axis_index("gy"), lax.axis_index("gx")
    for q in range(region.shape[0]):
        plane = column * (block_y // 2) + q - EDGE // 2
        for side in range(3):
            block = place + side - 1
            there = (plane >= 0) & (plane < planes - 2) & (block >= 0) & (block < across)
            start = pl.multiple_of(jnp.clip(block, 0, across - 1) * block_x, block_x)
            value = first2[1 + jnp.clip(plane, 0, planes - 3), pl.ds(start, block_x), :]
            region[q, side * block_x : (side + 1) * block_x, :] = masked(there, value)
    wait(copies)


def fine_up_kernel(
    region, k1, b1, s1_own, wl, ws, wz, total, b, s_own, from_first, from_second,
    field_out, residual_out,
    wl1, ws1, wz1, total1, inverse1, inverse, first1, second1, grown, s, second, tall, thick, rest,
    out_sems,
):
    planes1, rows1, lanes1 = b1.shape
    planes, rows, lanes = b.shape
    w1, w = (wl1, ws1, wz1), (wl, ws, wz)
    weigh(k1, wl1, ws1, wz1, total1, inverse1, False, True)
    low, high = sides("gy", from_first, from_second)
    widen(first1, s1_own, from_row(low, 0, planes1), from_row(high, 0, planes1), S1)
    count_y, block_x = region.shape[0], region.shape[1] // 3
    expanded = widened(region[...], doubling(lanes1, 2 * lanes1, lanes1))
    for q in range(block_x + 2 * EDGE):
        line = expanded[:, block_x - EDGE + q, :]
        line = jnp.concatenate([line[EDGE // 2 :], line[: EDGE // 2]], axis=0)
        for r in range(4):
            half = line[:, (r // 2) * lanes1 : (r // 2 + 1) * lanes1]
            grown[q, pl.ds(r, count_y, stride=4), :] = half

    def add1(q):
        for side in range(2):
            first1[2 * q + side] = first1[2 * q + side] + grown[q]

    loop(0, block_x + 2 * EDGE, add1, b1.shape[1:])
    post_smooth(
        b1, first1, second1, w1, inverse1, 0.25, (1, planes1 - 1), (2, planes1 - 2)
    )
    begin, count = S1 - EDGE, planes1 - 2 * S1 + 2 * EDGE
    own1 = rows1 - 2 * S1
    edge = 2 * EDGE
    for half, at, where in ((own1 + EDGE, 0, 0), (EDGE, rows1 - EDGE, 2 * (own1 + EDGE))):
        part = first1[begin : begin + count, at : at + half, :]
        tall[:, pl.ds(where, half, stride=2), :] = part
        tall[:, pl.ds(where + 1, half, stride=2), :] = part
    matrix = doubling(lanes1, lanes, lanes1)
    thick[...] = pick(tall[...].reshape(count * rows, lanes1), matrix).reshape(thick.shape)
    s[0] = s_own[0] + thick[0]
    s[planes - 1] = s_own[planes - 1] + thick[count - 1]

    def add(q):
        for side in range(2):
            i = 2 * q + side - 1
            s[i] = s_own[i] + thick[q]

    loop(1, count - 1, add, b.shape[1:])

    post_smooth(
        b, s, second, w, inverse, 1.0, (1, planes - 1), (2, planes - 2), total
    )
    own, own_rows = field_out.shape[0], field_out.shape[1]
    mine = s.at[K0 : K0 + own, 0:own_rows]
    copies = [pltpu.make_async_copy(mine, field_out, out_sems.at[0])]
    copies[0].start()

    def finish(j):
        rest[j] = residual(b, s, w, total, 1.0, j + K0)[0:own_rows]

    parts = out_sems.shape[0] - 1
    for part in range(parts):
        begin, end = own * part // parts, own * (part + 1) // parts
        loop(begin, end, finish, b.shape[1:])
        copy = pltpu.make_async_copy(
            rest.at[begin:end], residual_out.at[begin:end], out_sems.at[1 + part]
        )
        copy.start()
        copies.append(copy)
    wait(copies)


def call(kernel, outs, scratch=(), held=0, kept=(), sems=(), cost=0, registers=48):
    def body(*refs):
        REGISTERS[0] = registers
        kernel(*refs)

    def run(*operands):
        inputs = [o.shape for i, o in enumerate(operands) if i not in kept]
        shapes = inputs + list(outs[held:]) + list(scratch)
        words = sum(math.prod(s[:-2]) * eight(s[-2]) * s[-1] for s in shapes)
        places = [pltpu.HBM if i in kept else pltpu.VMEM for i in range(len(operands))]
        out_places = [pltpu.HBM if i < held else pltpu.VMEM for i in range(len(outs))]
        return pl.pallas_call(
            body,
            out_shape=[jax.ShapeDtypeStruct(shape, F32) for shape in outs],
            in_specs=[pl.BlockSpec(memory_space=place) for place in places],
            out_specs=[pl.BlockSpec(memory_space=place) for place in out_places],
            scratch_shapes=[pltpu.VMEM(shape, F32) for shape in scratch]
            + [pltpu.SemaphoreType.DMA((n,)) for n in sems],
            cost_estimate=pl.CostEstimate(flops=cost, bytes_accessed=cost, transcendentals=0) if cost else None,
            compiler_params=pltpu.CompilerParams(vmem_limit_bytes=4 * words + SPARE),
        )(*operands)

    return run


def eight(rows):
    return -(-rows // 8) * 8


def per_device(right_side, coefficient):
    bx, by, nz = right_side.shape
    across, along = lax.axis_size("gx"), lax.axis_size("gy")
    devices = across * along
    hx, hy, hz = bx // 2, by // 2, nz // 2
    qx, qy = hx // 2, hy // 2
    both = ("gx", "gy")
    tall, tall1 = eight(by + 2 * K0), eight(hy + 2 * K1)
    pieces = (devices, qx * qy // 2, hz)

    slab = (K0 + B0, bx, nz)
    first, second, right_side, coefficient = call(
        slab_kernel, [slab, slab, (bx, by, nz), (bx, by, nz)]
    )(right_side, coefficient)
    from_first, from_second = swap(first, second, "gy")
    group = 4
    message, k1 = call(
        conduct_kernel,
        [pieces, (hx, hy, hz)],
        [(hx, by, nz), (hx, by, hz), (qx, hy, hz), (qx, hy, hz), (group, *pieces[1:])],
        held=1,
        sems=(devices // group,),
    )(coefficient)

    plane = (bx, tall, nz)
    slab = (diamond(K0, by) + diamond(B0, by), nz)
    k_own, b_own, first, second = call(widen_kernel, [plane, plane, slab, slab], cost=LONG)(
        right_side, coefficient, from_first, from_second
    )
    from_first, from_second = swap(first, second, "gx")

    k2 = lax.all_to_all(message, both, 0, 0, tiled=True)

    block = (bx + 2 * K0, tall, nz)
    inner = call(fine_inner_kernel, [block] * 8 + [(hx, by, nz)], [block], registers=72)(
        k_own, b_own
    )
    slab = (K1 + B1, hx, hz)
    edges = (2 * K0 + 2, tall, nz)
    field_slab = (2 * S0 * bx, hz)
    *outer, s, b1, first, second = call(
        fine_outer_kernel,
        [edges] * 5 + [(bx, by, nz), (hx, hy, hz), slab, slab],
        [block] * 8 + [(hx, by, nz), block, (hx, by, hz)],
    )(k_own, from_first, from_second, k1, *inner)
    planes = 5 * block[0] + VMEM_BYTES // (4 * tall * nz)
    (stash,) = call(stash_kernel, [(planes, tall, nz)], held=1, sems=(15,))(
        *inner[:4], inner[5], *outer
    )
    from_first, from_second = swap(first, second, "gy")
    s_first, s_second = swap(*call(field_slab_kernel, [field_slab, field_slab])(s), "gy")
    slab = (K1 + B1, tall1, hz)
    k1_own, b1_own, first, second = call(
        widen_middle_kernel, [(hx, tall1, hz), (hx, tall1, hz), slab, slab]
    )(k1, b1, from_first, from_second)
    from_first, from_second = swap(first, second, "gx")

    block1 = (hx + 2 * K1, tall1, hz)
    message, k1, b1, s1 = call(
        middle_down_kernel,
        [pieces] + [block1] * 2 + [(hx, hy, hz)],
        [block1] * 7 + [(qx, hy, hz), (qx, hy, hz), (group, *pieces[1:])],
        held=1,
        kept=(6,),
        sems=(devices // group,),
    )(k1_own, b1_own, from_first, from_second, s_first, s_second, stash)
    received = lax.all_to_all(message, both, 0, 0, tiled=True)

    x2, y2 = across * qx, along * qy
    level2, level3 = (y2 // 2 + 2, x2, hz), (y2 // 2 + 2, x2 // 2, hz)
    half2, half3 = (y2 // 2, x2, hz), (y2 // 4, x2 // 2, hz)
    valid = nz // 4
    coarse = call(
        partial(coarse_weights_kernel, valid),
        [level2] * 4 + [level3, (y2 // 4, x2 // 4, hz)],
        [level2] * 3 + [half2] + [level3] * 6 + [half3] * 2,
        registers=48,
    )(k2)
    slab = (2 * S0 * tall + S1 * hy, hz)
    s_rows, first, second = call(field_planes_kernel, [plane, slab, slab])(
        s, s1, s_first, s_second
    )
    from_first, from_second = swap(first, second, "gx")
    slab = (S1 * block1[0], hz)
    s_own, s1_own, first, second = call(
        field_rows_kernel, [block, (block1[0], hy, hz), slab, slab]
    )(s_rows, s1, from_first, from_second, coarse[-1])
    from_first, from_second = swap(first, second, "gy")

    region, *weights = call(
        partial(coarse_kernel, valid),
        [(qy // 2 + EDGE, 3 * qx, hz)] + [block] * 5,
        [level2] * 5 + [half2] * 2 + [level3] * 8 + [half3] * 2,
        kept=(7,),
        sems=(5,),
        registers=40,
    )(received, *coarse, stash)

    count = hx + 2 * EDGE
    field, rest = call(
        fine_up_kernel,
        [(bx, by, nz)] * 2,
        [block1] * 5 + [block, block1, block1, (qx + 2 * EDGE, tall1, hz)]
        + [block, block, (count, tall, hz), (count, tall, nz), (bx, by, nz)],
        held=2,
        sems=(5,),
        registers=96,
    )(region, k1, b1, s1_own, *weights, s_own, from_first, from_second)
    return field, rest


def solution(mesh):
    in_specs = (P("gx", "gy", None), P("gx", "gy", None))
    out_specs = (P("gx", "gy", None), P("gx", "gy", None))
    return jax.shard_map(
        per_device, mesh=mesh, in_specs=in_specs, out_specs=out_specs, check_vma=False
    )
```

```python
import math
from functools import partial

import jax
import jax.numpy as jnp
from jax import lax
from jax.experimental import pallas as pl
from jax.experimental.pallas import tpu as pltpu
from jax.sharding import PartitionSpec as P

F32 = jnp.float32
BF16 = jnp.bfloat16

THETA = 1.25
DELTA = 0.75
SIGMA = THETA / DELTA
RHO0 = 1.0 / SIGMA
RHO1 = 1.0 / (2.0 * SIGMA - RHO0)
KEEP = RHO1 * RHO0
GAIN = 2.0 * RHO1 / DELTA
BOTTOM = 8
BOTTOM_THETA = (2.0 + 0.05) / 2.0
BOTTOM_DELTA = (2.0 - 0.05) / 2.0

K0, B0, S0 = 3, 2, 3
K1, B1, S1 = 4, 3, 4
EDGE = 2
REGISTERS = [48]
SPARE = 4 * 1024 * 1024
VMEM_BYTES = 64 * 1024 * 1024
LONG = 10**12


def swap(first, second, axis):
    axes = ("gx", "gy")
    sizes = [lax.axis_size(name) for name in axes]
    along = axes.index(axis)
    size, other = sizes[along], sizes[1 - along]

    def place(i, j):
        return i * sizes[1] + j if along == 0 else j * sizes[1] + i

    def pairs(begin):
        found = []
        for j in range(other):
            for i in range(begin, size - 1, 2):
                found += [(place(i, j), place(i + 1, j)), (place(i + 1, j), place(i, j))]
        met = {source for source, _ in found}
        for i in range(size):
            for j in range(other):
                beside = j + 1 - 2 * (j % 2)
                target = place(i, beside) if beside < other else place(i, j)
                if place(i, j) not in met:
                    found.append((place(i, j), target))
        return found

    return lax.ppermute(first, axes, pairs(0)), lax.ppermute(second, axes, pairs(1))


def is_even(axis):
    return lax.rem(lax.axis_index(axis), 2) == 0


class Either:
    def __init__(self, flag, one, two):
        self.flag, self.one, self.two, self.shape = flag, one, two, one.shape

    def __getitem__(self, index):
        return jnp.where(self.flag, self.one[index], self.two[index])


def sides(axis, first, second):
    even = is_even(axis)
    return Either(even, second, first), Either(even, first, second)


def send(axis, first, second, fill):
    even = is_even(axis)

    @pl.when(even)
    def _():
        fill(first, second)

    @pl.when(jnp.logical_not(even))
    def _():
        fill(second, first)


def inside(axis, side):
    index = lax.axis_index(axis)
    if side < 0:
        return index > 0
    return index < lax.axis_size(axis) - 1


def masked(flag, value):
    return jnp.where(flag, value, jnp.zeros_like(value))


def iota(shape, dim):
    return lax.broadcasted_iota(jnp.int32, shape, dim)


def pick(x, matrix):
    high = x.astype(BF16)
    low = (x - high.astype(F32)).astype(BF16)
    return jnp.dot(high, matrix, preferred_element_type=F32) + jnp.dot(
        low, matrix, preferred_element_type=F32
    )


def halving(fine, coarse, valid):
    row, col = iota((fine, coarse), 0), iota((fine, coarse), 1)
    return jnp.where((row // 2 == col) & (row < valid), 0.125, 0.0).astype(BF16)


def doubling(coarse, fine, valid):
    row, col = iota((coarse, fine), 0), iota((coarse, fine), 1)
    return jnp.where((row == col // 2) & (row < valid), 1.0, 0.0).astype(BF16)


def fetch(refs, stash, sems):
    copies = []
    for i, ref in enumerate(refs):
        planes = ref.shape[0]
        there = stash.at[i * planes : (i + 1) * planes]
        copies.append(pltpu.make_async_copy(there, ref, sems.at[i]))
    for copy in copies:
        copy.start()
    return copies


def wait(copies):
    for copy in copies:
        copy.wait()


def face(a, b):
    product, total = a * b, a + b
    return jnp.where(product > 0.0, 2.0 * product / total, total)


def up(x, axis):
    return pltpu.roll(x, x.shape[axis] - 1, axis)


def down(x, axis):
    return pltpu.roll(x, 1, axis)


def sided(k, axis, edge):
    after = up(k, axis)
    if edge is None:
        w = face(k, after)
        return w, w + down(w, axis)
    place = iota(k.shape, axis)
    if edge < k.shape[axis]:
        place = lax.rem(place, edge)
    last = place == edge - 1
    w = face(k, jnp.where(last, 0.0, after))
    return jnp.where(last, 0.0, w), w + jnp.where(place == 0, k, down(w, axis))


def blocks_of(plane, count):
    most = max(1, REGISTERS[0] // max(1, plane[0] * plane[1] // 1024))
    best = None
    for blocks in range(max(1, count // (2 * most)), count + 1):
        steps = count // blocks
        cost = (count - blocks * steps) * 0.5 + abs(steps - most)
        if best is None or cost < best[0]:
            best = (cost, blocks, steps)
    return best[1:]


def carried(low, high, body, carry, plane):
    blocks, steps = blocks_of(plane, high - low)
    end = low + blocks * steps
    if blocks == 1:
        end = low
        steps = high - low
    elif blocks * steps:
        carry = lax.fori_loop(low, end, body, carry, unroll=steps)
    for i in range(end, high):
        carry = body(i, carry)
    return carry


def loop(low, high, body, plane):
    def step(i, carry):
        body(i)
        return carry

    carried(low, high, step, 0, plane)


def weigh(k, wl, ws, wz, total, inverse, row_edge, lane_edge, span=None, before=None):
    plane = k.shape[1:]
    low, high = span or (0, k.shape[0] - 1)

    def body(i, before):
        here = k[i]
        lead = face(here, k[i + 1])
        rows, row_sum = sided(here, 0, here.shape[0] if row_edge else None)
        lanes, lane_sum = sided(here, 1, here.shape[1] if lane_edge else None)
        wl[i] = lead
        ws[i] = rows
        wz[i] = lanes
        whole = (before + lead) + (row_sum + lane_sum)
        there = here > 0.0
        total[i] = jnp.where(there, whole, 0.0)
        inverse[i] = jnp.where(there, 1.0 / whole, 0.0)
        return lead

    before = jnp.zeros(plane, F32) if before is None else before
    carried(low, high, body, before, plane)


def beside(x, w, i):
    if len(w) == 4:
        return beside_packed(x, w, i)
    wl, ws, wz = w
    here = x[i]
    rows, lanes = ws[i], wz[i]
    out = wl[i] * x[i + 1] + wl[i - 1] * x[i - 1]
    out = out + (rows * up(here, 0) + down(rows * here, 0))
    return out + (lanes * up(here, 1) + down(lanes * here, 1))


def pre_smooth(b, first, second, w, inverse, scale, outer, inner, total=None):
    def start(i):
        if total is not None:
            inverse[i] = invert(total[i])
        first[i] = b[i] * inverse[i] * (1.0 / (scale * THETA))

    for span in outer:
        loop(*span, start, b.shape[1:])

    def sweep(i):
        near = beside(first, w, i)
        second[i] = (1.0 + KEEP + GAIN * (THETA - 1.0)) * first[i] + GAIN * (inverse[i] * near)

    for span in inner:
        loop(*span, sweep, b.shape[1:])


def post_smooth(b, first, second, w, inverse, scale, outer, inner, total=None):
    def sweep(i):
        x = first[i]
        near = beside(first, w, i)
        if total is not None:
            inverse[i] = invert(total[i])
        second[i] = x + ((b[i] * (1.0 / scale) + near) * inverse[i] - x) * (1.0 / THETA)

    loop(*outer, sweep, b.shape[1:])

    def last(i):
        x = second[i]
        near = beside(second, w, i)
        step = KEEP * (x - first[i]) + GAIN * ((b[i] * (1.0 / scale) + near) * inverse[i] - x)
        first[i] = x + step

    loop(*inner, last, b.shape[1:])


def residual(b, field, w, total, scale, i):
    return b[i] - scale * (total[i] * field[i] - beside(field, w, i))


def coarser(pairs, halves, matrix):
    planes, rows, lanes = pairs.shape
    halves[...] = pick(pairs.reshape(planes * rows, lanes), matrix).reshape(halves.shape)
    count = rows // 2
    return halves[:, pl.ds(0, count, stride=2), :] + halves[:, pl.ds(1, count, stride=2), :]


def packed(pairs, halves, valid):
    planes, rows, lanes = pairs.shape
    matrix = halving(lanes, halves.shape[2], valid)
    halves[...] = pick(pairs.reshape(planes * rows, lanes), matrix).reshape(halves.shape)
    count = rows // 4
    quarter = [halves[:, pl.ds(r, count, stride=4), :] for r in range(4)]
    odd = pltpu.roll(quarter[2] + quarter[3], halves.shape[2] // 2, 2)
    return (quarter[0] + quarter[1]) + odd


def spread_copies(out, held, sems, *fields):
    for f, rows in enumerate(fields):
        size, count = rows.shape[0], rows.shape[1]
        for i in range(size):
            held[0, pl.ds(f * size * count + i, count, stride=size), :] = rows[i]
    group = held.shape[0]
    for d in range(1, group):
        held[d] = held[0]
    copies = []
    for d in range(out.shape[0] // group):
        there = out.at[d * group : (d + 1) * group]
        copies.append(pltpu.make_async_copy(held, there, sems.at[d]))
    for copy in copies:
        copy.start()
    return copies


def slab_kernel(b, k, first, second, b_out, k_out):
    rows = k.shape[1]
    b_out[...] = b[...]
    k_out[...] = k[...]

    def fill(after, before):
        for r in range(K0):
            after[r] = k[:, rows - K0 + r, :]
            before[r] = k[:, r, :]
        for r in range(B0):
            after[K0 + r] = b[:, rows - B0 + r, :]
            before[K0 + r] = b[:, r, :]

    send("gy", first, second, fill)


def conduct_kernel(k, message, k1, pairs, halves, pairs1, halves1, held, sems):
    def add(j):
        pairs[j] = k[2 * j] + k[2 * j + 1]

    loop(0, pairs.shape[0], add, pairs.shape[1:])
    lanes = k.shape[2]
    k1[...] = coarser(pairs[...], halves, halving(lanes, lanes // 2, lanes))

    def add1(j):
        pairs1[j] = k1[2 * j] + k1[2 * j + 1]

    loop(0, pairs1.shape[0], add1, pairs1.shape[1:])
    wait(spread_copies(message, held, sems, packed(pairs1[...], halves1, k1.shape[2])))


def widen(out, own, low, high, count):
    planes, rows, lanes = own.shape
    size = out.shape[1]
    out[:, 0:rows, :] = own[...]
    out[:, rows:, :] = jnp.zeros((planes, size - rows, lanes), F32)
    below, above = inside("gy", -1), inside("gy", 1)
    for r in range(count):
        out[:, size - count + r, :] = masked(below, low(r))
        out[:, rows + r, :] = masked(above, high(r))


def diamond(count, own):
    return count * own + sum(2 * (count - d) for d in range(1, count + 1))


def put_planes(out, at, ref, planes, own):
    count, size = len(planes), ref.shape[1]
    for p in planes:
        out[at : at + own] = ref[p, 0:own, :]
        at += own
    for d, p in enumerate(planes, 1):
        n = count - d
        if n:
            out[at : at + n] = ref[p, own : own + n, :]
            out[at + n : at + 2 * n] = ref[p, size - n : size, :]
            at += 2 * n
    return at


def get_planes(out, planes, message, at, own, flag):
    count, size = len(planes), out.shape[1]
    halo = at + count * own
    for d, p in enumerate(planes, 1):
        out[p, 0:own, :] = masked(flag, message[at : at + own])
        out[p, own:size, :] = jnp.zeros((size - own, out.shape[2]), F32)
        at += own
        n = count - d
        if n:
            out[p, own : own + n, :] = masked(flag, message[halo : halo + n])
            out[p, size - n : size, :] = masked(flag, message[halo + n : halo + 2 * n])
            halo += 2 * n


def ends(planes, halo, count):
    below = [halo - 1 - d for d in range(count)]
    return below, [halo + planes + d for d in range(count)]


def widen_kernel(b, k, from_first, from_second, k_out, b_out, first, second):
    low, high = sides("gy", from_first, from_second)
    widen(k_out, k, lambda r: low[r], lambda r: high[r], K0)
    widen(b_out, b, lambda r: low[K0 + r], lambda r: high[K0 + r], B0)
    planes, rows = k.shape[0], k.shape[1]

    def fill(after, before):
        at = put_planes(after, 0, k_out, [planes - 1 - d for d in range(K0)], rows)
        put_planes(after, at, b_out, [planes - 1 - d for d in range(B0)], rows)
        at = put_planes(before, 0, k_out, list(range(K0)), rows)
        put_planes(before, at, b_out, list(range(B0)), rows)

    send("gx", first, second, fill)


def join(out, own, low, high, count, halo):
    planes = own.shape[0]
    left, right = inside("gx", -1), inside("gx", 1)
    out[halo : halo + planes] = own[...]
    for r in range(halo):
        below, above = halo - 1 - r, halo + planes + r
        if r < count:
            out[below] = masked(left, low(count - 1 - r))
            out[above] = masked(right, high(r))
        else:
            out[below] = jnp.zeros(out.shape[1:], F32)
            out[above] = jnp.zeros(out.shape[1:], F32)


def fine_inner_kernel(k_own, b_own, wl, ws, wz, total, inverse, b, first, second, pairs, k):
    own, planes = k_own.shape[0], b.shape[0]
    k[K0 : K0 + own] = k_own[...]
    b[K0 : K0 + own] = b_own[...]
    low, high, rows = K0, planes - K0, pairs.shape[1]
    weigh(k, wl, ws, wz, total, inverse, False, True, (low, high - 1))
    pre_smooth(
        b, first, second, (wl, ws, wz), inverse, 1.0, [(low + 1, high - 1)], [(low + 2, high - 2)]
    )
    fine_restrict(b, second, (wl, ws, wz), total, pairs, (2, own // 2 - 2))


def fine_restrict(b, field, w, total, pairs, span):
    rows = pairs.shape[1]

    def restrict(j):
        i = 2 * j + K0
        both = residual(b, field, w, total, 1.0, i) + residual(b, field, w, total, 1.0, i + 1)
        pairs[j] = both[0:rows]

    loop(*span, restrict, (2 * b.shape[1], b.shape[2]))


def put_rows(out, at, parts):
    lanes = out.shape[1]
    for part in parts:
        rows = part.shape[0]
        for h in range(part.shape[1] // lanes):
            out[at : at + rows] = part[:, h * lanes : (h + 1) * lanes]
            at += rows
    return at


def fine_outer_kernel(
    k_own, from_first, from_second, k1,
    wl_in, ws_in, wz_in, total_in, inverse_in, b_in, first_in, second_in, pairs_in,
    wl_out, ws_out, wz_out, total_out, b_out, s_out, b1_out, first_out, second_out,
    wl, ws, wz, total, inverse, b, first, second, pairs, k, halves,
):
    low, high = sides("gx", from_first, from_second)
    planes, rows, lanes = b.shape[0], s_out.shape[1], b.shape[2]
    own, end = planes - 2 * K0, planes - K0
    for mine, inner in (
        (wl, wl_in), (ws, ws_in), (wz, wz_in), (total, total_in), (inverse, inverse_in), (b, b_in),
        (first, first_in), (second, second_in),
    ):
        mine[K0 : K0 + 5] = inner[K0 : K0 + 5]
        mine[end - 5 : end] = inner[end - 5 : end]
    left, right = inside("gx", -1), inside("gx", 1)
    for ref, count, at in ((k, K0, 0), (b, B0, diamond(K0, rows))):
        below, above = ends(own, K0, count)
        get_planes(ref, below, low, at, rows, left)
        get_planes(ref, above, high, at, rows, right)
    for r in range(2):
        k[K0 + r] = k_own[r]
        k[end - 2 + r] = k_own[own - 2 + r]
    w = (wl, ws, wz)
    weigh(k, wl, ws, wz, total, inverse, False, True, (0, K0 + 1))
    weigh(k, wl, ws, wz, total, inverse, False, True, (end - 1, planes - 1), wl[end - 2])
    pre_smooth(
        b, first, second, w, inverse, 1.0,
        [(1, K0 + 1), (end - 1, planes - 1)], [(2, K0 + 2), (end - 2, planes - 2)],
    )
    pairs[2 : own // 2 - 2] = pairs_in[2 : own // 2 - 2]
    fine_restrict(b, second, w, total, pairs, (0, 2))
    fine_restrict(b, second, w, total, pairs, (own // 2 - 2, own // 2))
    b1_out[...] = coarser(pairs[...], halves, halving(lanes, lanes // 2, lanes))
    s_out[2 : own - 2] = second_in[K0 + 2 : end - 2, 0:rows, :]
    for at in (0, own - 2):
        s_out[at : at + 2] = second[K0 + at : K0 + at + 2, 0:rows, :]
    for out, mine in ((wl_out, wl), (ws_out, ws), (wz_out, wz), (total_out, total), (b_out, b)):
        out[0 : K0 + 1] = mine[0 : K0 + 1]
        out[K0 + 1 :] = mine[end - 1 :]
    count = b1_out.shape[1]

    def fill(after, before):
        for out, k_from, b_from in ((after, count - K1, count - B1), (before, 0, 0)):
            for r in range(K1):
                out[r] = k1[:, k_from + r, :]
            for r in range(B1):
                out[K1 + r] = b1_out[:, b_from + r, :]

    send("gy", first_out, second_out, fill)


def field_slab_kernel(s, first, second):
    rows = s.shape[1]

    def fill(after, before):
        put_rows(after, 0, [s[:, rows - S0 + r, :] for r in range(S0)])
        put_rows(before, 0, [s[:, r, :] for r in range(S0)])

    send("gy", first, second, fill)


def stash_kernel(*refs):
    inner, outer, (stash, sems) = refs[:5], refs[5:10], refs[10:]
    planes, edge = inner[0].shape[0], K0 + 1
    copies = []
    for i in range(5):
        for j, (source, first, at, count) in enumerate((
            (inner[i], edge, edge, planes - 2 * edge),
            (outer[i], 0, 0, edge),
            (outer[i], edge, planes - edge, edge),
        )):
            copies.append(
                pltpu.make_async_copy(
                    source.at[first : first + count],
                    stash.at[i * planes + at : i * planes + at + count],
                    sems.at[3 * i + j],
                )
            )
    for copy in copies:
        copy.start()
    wait(copies)


def widen_middle_kernel(
    k1, b1, from_first, from_second, k_out, b_out, first, second
):
    low, high = sides("gy", from_first, from_second)
    widen(k_out, k1, lambda r: low[r], lambda r: high[r], K1)
    widen(b_out, b1, lambda r: low[K1 + r], lambda r: high[K1 + r], B1)
    planes = k1.shape[0]

    def fill(after, before):
        after[0:K1] = k_out[planes - K1 :]
        after[K1:] = b_out[planes - B1 :]
        before[0:K1] = k_out[0:K1]
        before[K1:] = b_out[0:B1]

    send("gx", first, second, fill)


def middle_down_kernel(
    k_own, b_own, from_first, from_second, _s_first, _s_second, _stash,
    message, k, b, s_out,
    wl, ws, wz, inverse, total, first, second, pairs, halves, held, sems,
):
    scale = 0.25
    low, high = sides("gx", from_first, from_second)
    join(k, k_own, lambda r: low[r], lambda r: high[r], K1, K1)
    join(b, b_own, lambda r: low[K1 + r], lambda r: high[K1 + r], B1, K1)
    w = (wl, ws, wz)
    weigh(k, wl, ws, wz, total, inverse, False, True)
    planes, lanes = b.shape[0], b.shape[2]
    own, rows = planes - 2 * K1, s_out.shape[1]
    pre_smooth(b, first, second, w, inverse, scale, [(1, planes - 1)], [(2, planes - 2)])

    def restrict(j):
        i = 2 * j + K1
        both = residual(b, second, w, total, scale, i) + residual(b, second, w, total, scale, i + 1)
        pairs[j] = both[0:rows]

    loop(0, own // 2, restrict, (2 * b.shape[1], b.shape[2]))
    copies = spread_copies(message, held, sems, packed(pairs[...], halves, lanes))
    s_out[...] = second[K1 : K1 + own, 0:rows, :]
    wait(copies)


def split_lanes(ref, first, rows):
    def get(r):
        at = first + 2 * r * rows
        return jnp.concatenate([ref[at : at + rows], ref[at + rows : at + 2 * rows]], axis=1)

    return get


def from_row(ref, first, rows):
    def get(r):
        return ref[first + r * rows : first + (r + 1) * rows]

    return get


def field_planes_kernel(s, s1, from_first, from_second, s_out, first, second):
    low, high = sides("gy", from_first, from_second)
    fine, own = s.shape[0], s1.shape[0]
    widen(s_out, s, split_lanes(low, 0, fine), split_lanes(high, 0, fine), S0)

    def fill(after, before):
        for out, from0, from1 in ((after, fine - S0, own - S1), (before, 0, 0)):
            at = put_rows(out, 0, [s_out[from0 + r] for r in range(S0)])
            put_rows(out, at, [s1[from1 + r] for r in range(S1)])

    send("gx", first, second, fill)


def field_rows_kernel(
    s, s1, from_first, from_second, _weights, s_out, s1_out, first, second
):
    low, high = sides("gx", from_first, from_second)
    rows, rows1 = s.shape[1], s1.shape[1]
    join(s_out, s, split_lanes(low, 0, rows), split_lanes(high, 0, rows), S0, S0)
    at = 2 * S0 * rows
    join(s1_out, s1, from_row(low, at, rows1), from_row(high, at, rows1), S1, S1)

    def fill(after, before):
        put_rows(after, 0, [s1_out[:, rows1 - S1 + r, :] for r in range(S1)])
        put_rows(before, 0, [s1_out[:, r, :] for r in range(S1)])

    send("gy", first, second, fill)


def unpack(received, out, first, block_x, block_y, across, along):
    clear_ends(out)

    def place(column):
        for row in range(across):
            for j in range(block_y // 2):
                piece = received[row * along + column, pl.ds(first + j * block_x, block_x), :]
                at = 1 + column * (block_y // 2) + j
                out[at, row * block_x : (row + 1) * block_x, :] = piece

    loop(0, along, place, (out.shape[1], block_y // 2 * out.shape[2]))


def clear_ends(ref):
    for end in (0, ref.shape[0] - 1):
        ref[end] = jnp.zeros(ref.shape[1:], F32)


def across_up(x, after):
    half = x.shape[1] // 2
    return pltpu.roll(jnp.where(iota(x.shape, 1) < half, after, x), half, 1)


def across_down(x, before):
    half = x.shape[1] // 2
    return pltpu.roll(jnp.where(iota(x.shape, 1) < half, x, before), half, 1)


def weigh_packed(k, wl, wl_low, ws, wz, total, inverse):
    planes = k.shape[0]

    def body(i, before):
        here = k[i]
        lead = face(here, across_up(here, k[i + 1]))
        lead_low = across_down(lead, before)
        rows, row_sum = sided(here, 0, here.shape[0])
        lanes, lane_sum = sided(here, 1, here.shape[1] // 2)
        wl[i] = lead
        wl_low[i] = lead_low
        ws[i] = rows
        wz[i] = lanes
        whole = (lead_low + lead) + (row_sum + lane_sum)
        there = here > 0.0
        total[i] = jnp.where(there, whole, 0.0)
        inverse[i] = jnp.where(there, 1.0 / whole, 0.0)
        return lead

    carried(0, planes - 1, body, jnp.zeros(k.shape[1:], F32), k.shape[1:])


def beside_packed(x, w, i):
    wl, wl_low, ws, wz = w
    here = x[i]
    rows, lanes = ws[i], wz[i]
    out = wl[i] * across_up(here, x[i + 1]) + wl_low[i] * across_down(here, x[i - 1])
    out = out + (rows * up(here, 0) + down(rows * here, 0))
    return out + (lanes * up(here, 1) + down(lanes * here, 1))


def coarse_pre(b, w, inverse, first, second, scale, total):
    ends = [(1, b.shape[0] - 1)]
    clear_ends(first)
    clear_ends(second)
    pre_smooth(b, first, second, w, inverse, scale, ends, ends, total)


def widened(x, matrix):
    planes, rows, lanes = x.shape
    return pick(x.reshape(planes * rows, lanes), matrix).reshape(planes, rows, matrix.shape[1])


def twice(out, x):
    out[:, pl.ds(0, x.shape[1], stride=2), :] = x
    out[:, pl.ds(1, x.shape[1], stride=2), :] = x


def bottom(k, b, scale):
    planes, rows, lanes = k.shape
    none = jnp.zeros((1, rows, lanes), F32)

    def after(v):
        return jnp.concatenate([v[1:], none], axis=0)

    def before(v):
        return jnp.concatenate([none, v[:-1]], axis=0)

    lead = face(k, after(k))
    lead_low = jnp.concatenate([k[:1], lead[:-1]], axis=0)
    row = iota(k.shape, 1)
    row_w = face(k, jnp.where(row == rows - 1, 0.0, up(k, 1)))
    row_low = jnp.where(row == 0, k, down(row_w, 1))
    lane_w = face(k, up(k, 2))
    lane_low = down(lane_w, 2)
    whole = ((lead + lead_low) + (row_w + row_low)) + (lane_w + lane_low)
    inverse = jnp.where(k > 0.0, 1.0 / whole, 0.0)
    source = b * inverse * (1.0 / scale)
    lead_i, lead_low_i = lead * inverse, lead_low * inverse
    row_i = jnp.where(row == rows - 1, 0.0, row_w) * inverse
    row_low_i = jnp.where(row == 0, 0.0, row_low) * inverse
    lane_i, lane_low_i = lane_w * inverse, lane_low * inverse
    sigma = BOTTOM_THETA / BOTTOM_DELTA
    rho = 1.0 / sigma
    step = source * (1.0 / BOTTOM_THETA)
    x = step
    for _ in range(BOTTOM - 1):
        following = 1.0 / (2.0 * sigma - rho)
        near = (lead_i * after(x) + lead_low_i * before(x)) + (
            row_i * up(x, 1) + row_low_i * down(x, 1)
        )
        near = near + (lane_i * up(x, 2) + lane_low_i * down(x, 2))
        step = (following * rho) * step + (2.0 * following / BOTTOM_DELTA) * (source - x + near)
        x = x + step
        rho = following
    return x


def mean_matrix(lanes, valid):
    row, col = iota((lanes, lanes), 0), iota((lanes, lanes), 1)
    return jnp.where(lax.rem(row, valid) // 2 == col, 0.125, 0.0).astype(BF16)


def coarse_weights_kernel(
    valid, received, wl2, ws2, wz2, total2, level3, k4,
    low2, inverse2, k2, halves2, wl3, ws3, wz3, total3, inverse3, k3, pairs3, halves3,
):
    planes, rows, lanes = k2.shape
    across, along = lax.axis_size("gx"), lax.axis_size("gy")
    unpack(received, k2, 0, rows // across, 2 * (planes - 2) // along, across, along)
    own3 = planes - 2
    clear_ends(k3)
    k3[1 : own3 + 1] = coarser(k2[1 : own3 + 1], halves2, mean_matrix(lanes, valid))

    def add3(j):
        pairs3[j] = k3[2 * j + 1] + k3[2 * j + 2]

    loop(0, pairs3.shape[0], add3, pairs3.shape[1:])
    k4[...] = coarser(pairs3[...], halves3, halving(lanes, lanes, valid // 2))
    weigh_packed(k2, wl2, low2, ws2, wz2, total2, inverse2)
    weigh(k3, wl3, ws3, wz3, total3, inverse3, True, False)

    def pack(i):
        lane = iota(level3.shape[1:], 1)
        parts = [jnp.where(lane < valid // 2, ref[i], 0.0) for ref in (wl3, ws3, wz3, total3)]
        level3[i] = sum(
            (pltpu.roll(part, f * (valid // 2), 1) for f, part in enumerate(parts) if f), parts[0]
        )

    loop(0, planes - 1, pack, level3.shape[1:])


def invert(total):
    return jnp.where(total > 0.0, 1.0 / total, 0.0)


def coarse_kernel(
    valid, received, wl2, ws2, wz2, total2, level3, k4, stash,
    region, wl, ws, wz, total, b,
    low2, inverse2, b2, first2, second2, pairs2, halves2,
    wl3, ws3, wz3, total3, inverse3, b3, first3, second3, pairs3, halves3, sems,
):
    copies = fetch((wl, ws, wz, total, b), stash, sems)
    planes, rows, lanes = b2.shape
    across, along = lax.axis_size("gx"), lax.axis_size("gy")
    block_x, block_y = rows // across, 2 * (planes - 2) // along
    own3, half = planes - 2, valid // 2
    unpack(received, b2, 0, block_x, block_y, across, along)
    row, col = iota((lanes, lanes), 0), iota((lanes, lanes), 1)
    matrix2, matrix3 = mean_matrix(lanes, valid), halving(lanes, lanes, half)

    def complete(i):
        low2[i] = across_down(wl2[i], wl2[i - 1])

    def unpack3(i):
        lane = iota(level3.shape[1:], 1)
        for f, ref in enumerate((wl3, ws3, wz3, total3)):
            part = level3[i]
            if f:
                part = pltpu.roll(part, lanes - f * half, 1)
            ref[i] = jnp.where(lane < half, part, 0.0)

    loop(1, own3 + 1, complete, b2.shape[1:])
    loop(0, own3 + 1, unpack3, level3.shape[1:])
    w2, w3 = (wl2, low2, ws2, wz2), (wl3, ws3, wz3)
    scale2, scale3 = 0.25**2, 0.25**3
    coarse_pre(b2, w2, inverse2, first2, second2, scale2, total2)

    def rest2(j):
        pairs2[j] = residual(b2, second2, w2, total2, scale2, j + 1)

    loop(0, own3, rest2, pairs2.shape[1:])
    clear_ends(b3)
    b3[1 : own3 + 1] = coarser(pairs2[...], halves2, matrix2)
    coarse_pre(b3, w3, inverse3, first3, second3, scale3, total3)

    def rest3(j):
        i = 2 * j + 1
        pairs3[j] = residual(b3, second3, w3, total3, scale3, i) + residual(
            b3, second3, w3, total3, scale3, i + 1
        )

    loop(0, pairs3.shape[0], rest3, pairs3.shape[1:])
    x4 = bottom(k4[...], coarser(pairs3[...], halves3, matrix3), 0.25**4)
    twice(pairs3, widened(x4, doubling(lanes, lanes, half // 2)))

    def add_up3(j):
        for side in range(2):
            i = 2 * j + 1 + side
            first3[i] = second3[i] + pairs3[j]

    loop(0, pairs3.shape[0], add_up3, pairs3.shape[1:])
    ends = (1, own3 + 1)
    post_smooth(b3, first3, second3, w3, inverse3, scale3, ends, ends)
    matrix = jnp.where((lax.rem(col, valid) // 2 == row) & (row < half), 1.0, 0.0).astype(BF16)
    twice(pairs2, widened(first3[1 : own3 + 1], matrix))

    def add_up2(i):
        first2[i] = second2[i] + pairs2[i - 1]

    loop(1, own3 + 1, add_up2, pairs2.shape[1:])
    post_smooth(b2, first2, second2, w2, inverse2, scale2, ends, ends)
    column, place = lax.axis_index("gy"), lax.axis_index("gx")
    for q in range(region.shape[0]):
        plane = column * (block_y // 2) + q - EDGE // 2
        for side in range(3):
            block = place + side - 1
            there = (plane >= 0) & (plane < planes - 2) & (block >= 0) & (block < across)
            start = pl.multiple_of(jnp.clip(block, 0, across - 1) * block_x, block_x)
            value = first2[1 + jnp.clip(plane, 0, planes - 3), pl.ds(start, block_x), :]
            region[q, side * block_x : (side + 1) * block_x, :] = masked(there, value)
    wait(copies)


def fine_up_kernel(
    region, k1, b1, s1_own, wl, ws, wz, total, b, s_own, from_first, from_second,
    field_out, residual_out,
    wl1, ws1, wz1, total1, inverse1, inverse, first1, second1, grown, s, second, tall, thick, rest,
    out_sems,
):
    planes1, rows1, lanes1 = b1.shape
    planes, rows, lanes = b.shape
    w1, w = (wl1, ws1, wz1), (wl, ws, wz)
    weigh(k1, wl1, ws1, wz1, total1, inverse1, False, True)
    low, high = sides("gy", from_first, from_second)
    widen(first1, s1_own, from_row(low, 0, planes1), from_row(high, 0, planes1), S1)
    count_y, block_x = region.shape[0], region.shape[1] // 3
    expanded = widened(region[...], doubling(lanes1, 2 * lanes1, lanes1))
    for q in range(block_x + 2 * EDGE):
        line = expanded[:, block_x - EDGE + q, :]
        line = jnp.concatenate([line[EDGE // 2 :], line[: EDGE // 2]], axis=0)
        for r in range(4):
            half = line[:, (r // 2) * lanes1 : (r // 2 + 1) * lanes1]
            grown[q, pl.ds(r, count_y, stride=4), :] = half

    def add1(q):
        for side in range(2):
            first1[2 * q + side] = first1[2 * q + side] + grown[q]

    loop(0, block_x + 2 * EDGE, add1, b1.shape[1:])
    post_smooth(
        b1, first1, second1, w1, inverse1, 0.25, (1, planes1 - 1), (2, planes1 - 2)
    )
    begin, count = S1 - EDGE, planes1 - 2 * S1 + 2 * EDGE
    own1 = rows1 - 2 * S1
    edge = 2 * EDGE
    for half, at, where in ((own1 + EDGE, 0, 0), (EDGE, rows1 - EDGE, 2 * (own1 + EDGE))):
        part = first1[begin : begin + count, at : at + half, :]
        tall[:, pl.ds(where, half, stride=2), :] = part
        tall[:, pl.ds(where + 1, half, stride=2), :] = part
    matrix = doubling(lanes1, lanes, lanes1)
    thick[...] = pick(tall[...].reshape(count * rows, lanes1), matrix).reshape(thick.shape)
    s[0] = s_own[0] + thick[0]
    s[planes - 1] = s_own[planes - 1] + thick[count - 1]

    def add(q):
        for side in range(2):
            i = 2 * q + side - 1
            s[i] = s_own[i] + thick[q]

    loop(1, count - 1, add, b.shape[1:])

    post_smooth(
        b, s, second, w, inverse, 1.0, (1, planes - 1), (2, planes - 2), total
    )
    own, own_rows = field_out.shape[0], field_out.shape[1]
    mine = s.at[K0 : K0 + own, 0:own_rows]
    copies = [pltpu.make_async_copy(mine, field_out, out_sems.at[0])]
    copies[0].start()

    def finish(j):
        rest[j] = residual(b, s, w, total, 1.0, j + K0)[0:own_rows]

    parts = out_sems.shape[0] - 1
    for part in range(parts):
        begin, end = own * part // parts, own * (part + 1) // parts
        loop(begin, end, finish, b.shape[1:])
        copy = pltpu.make_async_copy(
            rest.at[begin:end], residual_out.at[begin:end], out_sems.at[1 + part]
        )
        copy.start()
        copies.append(copy)
    wait(copies)


def call(kernel, outs, scratch=(), held=0, kept=(), sems=(), cost=0, registers=48):
    def body(*refs):
        REGISTERS[0] = registers
        kernel(*refs)

    def run(*operands):
        inputs = [o.shape for i, o in enumerate(operands) if i not in kept]
        shapes = inputs + list(outs[held:]) + list(scratch)
        words = sum(math.prod(s[:-2]) * eight(s[-2]) * s[-1] for s in shapes)
        places = [pltpu.HBM if i in kept else pltpu.VMEM for i in range(len(operands))]
        out_places = [pltpu.HBM if i < held else pltpu.VMEM for i in range(len(outs))]
        return pl.pallas_call(
            body,
            out_shape=[jax.ShapeDtypeStruct(shape, F32) for shape in outs],
            in_specs=[pl.BlockSpec(memory_space=place) for place in places],
            out_specs=[pl.BlockSpec(memory_space=place) for place in out_places],
            scratch_shapes=[pltpu.VMEM(shape, F32) for shape in scratch]
            + [pltpu.SemaphoreType.DMA((n,)) for n in sems],
            cost_estimate=pl.CostEstimate(flops=cost, bytes_accessed=cost, transcendentals=0) if cost else None,
            compiler_params=pltpu.CompilerParams(vmem_limit_bytes=4 * words + SPARE),
        )(*operands)

    return run


def eight(rows):
    return -(-rows // 8) * 8


def per_device(right_side, coefficient):
    bx, by, nz = right_side.shape
    across, along = lax.axis_size("gx"), lax.axis_size("gy")
    devices = across * along
    hx, hy, hz = bx // 2, by // 2, nz // 2
    qx, qy = hx // 2, hy // 2
    both = ("gx", "gy")
    tall, tall1 = eight(by + 2 * K0), eight(hy + 2 * K1)
    pieces = (devices, qx * qy // 2, hz)

    slab = (K0 + B0, bx, nz)
    first, second, right_side, coefficient = call(
        slab_kernel, [slab, slab, (bx, by, nz), (bx, by, nz)]
    )(right_side, coefficient)
    from_first, from_second = swap(first, second, "gy")
    group = 4
    message, k1 = call(
        conduct_kernel,
        [pieces, (hx, hy, hz)],
        [(hx, by, nz), (hx, by, hz), (qx, hy, hz), (qx, hy, hz), (group, *pieces[1:])],
        held=1,
        sems=(devices // group,),
    )(coefficient)

    plane = (bx, tall, nz)
    slab = (diamond(K0, by) + diamond(B0, by), nz)
    k_own, b_own, first, second = call(widen_kernel, [plane, plane, slab, slab], cost=LONG)(
        right_side, coefficient, from_first, from_second
    )
    from_first, from_second = swap(first, second, "gx")

    k2 = lax.all_to_all(message, both, 0, 0, tiled=True)

    block = (bx + 2 * K0, tall, nz)
    inner = call(fine_inner_kernel, [block] * 8 + [(hx, by, nz)], [block], registers=72)(
        k_own, b_own
    )
    slab = (K1 + B1, hx, hz)
    edges = (2 * K0 + 2, tall, nz)
    field_slab = (2 * S0 * bx, hz)
    *outer, s, b1, first, second = call(
        fine_outer_kernel,
        [edges] * 5 + [(bx, by, nz), (hx, hy, hz), slab, slab],
        [block] * 8 + [(hx, by, nz), block, (hx, by, hz)],
    )(k_own, from_first, from_second, k1, *inner)
    planes = 5 * block[0] + VMEM_BYTES // (4 * tall * nz)
    (stash,) = call(stash_kernel, [(planes, tall, nz)], held=1, sems=(15,))(
        *inner[:4], inner[5], *outer
    )
    from_first, from_second = swap(first, second, "gy")
    s_first, s_second = swap(*call(field_slab_kernel, [field_slab, field_slab])(s), "gy")
    slab = (K1 + B1, tall1, hz)
    k1_own, b1_own, first, second = call(
        widen_middle_kernel, [(hx, tall1, hz), (hx, tall1, hz), slab, slab]
    )(k1, b1, from_first, from_second)
    from_first, from_second = swap(first, second, "gx")

    block1 = (hx + 2 * K1, tall1, hz)
    message, k1, b1, s1 = call(
        middle_down_kernel,
        [pieces] + [block1] * 2 + [(hx, hy, hz)],
        [block1] * 7 + [(qx, hy, hz), (qx, hy, hz), (group, *pieces[1:])],
        held=1,
        kept=(6,),
        sems=(devices // group,),
    )(k1_own, b1_own, from_first, from_second, s_first, s_second, stash)
    received = lax.all_to_all(message, both, 0, 0, tiled=True)

    x2, y2 = across * qx, along * qy
    level2, level3 = (y2 // 2 + 2, x2, hz), (y2 // 2 + 2, x2 // 2, hz)
    half2, half3 = (y2 // 2, x2, hz), (y2 // 4, x2 // 2, hz)
    valid = nz // 4
    coarse = call(
        partial(coarse_weights_kernel, valid),
        [level2] * 4 + [level3, (y2 // 4, x2 // 4, hz)],
        [level2] * 3 + [half2] + [level3] * 6 + [half3] * 2,
        registers=48,
    )(k2)
    slab = (2 * S0 * tall + S1 * hy, hz)
    s_rows, first, second = call(field_planes_kernel, [plane, slab, slab])(
        s, s1, s_first, s_second
    )
    from_first, from_second = swap(first, second, "gx")
    slab = (S1 * block1[0], hz)
    s_own, s1_own, first, second = call(
        field_rows_kernel, [block, (block1[0], hy, hz), slab, slab]
    )(s_rows, s1, from_first, from_second, coarse[-1])
    from_first, from_second = swap(first, second, "gy")

    region, *weights = call(
        partial(coarse_kernel, valid),
        [(qy // 2 + EDGE, 3 * qx, hz)] + [block] * 5,
        [level2] * 5 + [half2] * 2 + [level3] * 8 + [half3] * 2,
        kept=(7,),
        sems=(5,),
        registers=40,
    )(received, *coarse, stash)

    count = hx + 2 * EDGE
    field, rest = call(
        fine_up_kernel,
        [(bx, by, nz)] * 2,
        [block1] * 5 + [block, block1, block1, (qx + 2 * EDGE, tall1, hz)]
        + [block, block, (count, tall, hz), (count, tall, nz), (bx, by, nz)],
        held=2,
        sems=(5,),
        registers=96,
    )(region, k1, b1, s1_own, *weights, s_own, from_first, from_second)
    return field, rest


def solution(mesh):
    in_specs = (P("gx", "gy", None), P("gx", "gy", None))
    out_specs = (P("gx", "gy", None), P("gx", "gy", None))
    return jax.shard_map(
        per_device, mesh=mesh, in_specs=in_specs, out_specs=out_specs, check_vma=False
    )
```
